128 devices in a mesh: seq: 16 (over y, x), row: 4 (over z), col: 2 (over core).
Axes of the slice: x: 4, y: 4, z: 4, core: 2. Of those that a mesh axis runs over, the one named last changes fastest.
Arguments:
- student: bfloat16 [12288, 8192], P(('seq', 'row'), 'col'), may hold values from -130 to 130
- teacher: bfloat16 [12288, 8192], P('seq', ('row', 'col')), may hold values from -130 to 130
- starts: int32 [12288], P('seq'), may hold values from 0 to 12284, as said below
- weights: int32 [12288, 4], P('seq'), may hold values from 1 to 16
- counts: int32 [16, 4], P('seq'), may hold values from 2 to 192, as said below
Outputs:
- alignment: float32 [2, 16, 256, 8192], P('col', 'seq', None, 'row')
The draws below stay inside these ranges and needn't reach their ends.
Inputs may be any that keep to these rules, and one draw needn't show every extreme that they name: counts[s, r] live student tokens are the first slots of block s * 4 + r of 192 slots; in every draw some block is full. For a student token of block b, starts lies between b * 192 - 16 and (b + 1) * 192 + 12.
All inputs are finite; a program needn't handle non-finite values.
Results may differ from the reference program's by a relative error of at most 0.0013.
Values may be sent and summed in bfloat16 or wider, within the bound.
No kernel may reach another device: no remote copies, remote signals or barrier semaphores. Data moves between devices by JAX's collectives and lax.ppermute only.
A program may use at most 128 MiB of HBM per device.

```python
import math
import jax
import jax.numpy as jnp
from jax import lax

DS = 8192
DT = 8192
SUB = 192
BAND = 4
HALO = 16
TOKENS = 12288
SLICE = 256
N_SEQ = 16
N_ROW = 4
N_COL = 2


def live_counts(key):
    first_key, second_key = jax.random.split(key)
    blocks = N_SEQ * N_ROW
    roots = jax.random.randint(first_key, (blocks,), 1, SUB + 1)
    sizes = jnp.maximum(roots * roots // SUB, 2)
    fullest = jax.random.randint(second_key, (), 0, blocks)
    return jnp.where(jnp.arange(blocks) == fullest, SUB, sizes).astype(jnp.int32)


def layered(noise, column_scale, row_scale, centre, rise):
    ramp = 1.0 + rise * jnp.arange(TOKENS, dtype=jnp.float32)[:, None] / TOKENS
    return (noise * column_scale * row_scale + centre * ramp).astype(jnp.bfloat16)


def draw_student(key, part):
    key = jax.random.fold_in(key, 7)
    noise_key, column_key, row_key, centre_key = jax.random.split(key, 4)
    noise = jnp.clip(jax.random.normal(noise_key, (TOKENS, DS), jnp.float32), -3.5, 3.5)
    column_scale = jnp.exp(jax.random.uniform(column_key, (1, DS), jnp.float32, 0.0, math.log(10.0)))
    row_scale = jnp.exp(jax.random.uniform(row_key, (TOKENS, 1), jnp.float32, 0.0, math.log(3.0)))
    centre = jax.random.uniform(centre_key, (1, DS), jnp.float32, -2.0, 2.0)
    return layered(noise, column_scale, row_scale, centre, 9.0)


def draw_teacher(key, part):
    key = jax.random.fold_in(key, 9)
    noise_key, column_key, row_key, centre_key = jax.random.split(key, 4)
    noise = jnp.clip(jax.random.normal(noise_key, (TOKENS, DT), jnp.float32), -4.0, 4.0)
    column_scale = jnp.exp(jax.random.uniform(column_key, (1, DT), jnp.float32, 0.0, math.log(10.0)))
    row_scale = jnp.exp(jax.random.uniform(row_key, (TOKENS, 1), jnp.float32, 0.0, math.log(3.0)))
    centre = jax.random.uniform(centre_key, (1, DT), jnp.float32, -2.0, 2.0)
    return layered(noise, column_scale, row_scale, centre, 2.0)


def draw_counts(key, part):
    sizes = live_counts(key)
    return sizes.reshape(N_SEQ, N_ROW)


def draw_starts(key, part):
    sizes = live_counts(key)
    key = jax.random.fold_in(key, 5)
    token_index = jnp.arange(TOKENS, dtype=jnp.int32)
    position = token_index % SUB
    block_ids = token_index // SUB
    alive = jnp.take(sizes, block_ids)
    span = SUB + 2 * HALO - BAND
    lower = block_ids * SUB - HALO
    live_start = lower + span * position // jnp.maximum(alive - 1, 1)
    dead_start = lower + jax.random.randint(key, (TOKENS,), 0, span + 1)
    chosen = jnp.where(position < alive, live_start, dead_start)
    return jnp.clip(chosen, 0, TOKENS - BAND).astype(jnp.int32)


def plant(result, stream_key, smallest, largest):
    spot = [jax.random.randint(jax.random.fold_in(stream_key, axis), (), 0, length) for axis, length in enumerate(result.shape)]
    main_axis = result.shape.index(max(result.shape))
    next_to = spot[:main_axis] + [(spot[main_axis] + 1) % result.shape[main_axis]] + spot[main_axis + 1:]
    return result.at[tuple(spot)].set(smallest).at[tuple(next_to)].set(largest)


def setup_inputs(seed: int = 0) -> dict:
    streams_of = jax.random.split(jax.random.key(seed), 6)
    return {
        "student": draw_student(jax.random.fold_in(streams_of[5], 71), 0),
        "teacher": draw_teacher(jax.random.fold_in(streams_of[5], 71), 0),
        "starts": draw_starts(jax.random.fold_in(streams_of[5], 71), 0),
        "weights": plant(jax.random.randint(streams_of[3], (TOKENS, BAND), 1, 17), jax.random.fold_in(streams_of[3], 1), 1, 16).astype(jnp.int32),
        "counts": draw_counts(jax.random.fold_in(streams_of[5], 71), 0),
    }


epsilon = 1e-05

def standardize(values, live_rows, total_tokens):
    column_mean = lax.optimization_barrier(jnp.sum(values * live_rows, axis=0)) / total_tokens
    centered = (values - column_mean) * live_rows
    column_var = lax.optimization_barrier(jnp.sum(centered * centered, axis=0)) / total_tokens
    return (centered * lax.rsqrt(column_var + epsilon)).astype(jnp.bfloat16)

def reference(student, teacher, starts, weights, counts):
    token_index = jnp.arange(TOKENS, dtype=jnp.int32)
    block_ids = token_index // SUB
    flat_counts = counts.reshape(-1)
    live_rows = (token_index % SUB < jnp.take(flat_counts, block_ids)).astype(jnp.float32)[:, None]
    total_tokens = jnp.sum(flat_counts).astype(jnp.float32)
    weighted = jnp.zeros((TOKENS, DT), jnp.float32)
    for band_pos in range(BAND):
        rows_here = jnp.take(teacher, starts + band_pos, axis=0)
        weighted = weighted + weights[:, band_pos:band_pos + 1].astype(jnp.float32) * rows_here.astype(jnp.float32)
    pooled = weighted / lax.optimization_barrier(jnp.sum(weights, axis=1, keepdims=True)).astype(jnp.float32)
    student_std = standardize(student.astype(jnp.float32), live_rows, total_tokens)
    pooled_std = standardize(pooled, live_rows, total_tokens)
    shard_len = SUB * N_ROW

    def add_shard(shard_idx, total):
        first = shard_idx * shard_len
        left = lax.dynamic_slice_in_dim(student_std, first, shard_len, 0)
        right = lax.dynamic_slice_in_dim(pooled_std, first, shard_len, 0)
        partial_term = lax.dot_general(left, right, (((0,), (0,)), ((), ())), preferred_element_type=jnp.float32)
        rounded = lax.optimization_barrier(partial_term.astype(jnp.bfloat16))
        return total + rounded.astype(jnp.float32)
    cross = lax.fori_loop(0, N_SEQ, add_shard, jnp.zeros((DS, DT), jnp.float32))
    cross = cross / jnp.sqrt(total_tokens)
    return cross.reshape(N_COL, N_SEQ, SLICE, DT)
```

```python
import jax
import jax.numpy as jnp
from jax import lax
from jax.experimental import pallas as pl
from jax.experimental.pallas import tpu as pltpu
from jax.sharding import Mesh
from jax.sharding import PartitionSpec as P

SUB = 192
BAND = 4
HALO = 16
SIDE = 4
epsilon = 1e-05


def ring(value, axis, step):
    return lax.ppermute(value, axis, [(i, (i + step) % SIDE) for i in range(SIDE)])


def ring_all(value, axis):
    return [value, ring(value, axis, 1), ring(value, axis, -1), ring(value, axis, 2)]


def swap(value):
    return lax.ppermute(value, "col", [(0, 1), (1, 0)])


def pool_kernel(counts, before, teacher, after, meta, centered, stats, mix, share, pooled):
    window = SUB + 2 * HALO
    blocks = SIDE

    @pl.when(pl.program_id(0) == 0)
    def _():
        for r in range(blocks):
            rows = slice(r * SUB, (r + 1) * SUB)
            place = lax.broadcasted_iota(jnp.int32, (SUB, window), 1)
            local = meta[rows, 0:1] - (r * SUB - HALO)
            found = jnp.zeros((SUB, window), jnp.int32)
            whole = jnp.zeros((SUB, 1), jnp.int32)
            for k in range(BAND):
                weight = meta[rows, 1 + k : 2 + k]
                found = found + jnp.where(place == local + k, weight, 0)
                whole = whole + weight
            mix[rows, :] = found.astype(jnp.float32).astype(jnp.bfloat16)
            share[rows, :] = jnp.broadcast_to(whole.astype(jnp.float32), (SUB, 128))

    total = jnp.zeros((1, teacher.shape[1]), jnp.float32)
    alive = jnp.int32(0)
    length = teacher.shape[0]
    for r in range(blocks):
        rows = slice(r * SUB, (r + 1) * SUB)
        low, high = r * SUB - HALO, (r + 1) * SUB + HALO
        parts = [teacher[max(low, 0) : min(high, length), :]]
        if low < 0:
            parts = [before[...]] + parts
        if high > length:
            parts = parts + [after[...]]
        seen = jnp.concatenate(parts, axis=0) if len(parts) > 1 else parts[0]
        value = jnp.dot(mix[rows, :], seen, preferred_element_type=jnp.float32)
        value = value / share[rows, 0:1]
        pooled[rows, :] = value
        live = lax.broadcasted_iota(jnp.int32, value.shape, 0) < counts[r]
        total = total + jnp.sum(jnp.where(live, value, 0.0), axis=0, keepdims=True)
        alive = alive + counts[r]
    mean = total / alive.astype(jnp.float32)
    square = jnp.zeros_like(total)
    for r in range(blocks):
        rows = slice(r * SUB, (r + 1) * SUB)
        value = pooled[rows, :]
        live = lax.broadcasted_iota(jnp.int32, value.shape, 0) < counts[r]
        dev = jnp.where(live, value - mean, 0.0)
        centered[rows, :] = dev.astype(jnp.bfloat16)
        square = square + jnp.sum(dev * dev, axis=0, keepdims=True)
    stats[0:1, :] = total
    stats[1:2, :] = square
    stats[2:3, :] = jnp.broadcast_to(alive.astype(jnp.float32), total.shape)


def pool(counts, before, teacher, after, meta):
    rows, columns = teacher.shape
    tile = 256
    return pl.pallas_call(
        pool_kernel,
        grid=(columns // tile,),
        in_specs=[
            pl.BlockSpec(memory_space=pltpu.SMEM),
            pl.BlockSpec((HALO, tile), lambda j: (0, j)),
            pl.BlockSpec((rows, tile), lambda j: (0, j)),
            pl.BlockSpec((HALO, tile), lambda j: (0, j)),
            pl.BlockSpec(meta.shape, lambda j: (0, 0)),
        ],
        out_specs=[
            pl.BlockSpec((rows, tile), lambda j: (0, j)),
            pl.BlockSpec((3, tile), lambda j: (0, j)),
        ],
        out_shape=[
            jax.ShapeDtypeStruct((rows, columns), jnp.bfloat16),
            jax.ShapeDtypeStruct((3, columns), jnp.float32),
        ],
        scratch_shapes=[
            pltpu.VMEM((rows, SUB + 2 * HALO), jnp.bfloat16),
            pltpu.VMEM((rows, 128), jnp.float32),
            pltpu.VMEM((rows, tile), jnp.float32),
        ],
        compiler_params=pltpu.CompilerParams(vmem_limit_bytes=32 * 2**20),
        cost_estimate=pl.CostEstimate(
            flops=2 * rows * 224 * columns, bytes_accessed=6 * rows * columns, transcendentals=0
        ),
    )(counts, before, teacher, after, meta)


def product_kernel(place, a0, a1, a2, a3, b0, b1, b2, b3, mean, out, sums):
    z = place[0]
    order = (0, SIDE - 1, 1, 2)
    mine = []
    for step in order:
        first = pl.multiple_of(lax.rem(z + step, SIDE) * SUB, 16)
        mine.append(
            jnp.concatenate([b[pl.ds(first, SUB), :] for b in (b0, b1, b2, b3)], axis=0)
        )

    @pl.when(pl.program_id(0) == 0)
    def _():
        ones = jnp.ones((16, mine[0].shape[0]), jnp.bfloat16)
        sums[...] = sum(jnp.dot(ones, m, preferred_element_type=jnp.float32) for m in mine)

    acc = None
    for a, m in zip((a0, a1, a2, a3), mine):
        term = jnp.dot(a[...], m, preferred_element_type=jnp.float32)
        acc = term if acc is None else acc + term
    out[...] = acc - mean[...] * sums[0:1, :]


def product(place, left, right, mean):
    rows, depth = left[0].shape
    columns = right[0].shape[1]
    part = rows // SIDE

    def slice_of(i, place):
        step = jnp.where(i == 0, 2, jnp.where(i == 1, 1, jnp.where(i == 2, 3, 0)))
        return (lax.rem(place[1] + step, SIDE), 0)

    spec = pltpu.PrefetchScalarGridSpec(
        num_scalar_prefetch=1,
        grid=(SIDE,),
        in_specs=[pl.BlockSpec((part, depth), slice_of)] * SIDE
        + [pl.BlockSpec(right[0].shape, lambda i, place: (0, 0))] * SIDE
        + [pl.BlockSpec((part, 1), slice_of)],
        out_specs=pl.BlockSpec((part, columns), lambda i, place: (i, 0)),
        scratch_shapes=[pltpu.VMEM((16, columns), jnp.float32)],
    )
    return pl.pallas_call(
        product_kernel,
        grid_spec=spec,
        out_shape=jax.ShapeDtypeStruct((rows, columns), jnp.float32),
        compiler_params=pltpu.CompilerParams(vmem_limit_bytes=40 * 2**20),
        cost_estimate=pl.CostEstimate(
            flops=2 * rows * depth * SIDE * columns,
            bytes_accessed=2 * SIDE * depth * (rows + columns) + 4 * rows * columns,
            transcendentals=0,
        ),
    )(place, *left, *right, mean)


def per_device(student, teacher, starts, weights, counts):
    y, x, z, c = (lax.axis_index(n) for n in ("y", "x", "row", "col"))
    shard = y * SIDE + x
    rows = starts.shape[0]
    width = student.shape[1] // SIDE
    part = width // SIDE

    by_x = student.reshape(SUB, SIDE, SIDE, part).transpose(2, 0, 1, 3).reshape(SIDE, SUB, width)

    def for_x(step):
        return lax.dynamic_index_in_dim(by_x, lax.rem(x + step, SIDE), 0, keepdims=False)

    got = [
        for_x(0),
        ring(for_x(1), "x", 1),
        ring(for_x(SIDE - 1), "x", -1),
        ring(for_x(2), "x", 2),
    ]

    up = [(i, (i + 1) % 16) for i in range(16)]
    down = [(j, i) for i, j in up]
    before = lax.ppermute(teacher[rows - HALO :], ("y", "x"), up)
    after = lax.ppermute(teacher[:HALO], ("y", "x"), down)
    meta = jnp.concatenate([(starts - shard * rows)[:, None], weights], axis=1)
    standard, stats = pool(counts[0], before, teacher, after, meta)
    columns = standard.shape[1]

    half = columns // 2
    right1 = ring(standard, "x", 1)
    left1 = ring(standard, "x", -1)
    far = [ring(right1[:, :half], "x", 1), ring(left1[:, half:], "x", -1)]
    own_sides = [
        [p[:, :half] for p in (standard, right1, left1)] + [far[0]],
        [p[:, half:] for p in (standard, right1, left1)] + [far[1]],
    ]
    t_standard, t_right1, t_left1 = swap(standard), swap(right1), swap(left1)
    t_far = [swap(f) for f in far]
    mate_sides = [
        [p[:, :half] for p in (t_standard, t_right1, t_left1)] + [t_far[0]],
        [p[:, half:] for p in (t_standard, t_right1, t_left1)] + [t_far[1]],
    ]

    block = jnp.concatenate(got, axis=0)
    turned = block.T
    z_up = ring(turned, "row", 1)
    z_down = ring(turned, "row", -1)
    z_far = jnp.concatenate(
        [ring(z_up[: width // 2], "row", 1), ring(z_down[width // 2 :], "row", -1)], axis=0
    )
    left = [turned, z_up, z_down, z_far]

    counts_row = jnp.pad(counts.astype(jnp.float32), ((0, 0), (0, columns - SIDE)))
    near = jnp.stack(ring_all(jnp.concatenate([stats, counts_row]), "x"))
    group_counts = near[:, 3, :SIDE]
    shards = jnp.concatenate(ring_all(near[:, :3], "y"), axis=0)
    t_sum, t_square, t_count = shards[:, 0], shards[:, 1], shards[:, 2]
    tokens = jnp.sum(t_count[:, 0])
    t_local = t_sum / t_count
    t_mean = jnp.sum(t_sum, axis=0) / tokens
    t_off = t_local - t_mean
    t_var = (jnp.sum(t_square, axis=0) + jnp.sum(t_count * t_off * t_off, axis=0)) / tokens
    t_scale = lax.rsqrt(t_var + epsilon)
    t_rows = jnp.concatenate([t_scale[None], t_off * t_scale])
    t_mate = swap(t_rows)

    own_counts = lax.dynamic_index_in_dim(group_counts, z, 1, keepdims=True)
    values = block.astype(jnp.float32).reshape(SIDE, SUB, width)
    live = (jnp.arange(SUB).astype(jnp.float32) < own_counts)[:, :, None]
    s_sum = jnp.sum(jnp.where(live, values, 0.0), axis=1)
    s_dev = jnp.where(live, values - (s_sum / own_counts)[:, None], 0.0)
    s_parts = jnp.stack([s_sum, jnp.sum(s_dev * s_dev, axis=1)])
    s_z = jnp.stack(ring_all(s_parts, "row"))
    z_counts = jnp.stack(
        [
            lax.dynamic_index_in_dim(group_counts, lax.rem(z + k, SIDE), 1, keepdims=True)
            for k in (0, SIDE - 1, 1, 2)
        ]
    )
    shard_count = jnp.sum(group_counts, axis=1, keepdims=True)
    shard_sum = jnp.sum(s_z[:, 0], axis=0)
    shard_off = s_z[:, 0] / z_counts - shard_sum / shard_count
    shard_square = jnp.sum(s_z[:, 1] + z_counts * shard_off * shard_off, axis=0)
    s_group = (jnp.sum(shard_sum, axis=0) / jnp.sum(shard_count))[:, None]
    s_all = jnp.stack(ring_all(jnp.stack([shard_sum, shard_square]), "y"))
    s_all = lax.dynamic_slice_in_dim(s_all, y * part, part, axis=3)
    s_all = s_all.transpose(1, 0, 2, 3).reshape(2, SIDE * SIDE, part)
    s_count = t_count[:, :1]
    s_mean = jnp.sum(s_all[0], axis=0) / tokens
    s_off = s_all[0] / s_count - s_mean
    s_var = (jnp.sum(s_all[1], axis=0) + jnp.sum(s_count * s_off * s_off, axis=0)) / tokens
    inverse = 1.0 / jnp.sqrt(tokens)
    s_scale = lax.rsqrt(s_var + epsilon) * inverse
    s_rows = s_off * s_scale * s_count

    place = jnp.stack([z, y]).astype(jnp.int32)

    def finish(sides, direction, t_rows):
        partial = product(place, left, sides, s_group)
        far_p, next_p, back_p, own_p = (partial[i * part : (i + 1) * part] for i in range(SIDE))
        if direction < 0:
            next_p, back_p = back_p, next_p
        u = ring(far_p.astype(jnp.bfloat16), "y", direction)
        w = ring(back_p.astype(jnp.bfloat16), "y", -direction)
        v = ring((next_p + u.astype(jnp.float32)).astype(jnp.bfloat16), "y", direction)
        between = lax.dot_general(
            s_rows, t_rows[1:], (((0,), (0,)), ((), ())), precision=lax.Precision.HIGHEST
        )
        inside = own_p + v.astype(jnp.float32) + w.astype(jnp.float32)
        return inside * s_scale[:, None] * t_rows[0] + between

    own_out = [
        finish(own_sides[0], 1, t_rows[:, :half]),
        finish(own_sides[1], -1, t_rows[:, half:]),
    ]
    mate_out = [
        finish(mate_sides[0], 1, t_mate[:, :half]),
        finish(mate_sides[1], -1, t_mate[:, half:]),
    ]
    own_out = jnp.concatenate(own_out, axis=1)
    mate_out = jnp.concatenate(mate_out, axis=1)
    first = jnp.where(c == 0, own_out, mate_out)
    second = jnp.where(c == 0, mate_out, own_out)
    return jnp.concatenate([first, second], axis=1)[None, None]


def solution(mesh):
    fine = Mesh(mesh.devices.reshape(SIDE, SIDE, SIDE, 2), ("y", "x", "row", "col"))
    seq = ("y", "x")
    placed = (
        P(seq + ("row",), "col"),
        P(seq, ("row", "col")),
        P(seq),
        P(seq, None),
        P(seq, None),
    )
    return jax.shard_map(
        per_device,
        mesh=fine,
        in_specs=placed,
        out_specs=P("col", seq, None, "row"),
        check_vma=False,
    )
```

```python
import jax
import jax.numpy as jnp
from jax import lax
from jax.experimental import pallas as pl
from jax.experimental.pallas import tpu as pltpu
from jax.sharding import Mesh
from jax.sharding import PartitionSpec as P

SUB = 192
BAND = 4
HALO = 16
SIDE = 4
COMING = (0, SIDE - 1, 1, 2)
epsilon = 1e-05
f32 = jnp.float32
bf16 = jnp.bfloat16


def ring(value, axis, step):
    return lax.ppermute(value, axis, [(i, (i + step) % SIDE) for i in range(SIDE)])


def ring_all(value, axis):
    return [value, ring(value, axis, 1), ring(value, axis, -1), ring(value, axis, 2)]


def swap(value):
    return lax.ppermute(value, "col", [(0, 1), (1, 0)])


def after(value, *others):
    return lax.optimization_barrier((value, others))[0]


def smem():
    return pl.BlockSpec(memory_space=pltpu.SMEM)


def vmem():
    return pl.BlockSpec(memory_space=pltpu.VMEM)


def pack_kernel(place, student, *outs):
    y, x = place[0], place[1]
    part = outs[0].shape[1] // 2
    for r, x_step in enumerate((0, 1, SIDE - 1, 2)):
        for k, y_steps in enumerate(((2, 0), (1, SIDE - 1))):
            for i, y_step in enumerate(y_steps):
                slot = lax.rem(y + y_step, SIDE) * SIDE + lax.rem(x + x_step, SIDE)
                first = pl.multiple_of(slot * part, 128)
                outs[2 * r + k][:, i * part : (i + 1) * part] = student[:, pl.ds(first, part)]


def pack(place, student):
    part = student.shape[1] // (SIDE * SIDE)
    shape = jax.ShapeDtypeStruct((SUB, 2 * part), bf16)
    return pl.pallas_call(
        pack_kernel,
        in_specs=[smem(), vmem()],
        out_specs=[vmem()] * 8,
        out_shape=[shape] * 8,
        compiler_params=pltpu.CompilerParams(vmem_limit_bytes=16 * 2**20),
        cost_estimate=pl.CostEstimate(
            flops=0, bytes_accessed=4 * SUB * student.shape[1], transcendentals=0
        ),
    )(place, student)


def turn_kernel(own_count, p0, p1, p2, p3, turned, near):
    rows = jnp.concatenate([p[...] for p in (p0, p1, p2, p3)], axis=0)
    flat = rows.T
    turned[...] = flat
    mine = flat[:, :SUB].astype(f32)
    live = lax.broadcasted_iota(jnp.int32, mine.shape, 1) < own_count[0]
    total = jnp.sum(jnp.where(live, mine, 0.0), axis=1, keepdims=True)
    near[...] = total / own_count[0].astype(f32)


def turn(own_count, pieces):
    width = pieces[0].shape[1]
    return pl.pallas_call(
        turn_kernel,
        in_specs=[smem()] + [vmem()] * SIDE,
        out_specs=[vmem()] * 2,
        out_shape=[
            jax.ShapeDtypeStruct((width, SIDE * SUB), bf16),
            jax.ShapeDtypeStruct((width, 1), f32),
        ],
        compiler_params=pltpu.CompilerParams(vmem_limit_bytes=16 * 2**20),
        cost_estimate=pl.CostEstimate(
            flops=0, bytes_accessed=4 * SUB * SIDE * width, transcendentals=0
        ),
    )(own_count, *pieces)


def moments_kernel(counts, *refs):
    out = refs[-1]
    for r in range(SIDE):
        for k in range(2):
            value = refs[2 * r + k][...].astype(f32)
            columns = slice(k * value.shape[1], (k + 1) * value.shape[1])
            live = lax.broadcasted_iota(jnp.int32, value.shape, 0) < counts[r]
            total = jnp.sum(jnp.where(live, value, 0.0), axis=0, keepdims=True)
            dev = jnp.where(live, value - total / counts[r].astype(f32), 0.0)
            out[r : r + 1, columns] = total
            out[SIDE + r : SIDE + r + 1, columns] = jnp.sum(dev * dev, axis=0, keepdims=True)


def moments(counts, pieces):
    width = pieces[0].shape[1]
    return pl.pallas_call(
        moments_kernel,
        in_specs=[smem()] + [vmem()] * len(pieces),
        out_specs=vmem(),
        out_shape=jax.ShapeDtypeStruct((2 * SIDE, 2 * width), f32),
        compiler_params=pltpu.CompilerParams(vmem_limit_bytes=16 * 2**20),
        cost_estimate=pl.CostEstimate(
            flops=8 * SUB * SIDE * width, bytes_accessed=4 * SUB * SIDE * width, transcendentals=0
        ),
    )(counts, *pieces)


def pool_kernel(counts, before, teacher, behind, meta, full, first, second, stats, mix, share, pooled):
    window = SUB + 2 * HALO
    length = teacher.shape[0]
    j = pl.program_id(0)

    @pl.when(j == 0)
    def _():
        for r in range(SIDE):
            rows = slice(r * SUB, (r + 1) * SUB)
            place = lax.broadcasted_iota(jnp.int32, (SUB, window), 1)
            local = meta[rows, 0:1] - (r * SUB - HALO)
            found = jnp.zeros((SUB, window), jnp.int32)
            whole = jnp.zeros((SUB, 1), jnp.int32)
            for k in range(BAND):
                weight = meta[rows, 1 + k : 2 + k]
                found = found + jnp.where(place == local + k, weight, 0)
                whole = whole + weight
            mix[rows, :] = found.astype(f32).astype(bf16)
            share[rows, :] = jnp.broadcast_to(whole.astype(f32), (SUB, 128))

    total = jnp.zeros((1, teacher.shape[1]), f32)
    alive = jnp.int32(0)
    for r in range(SIDE):
        rows = slice(r * SUB, (r + 1) * SUB)
        low, high = r * SUB - HALO, (r + 1) * SUB + HALO
        parts = [teacher[max(low, 0) : min(high, length), :]]
        if low < 0:
            parts = [before[...]] + parts
        if high > length:
            parts = parts + [behind[...]]
        seen = jnp.concatenate(parts, axis=0) if len(parts) > 1 else parts[0]
        value = jnp.dot(mix[rows, :], seen, preferred_element_type=f32)
        value = value / share[rows, 0:1]
        pooled[rows, :] = value
        live = lax.broadcasted_iota(jnp.int32, value.shape, 0) < counts[r]
        total = total + jnp.sum(jnp.where(live, value, 0.0), axis=0, keepdims=True)
        alive = alive + counts[r]
    mean = total / alive.astype(f32)
    square = jnp.zeros_like(total)
    for r in range(SIDE):
        rows = slice(r * SUB, (r + 1) * SUB)
        value = pooled[rows, :]
        live = lax.broadcasted_iota(jnp.int32, value.shape, 0) < counts[r]
        dev = jnp.where(live, value - mean, 0.0)
        small = dev.astype(bf16)
        full[rows, :] = small

        @pl.when(j < pl.num_programs(0) // 2)
        def _():
            first[rows, :] = small

        @pl.when(j >= pl.num_programs(0) // 2)
        def _():
            second[rows, :] = small

        square = square + jnp.sum(dev * dev, axis=0, keepdims=True)
    stats[0:1, :] = total
    stats[1:2, :] = square
    stats[2:3, :] = jnp.broadcast_to(alive.astype(f32), total.shape)


def pool(counts, before, teacher, behind, meta):
    rows, columns = teacher.shape
    tile = 256
    last = columns // tile // 2
    return pl.pallas_call(
        pool_kernel,
        grid=(columns // tile,),
        in_specs=[
            smem(),
            pl.BlockSpec((HALO, tile), lambda j: (0, j)),
            pl.BlockSpec((rows, tile), lambda j: (0, j)),
            pl.BlockSpec((HALO, tile), lambda j: (0, j)),
            pl.BlockSpec(meta.shape, lambda j: (0, 0)),
        ],
        out_specs=[
            pl.BlockSpec((rows, tile), lambda j: (0, j)),
            pl.BlockSpec((rows, tile), lambda j: (0, jnp.minimum(j, last - 1))),
            pl.BlockSpec((rows, tile), lambda j: (0, jnp.maximum(j - last, 0))),
            pl.BlockSpec((3, tile), lambda j: (0, j)),
        ],
        out_shape=[
            jax.ShapeDtypeStruct((rows, columns), bf16),
            jax.ShapeDtypeStruct((rows, columns // 2), bf16),
            jax.ShapeDtypeStruct((rows, columns // 2), bf16),
            jax.ShapeDtypeStruct((3, columns), f32),
        ],
        scratch_shapes=[
            pltpu.VMEM((rows, SUB + 2 * HALO), bf16),
            pltpu.VMEM((rows, 128), f32),
            pltpu.VMEM((rows, tile), f32),
        ],
        compiler_params=pltpu.CompilerParams(vmem_limit_bytes=32 * 2**20),
        cost_estimate=pl.CostEstimate(
            flops=2 * rows * 256 * columns, bytes_accessed=6 * rows * columns, transcendentals=0
        ),
    )(counts, before, teacher, behind, meta)


def sums_of(place, near, left, right):
    z = place[0]
    total = None
    for a, step in zip(left, COMING):
        first = pl.multiple_of(lax.rem(z + step, SIDE) * SUB, 16)
        rows = pl.ds(first, SUB)
        far = jnp.concatenate([right[3][rows, :], right[4][rows, :]], axis=1)
        b = jnp.concatenate([right[0][rows, :], right[1][rows, :], right[2][rows, :], far], axis=0)
        term = jnp.dot(a, b, preferred_element_type=f32)
        total = term if total is None else total + term
    part = total.shape[0] - 16
    return total[:part] - near * total[part : part + 1]


def left_of(refs, i):
    ones = jnp.ones((16, refs[0].shape[1]), bf16)
    far = jnp.where(i == 0, refs[3][...], refs[4][...])
    return [jnp.concatenate([a, ones], axis=0) for a in [r[...] for r in refs[:3]] + [far]]


def open_kernel(place, *refs):
    left, own, mate, near = refs[:5], refs[5:10], refs[10:15], refs[15]
    up, down, kept = refs[16:]
    i = pl.program_id(0)
    half = up.shape[1]
    a = left_of(left, i)
    results = [sums_of(place, near[...], a, side) for side in (own, mate)]

    @pl.when(i == 0)
    def _():
        up[...] = results[0].astype(bf16)
        down[...] = results[1].astype(bf16)

    @pl.when(i == 1)
    def _():
        kept[:, :half] = results[0]
        kept[:, half:] = results[1]


def close_kernel(place, *refs):
    left, own, mate, near = refs[:5], refs[5:10], refs[10:15], refs[15]
    from_back, from_next, up, down = refs[16:]
    i = pl.program_id(0)
    half = from_back.shape[1]
    a = left_of(left, i)
    results = [sums_of(place, near[...], a, side) for side in (own, mate)]

    @pl.when(i == 0)
    def _():
        up[:, :half] = (results[0] + from_back[...].astype(f32)).astype(bf16)
        up[:, half:] = results[1].astype(bf16)

    @pl.when(i == 1)
    def _():
        down[:, :half] = results[0].astype(bf16)
        down[:, half:] = (results[1] + from_next[...].astype(f32)).astype(bf16)


def product(place, k, left, own, mate, near, arrived=None):
    depth = left[0].shape[1]
    part = left[0].shape[0] // 2
    rows = own[1].shape[0]
    half = own[1].shape[1]
    one = lambda i, place: (0, 0)
    side = (
        [pl.BlockSpec((rows, half), lambda i, place: (0, k))]
        + [pl.BlockSpec((rows, half), one)] * 2
        + [pl.BlockSpec((rows, half // 2), one)] * 2
    )
    in_specs = (
        [pl.BlockSpec((part, depth), lambda i, place: (i, 0))] * 3
        + [pl.BlockSpec((part, depth), one)] * 2
        + side * 2
        + [pl.BlockSpec((part, 1), lambda i, place: (i, 0))]
    )
    S = jax.ShapeDtypeStruct
    if arrived is None:
        kernel, extra = open_kernel, ()
        shapes = [S((part, half), bf16), S((part, half), bf16), S((part, 2 * half), f32)]
    else:
        kernel, extra = close_kernel, arrived
        in_specs = in_specs + [pl.BlockSpec((part, half), one)] * 2
        shapes = [S((part, 2 * half), bf16), S((part, 2 * half), bf16)]
    return pl.pallas_call(
        kernel,
        grid_spec=pltpu.PrefetchScalarGridSpec(
            num_scalar_prefetch=1,
            grid=(2,),
            in_specs=in_specs,
            out_specs=[pl.BlockSpec(s.shape, one) for s in shapes],
        ),
        out_shape=shapes,
        compiler_params=pltpu.CompilerParams(vmem_limit_bytes=40 * 2**20),
        cost_estimate=pl.CostEstimate(
            flops=2 * 2 * part * depth * SIDE * 2 * half,
            bytes_accessed=2 * SIDE * depth * (2 * part + 2 * half) + 6 * part * half,
            transcendentals=0,
        ),
    )(place, *left, *own, *mate, near, *extra)


def final_kernel(place, kept, first, second, between, row_scale, column_scale, *rest):
    out = rest[-1]
    inside = kept[...] + first[...].astype(f32) + second[...].astype(f32)
    out[...] = inside * row_scale[...] * column_scale[...] + between[...]


def final(place, k, kept, first, second, between, row_scale, column_scale, whole=None):
    part, columns = kept.shape
    half = columns // 2
    block = pl.BlockSpec((part, half), lambda i, place: (0, i))
    in_specs = [block] * 4 + [
        pl.BlockSpec((part, 1), lambda i, place: (0, 0)),
        pl.BlockSpec((1, half), lambda i, place: (0, i)),
    ]
    more, aliases = (), {}
    if whole is not None:
        in_specs = in_specs + [pl.BlockSpec(memory_space=pl.ANY)]
        more, aliases = (whole,), {7: 0}
    return pl.pallas_call(
        final_kernel,
        grid_spec=pltpu.PrefetchScalarGridSpec(
            num_scalar_prefetch=1,
            grid=(2,),
            in_specs=in_specs,
            out_specs=pl.BlockSpec(
                (part, half), lambda i, place: (0, lax.rem(place[1] + i, 2) * 2 + k)
            ),
        ),
        out_shape=jax.ShapeDtypeStruct((part, 2 * columns), f32),
        input_output_aliases=aliases,
        compiler_params=pltpu.CompilerParams(vmem_limit_bytes=16 * 2**20),
        cost_estimate=pl.CostEstimate(
            flops=6 * part * columns, bytes_accessed=16 * part * columns, transcendentals=0
        ),
    )(place, kept, first, second, between, row_scale, column_scale, *more)


def per_device(student, teacher, starts, weights, counts):
    y, x, z, c = (lax.axis_index(n) for n in ("y", "x", "row", "col"))
    shard = y * SIDE + x
    rows = starts.shape[0]
    columns = teacher.shape[1]
    half = columns // 2
    width = student.shape[1] // SIDE
    part = width // SIDE

    up = [(i, (i + 1) % 16) for i in range(16)]
    down = [(j, i) for i, j in up]
    before = lax.ppermute(teacher[rows - HALO :], ("y", "x"), up)
    behind = lax.ppermute(teacher[:HALO], ("y", "x"), down)

    packed = pack(jnp.stack([y, x]).astype(jnp.int32), student)
    packed, before, behind = lax.optimization_barrier((packed, before, behind))
    steps = (0, 1, -1, 2)
    got0 = [packed[0]] + [ring(packed[2 * r], "x", steps[r]) for r in (1, 2, 3)]

    meta = jnp.concatenate([(starts - shard * rows)[:, None], weights], axis=1)
    standard, *halves, stats = pool(counts[0], before, teacher, behind, meta)
    later = after([packed[2 * r + 1] for r in range(SIDE)], stats)
    got1 = [later[0]] + [ring(later[r], "x", steps[r]) for r in (1, 2, 3)]

    counts_row = jnp.pad(counts.astype(f32), ((0, 0), (0, columns - SIDE)))
    near = jnp.stack(ring_all(jnp.concatenate([stats, counts_row]), "x"))
    group_counts = near[:, 3, :SIDE]
    halves = after(halves, near)

    own_count = lax.dynamic_slice_in_dim(counts[0], z, 1)
    lefts, means = [], []
    for got in (got0, got1):
        turned, mean = turn(own_count, got)
        z_up = ring(turned, "row", 1)
        z_down = ring(turned, "row", -1)
        far = [ring(z_up[:part], "row", 1), ring(z_down[part:], "row", -1)]
        lefts.append([turned, z_up, z_down] + far)
        means.append(mean)

    t_standard = swap(standard)
    owns, mates = [], []
    for k in range(2):
        right1 = ring(halves[k], "x", 1)
        left1 = ring(halves[k], "x", -1)
        quarter = half // 2
        far = [ring(right1[:, :quarter], "x", 1), ring(left1[:, quarter:], "x", -1)]
        own = [right1, left1] + far
        owns.append([standard] + own)
        mates.append([t_standard] + [swap(p) for p in own])

    own_counts = lax.dynamic_index_in_dim(group_counts, z, 1, keepdims=True)
    pieces = [p for pair in zip(got0, got1) for p in pair]
    s_z = jnp.stack(ring_all(moments(own_counts[:, 0].astype(jnp.int32), pieces), "row"))
    z_counts = jnp.stack(
        [
            lax.dynamic_index_in_dim(group_counts, lax.rem(z + k, SIDE), 1, keepdims=True)
            for k in COMING
        ]
    )
    shard_count = jnp.sum(group_counts, axis=1, keepdims=True)
    shard_sum = jnp.sum(s_z[:, :SIDE], axis=0)
    shard_off = s_z[:, :SIDE] / z_counts - shard_sum / shard_count
    shard_square = jnp.sum(s_z[:, SIDE:] + z_counts * shard_off * shard_off, axis=0)

    both = jnp.concatenate([near[:, 0], near[:, 1], near[:, 2], shard_sum, shard_square])
    every = ring_all(both, "y")
    t_sum, t_square, t_count = (
        jnp.concatenate([e[i * SIDE : (i + 1) * SIDE] for e in every]) for i in range(3)
    )
    s_sum, s_square = (
        jnp.concatenate(
            [
                e[i * SIDE : (i + 1) * SIDE, slot * part : (slot + 1) * part]
                for e, slot in zip(every, (1, 2, 3, 0))
            ]
        )
        for i in (3, 4)
    )
    s_count = t_count[:, :1]
    tokens = jnp.sum(s_count)
    t_local = t_sum / t_count
    t_mean = jnp.sum(t_sum, axis=0) / tokens
    t_off = t_local - t_mean
    t_var = (jnp.sum(t_square, axis=0) + jnp.sum(t_count * t_off * t_off, axis=0)) / tokens
    t_scale = lax.rsqrt(t_var + epsilon)
    t_rows = jnp.concatenate([t_off * t_scale, t_scale[None]])
    t_mate = swap(t_rows)
    s_mean = jnp.sum(s_sum, axis=0) / tokens
    s_off = s_sum / s_count - s_mean
    s_var = (jnp.sum(s_square, axis=0) + jnp.sum(s_count * s_off * s_off, axis=0)) / tokens
    s_scale = lax.rsqrt(s_var + epsilon) / jnp.sqrt(tokens)
    s_rows = s_off * s_scale * s_count

    place = jnp.stack([z, c]).astype(jnp.int32)
    opened = []
    for k in range(2):
        u_up, u_down, kept = product(place, k, lefts[0], owns[k], mates[k], means[0])
        opened.append((ring(u_up, "y", 1), ring(u_down, "y", -1), kept))
    out = None
    for k in range(2):
        u_up, u_down, kept = opened[k]
        v_up, v_down = product(place, k, lefts[1], owns[k], mates[k], means[1], (u_up, u_down))
        v_up, v_down = ring(v_up, "y", 1), ring(v_down, "y", -1)
        t_k = jnp.concatenate(
            [t[:, k * half : (k + 1) * half] for t in (t_rows, t_mate)], axis=1
        )
        between = lax.dot_general(
            s_rows, t_k[:-1], (((0,), (0,)), ((), ())), precision=lax.Precision.HIGHEST
        )
        out = final(
            place, k, kept, v_up, v_down, between, s_scale[:, None], t_k[-1:], out
        )
    return out[None, None]


def solution(mesh):
    fine = Mesh(mesh.devices.reshape(SIDE, SIDE, SIDE, 2), ("y", "x", "row", "col"))
    seq = ("y", "x")
    placed = (
        P(seq + ("row",), "col"),
        P(seq, ("row", "col")),
        P(seq),
        P(seq, None),
        P(seq, None),
    )
    return jax.shard_map(
        per_device,
        mesh=fine,
        in_specs=placed,
        out_specs=P("col", seq, None, "row"),
        check_vma=False,
    )
```

```python
import jax
import jax.numpy as jnp
from jax import lax
from jax.experimental import pallas as pl
from jax.experimental.pallas import tpu as pltpu
from jax.sharding import Mesh
from jax.sharding import PartitionSpec as P

SUB = 192
BAND = 4
HALO = 16
SIDE = 4
COMING = (0, SIDE - 1, 1, 2)
epsilon = 1e-05
f32 = jnp.float32
bf16 = jnp.bfloat16


def ring(value, axis, step):
    return lax.ppermute(value, axis, [(i, (i + step) % SIDE) for i in range(SIDE)])


def ring_all(value, axis):
    return [value, ring(value, axis, 1), ring(value, axis, -1), ring(value, axis, 2)]


def swap(value):
    return lax.ppermute(value, "col", [(0, 1), (1, 0)])


def after(value, *others):
    return lax.optimization_barrier((value, others))[0]


def smem():
    return pl.BlockSpec(memory_space=pltpu.SMEM)


def vmem():
    return pl.BlockSpec(memory_space=pltpu.VMEM)


def pack_kernel(place, student, *outs):
    y, x = place[0], place[1]
    part = outs[0].shape[1] // 2
    for r, x_step in enumerate((0, 1, SIDE - 1, 2)):
        for k, y_steps in enumerate(((2, 0), (1, SIDE - 1))):
            for i, y_step in enumerate(y_steps):
                slot = lax.rem(y + y_step, SIDE) * SIDE + lax.rem(x + x_step, SIDE)
                first = pl.multiple_of(slot * part, 128)
                outs[2 * r + k][:, i * part : (i + 1) * part] = student[:, pl.ds(first, part)]


def pack(place, student):
    part = student.shape[1] // (SIDE * SIDE)
    shape = jax.ShapeDtypeStruct((SUB, 2 * part), bf16)
    return pl.pallas_call(
        pack_kernel,
        in_specs=[smem(), vmem()],
        out_specs=[vmem()] * 8,
        out_shape=[shape] * 8,
        compiler_params=pltpu.CompilerParams(vmem_limit_bytes=16 * 2**20),
        cost_estimate=pl.CostEstimate(
            flops=0, bytes_accessed=4 * SUB * student.shape[1], transcendentals=0
        ),
    )(place, student)


def turn_kernel(own_count, p0, p1, p2, p3, turned, near):
    rows = jnp.concatenate([p[...] for p in (p0, p1, p2, p3)], axis=0)
    flat = rows.T
    turned[...] = flat
    mine = flat[:, :SUB].astype(f32)
    live = lax.broadcasted_iota(jnp.int32, mine.shape, 1) < own_count[0]
    total = jnp.sum(jnp.where(live, mine, 0.0), axis=1, keepdims=True)
    near[...] = total / own_count[0].astype(f32)


def turn(own_count, pieces):
    width = pieces[0].shape[1]
    return pl.pallas_call(
        turn_kernel,
        in_specs=[smem()] + [vmem()] * SIDE,
        out_specs=[vmem()] * 2,
        out_shape=[
            jax.ShapeDtypeStruct((width, SIDE * SUB), bf16),
            jax.ShapeDtypeStruct((width, 1), f32),
        ],
        compiler_params=pltpu.CompilerParams(vmem_limit_bytes=16 * 2**20),
        cost_estimate=pl.CostEstimate(
            flops=0, bytes_accessed=4 * SUB * SIDE * width, transcendentals=0
        ),
    )(own_count, *pieces)


def moments_kernel(counts, *refs):
    out = refs[-1]
    for r in range(SIDE):
        for k in range(2):
            value = refs[2 * r + k][...].astype(f32)
            columns = slice(k * value.shape[1], (k + 1) * value.shape[1])
            live = lax.broadcasted_iota(jnp.int32, value.shape, 0) < counts[r]
            total = jnp.sum(jnp.where(live, value, 0.0), axis=0, keepdims=True)
            dev = jnp.where(live, value - total / counts[r].astype(f32), 0.0)
            out[r : r + 1, columns] = total
            out[SIDE + r : SIDE + r + 1, columns] = jnp.sum(dev * dev, axis=0, keepdims=True)


def moments(counts, pieces):
    width = pieces[0].shape[1]
    return pl.pallas_call(
        moments_kernel,
        in_specs=[smem()] + [vmem()] * len(pieces),
        out_specs=vmem(),
        out_shape=jax.ShapeDtypeStruct((2 * SIDE, 2 * width), f32),
        compiler_params=pltpu.CompilerParams(vmem_limit_bytes=16 * 2**20),
        cost_estimate=pl.CostEstimate(
            flops=8 * SUB * SIDE * width, bytes_accessed=4 * SUB * SIDE * width, transcendentals=0
        ),
    )(counts, *pieces)


def shards_kernel(counts, *refs):
    blocks, teachers, out = refs[:SIDE], refs[SIDE : 2 * SIDE], refs[-1]
    for r in range(SIDE):
        for i in range(3):
            out[i * SIDE + r : i * SIDE + r + 1, :] = teachers[r][i : i + 1, :]
        size = [counts[q * SIDE + r].astype(f32) for q in range(SIDE)]
        totals = [b[r : r + 1, :] for b in blocks]
        total = totals[0] + totals[1] + totals[2] + totals[3]
        mean = total / (size[0] + size[1] + size[2] + size[3])
        square = jnp.zeros_like(total)
        for q in range(SIDE):
            off = totals[q] / size[q] - mean
            square = square + blocks[q][SIDE + r : SIDE + r + 1, :] + size[q] * off * off
        out[3 * SIDE + r : 3 * SIDE + r + 1, :] = total
        out[4 * SIDE + r : 4 * SIDE + r + 1, :] = square


def shards(counts, blocks, teachers):
    columns = blocks[0].shape[1]
    return pl.pallas_call(
        shards_kernel,
        in_specs=[smem()] + [vmem()] * (2 * SIDE),
        out_specs=vmem(),
        out_shape=jax.ShapeDtypeStruct((5 * SIDE, columns), f32),
        compiler_params=pltpu.CompilerParams(vmem_limit_bytes=8 * 2**20),
    )(counts, *blocks, *teachers)


def settle_kernel(e0, e1, e2, e3, t_rows, s_left, work):
    every = (e0, e1, e2, e3)
    part = work.shape[1]

    def pieces(first, columns):
        return [e[first * SIDE : (first + 1) * SIDE, c] for e, c in zip(every, columns)]

    def combine(totals, squares, counts):
        tokens = sum(jnp.sum(n, axis=0, keepdims=True) for n in counts)
        mean = sum(jnp.sum(t, axis=0, keepdims=True) for t in totals) / tokens
        offs = [t / n - mean for t, n in zip(totals, counts)]
        square = sum(
            jnp.sum(q + n * o * o, axis=0, keepdims=True)
            for q, n, o in zip(squares, counts, offs)
        )
        return offs, lax.rsqrt(square / tokens + epsilon), tokens

    whole = [slice(None)] * SIDE
    offs, scale, _ = combine(pieces(0, whole), pieces(1, whole), pieces(2, whole))
    for j in range(SIDE):
        t_rows[j * SIDE : (j + 1) * SIDE, :] = offs[j] * scale
    t_rows[SIDE * SIDE : SIDE * SIDE + 1, :] = scale
    slots = [slice(i * part, (i + 1) * part) for i in (1, 2, 3, 0)]
    counts = pieces(2, [slice(0, part)] * SIDE)
    offs, scale, tokens = combine(pieces(3, slots), pieces(4, slots), counts)
    scale = scale / jnp.sqrt(tokens)
    work[...] = jnp.zeros_like(work)
    for j in range(SIDE):
        work[j * SIDE : (j + 1) * SIDE, :] = offs[j] * scale * counts[j]
    work[SIDE * SIDE : SIDE * SIDE + 1, :] = scale
    s_left[...] = work[...].T


def settle(every):
    columns = every[0].shape[1]
    part = columns // SIDE
    return pl.pallas_call(
        settle_kernel,
        in_specs=[vmem()] * SIDE,
        out_specs=[vmem()] * 2,
        out_shape=[
            jax.ShapeDtypeStruct((SIDE * SIDE + 1, columns), f32),
            jax.ShapeDtypeStruct((part, 128), f32),
        ],
        scratch_shapes=[pltpu.VMEM((128, part), f32)],
        compiler_params=pltpu.CompilerParams(vmem_limit_bytes=8 * 2**20),
    )(*every)


def pool_kernel(counts, before, teacher, behind, meta, full, first, second, stats, mix, share, pooled):
    window = SUB + 2 * HALO
    length = teacher.shape[0]
    j = pl.program_id(0)

    @pl.when(j == 0)
    def _():
        for r in range(SIDE):
            rows = slice(r * SUB, (r + 1) * SUB)
            place = lax.broadcasted_iota(jnp.int32, (SUB, window), 1)
            local = meta[rows, 0:1] - (r * SUB - HALO)
            found = jnp.zeros((SUB, window), jnp.int32)
            whole = jnp.zeros((SUB, 1), jnp.int32)
            for k in range(BAND):
                weight = meta[rows, 1 + k : 2 + k]
                found = found + jnp.where(place == local + k, weight, 0)
                whole = whole + weight
            mix[rows, :] = found.astype(f32).astype(bf16)
            share[rows, :] = jnp.broadcast_to(whole.astype(f32), (SUB, 128))

    total = jnp.zeros((1, teacher.shape[1]), f32)
    alive = jnp.int32(0)
    for r in range(SIDE):
        rows = slice(r * SUB, (r + 1) * SUB)
        low, high = r * SUB - HALO, (r + 1) * SUB + HALO
        parts = [teacher[max(low, 0) : min(high, length), :]]
        if low < 0:
            parts = [before[...]] + parts
        if high > length:
            parts = parts + [behind[...]]
        seen = jnp.concatenate(parts, axis=0) if len(parts) > 1 else parts[0]
        value = jnp.dot(mix[rows, :], seen, preferred_element_type=f32)
        value = value / share[rows, 0:1]
        pooled[rows, :] = value
        live = lax.broadcasted_iota(jnp.int32, value.shape, 0) < counts[r]
        total = total + jnp.sum(jnp.where(live, value, 0.0), axis=0, keepdims=True)
        alive = alive + counts[r]
    mean = total / alive.astype(f32)
    square = jnp.zeros_like(total)
    for r in range(SIDE):
        rows = slice(r * SUB, (r + 1) * SUB)
        value = pooled[rows, :]
        live = lax.broadcasted_iota(jnp.int32, value.shape, 0) < counts[r]
        dev = jnp.where(live, value - mean, 0.0)
        small = dev.astype(bf16)
        full[rows, :] = small

        @pl.when(j < pl.num_programs(0) // 2)
        def _():
            first[rows, :] = small

        @pl.when(j >= pl.num_programs(0) // 2)
        def _():
            second[rows, :] = small

        square = square + jnp.sum(dev * dev, axis=0, keepdims=True)
    stats[0:1, :] = total
    stats[1:2, :] = square
    stats[2:3, :] = jnp.broadcast_to(alive.astype(f32), total.shape)
    lane = lax.broadcasted_iota(jnp.int32, total.shape, 1)
    row = jnp.zeros(total.shape, jnp.int32)
    for r in range(SIDE):
        row = row + jnp.where(lane == r, counts[r], 0)
    stats[3:4, :] = row.astype(f32)


def pool(counts, before, teacher, behind, meta):
    rows, columns = teacher.shape
    tile = 256
    last = columns // tile // 2
    return pl.pallas_call(
        pool_kernel,
        grid=(columns // tile,),
        in_specs=[
            smem(),
            pl.BlockSpec((HALO, tile), lambda j: (0, j)),
            pl.BlockSpec((rows, tile), lambda j: (0, j)),
            pl.BlockSpec((HALO, tile), lambda j: (0, j)),
            pl.BlockSpec(meta.shape, lambda j: (0, 0)),
        ],
        out_specs=[
            pl.BlockSpec((rows, tile), lambda j: (0, j)),
            pl.BlockSpec((rows, tile), lambda j: (0, jnp.minimum(j, last - 1))),
            pl.BlockSpec((rows, tile), lambda j: (0, jnp.maximum(j - last, 0))),
            pl.BlockSpec((4, tile), lambda j: (0, j)),
        ],
        out_shape=[
            jax.ShapeDtypeStruct((rows, columns), bf16),
            jax.ShapeDtypeStruct((rows, columns // 2), bf16),
            jax.ShapeDtypeStruct((rows, columns // 2), bf16),
            jax.ShapeDtypeStruct((4, columns), f32),
        ],
        scratch_shapes=[
            pltpu.VMEM((rows, SUB + 2 * HALO), bf16),
            pltpu.VMEM((rows, 128), f32),
            pltpu.VMEM((rows, tile), f32),
        ],
        compiler_params=pltpu.CompilerParams(vmem_limit_bytes=32 * 2**20),
        cost_estimate=pl.CostEstimate(
            flops=2 * rows * 256 * columns, bytes_accessed=6 * rows * columns, transcendentals=0
        ),
    )(counts, before, teacher, behind, meta)


def sums_of(place, near, left, right):
    z = place[0]
    total = None
    for a, step in zip(left, COMING):
        first = pl.multiple_of(lax.rem(z + step, SIDE) * SUB, 16)
        rows = pl.ds(first, SUB)
        far = jnp.concatenate([right[3][rows, :], right[4][rows, :]], axis=1)
        b = jnp.concatenate([right[0][rows, :], right[1][rows, :], right[2][rows, :], far], axis=0)
        term = jnp.dot(a, b, preferred_element_type=f32)
        total = term if total is None else total + term
    part = total.shape[0] - 16
    return total[:part] - near * total[part : part + 1]


def left_of(refs, i):
    ones = jnp.ones((16, refs[0].shape[1]), bf16)
    far = jnp.where(i == 0, refs[3][...], refs[4][...])
    return [jnp.concatenate([a, ones], axis=0) for a in [r[...] for r in refs[:3]] + [far]]


def open_kernel(place, *refs):
    left, own, mate, near = refs[:5], refs[5:10], refs[10:15], refs[15]
    up, down, kept = refs[16:]
    i = pl.program_id(0)
    half = up.shape[1]
    a = left_of(left, i)
    results = [sums_of(place, near[...], a, side) for side in (own, mate)]

    @pl.when(i == 0)
    def _():
        up[...] = results[0].astype(bf16)
        down[...] = results[1].astype(bf16)

    @pl.when(i == 1)
    def _():
        kept[:, :half] = results[0]
        kept[:, half:] = results[1]


def close_kernel(place, *refs):
    left, own, mate, near = refs[:5], refs[5:10], refs[10:15], refs[15]
    from_back, from_next, up, down = refs[16:]
    i = pl.program_id(0)
    half = from_back.shape[1]
    a = left_of(left, i)
    results = [sums_of(place, near[...], a, side) for side in (own, mate)]

    @pl.when(i == 0)
    def _():
        up[:, :half] = (results[0] + from_back[...].astype(f32)).astype(bf16)
        up[:, half:] = results[1].astype(bf16)

    @pl.when(i == 1)
    def _():
        down[:, :half] = results[0].astype(bf16)
        down[:, half:] = (results[1] + from_next[...].astype(f32)).astype(bf16)


def product(place, k, left, own, mate, near, arrived=None):
    depth = left[0].shape[1]
    part = left[0].shape[0] // 2
    rows = own[1].shape[0]
    half = own[1].shape[1]
    one = lambda i, place: (0, 0)
    side = (
        [pl.BlockSpec((rows, half), lambda i, place: (0, k))]
        + [pl.BlockSpec((rows, half), one)] * 2
        + [pl.BlockSpec((rows, half // 2), one)] * 2
    )
    in_specs = (
        [pl.BlockSpec((part, depth), lambda i, place: (i, 0))] * 3
        + [pl.BlockSpec((part, depth), one)] * 2
        + side * 2
        + [pl.BlockSpec((part, 1), lambda i, place: (i, 0))]
    )
    S = jax.ShapeDtypeStruct
    if arrived is None:
        kernel, extra = open_kernel, ()
        shapes = [S((part, half), bf16), S((part, half), bf16), S((part, 2 * half), f32)]
    else:
        kernel, extra = close_kernel, arrived
        in_specs = in_specs + [pl.BlockSpec((part, half), one)] * 2
        shapes = [S((part, 2 * half), bf16), S((part, 2 * half), bf16)]
    return pl.pallas_call(
        kernel,
        grid_spec=pltpu.PrefetchScalarGridSpec(
            num_scalar_prefetch=1,
            grid=(2,),
            in_specs=in_specs,
            out_specs=[pl.BlockSpec(s.shape, one) for s in shapes],
        ),
        out_shape=shapes,
        compiler_params=pltpu.CompilerParams(vmem_limit_bytes=40 * 2**20),
        cost_estimate=pl.CostEstimate(
            flops=2 * 2 * part * depth * SIDE * 2 * half,
            bytes_accessed=2 * SIDE * depth * (2 * part + 2 * half) + 6 * part * half,
            transcendentals=0,
        ),
    )(place, *left, *own, *mate, near, *extra)


def final_kernel(place, kept, first, second, s_left, t_own, t_mate, *rest):
    out = rest[-1]
    t = jnp.where(pl.program_id(0) == 0, t_own[...], t_mate[...])
    shards_all = SIDE * SIDE
    between = jnp.dot(
        s_left[:, :shards_all],
        t[:shards_all],
        preferred_element_type=f32,
        precision=lax.Precision.HIGHEST,
    )
    inside = kept[...] + first[...].astype(f32) + second[...].astype(f32)
    row_scale = s_left[:, shards_all : shards_all + 1]
    out[...] = inside * row_scale * t[shards_all : shards_all + 1] + between


def final(place, k, kept, first, second, s_left, t_own, t_mate, whole=None):
    part, columns = kept.shape
    half = columns // 2
    block = pl.BlockSpec((part, half), lambda i, place: (0, i))
    in_specs = (
        [block] * 3
        + [pl.BlockSpec(s_left.shape, lambda i, place: (0, 0))]
        + [pl.BlockSpec((t_own.shape[0], half), lambda i, place: (0, k))] * 2
    )
    more, aliases = (), {}
    if whole is not None:
        in_specs = in_specs + [pl.BlockSpec(memory_space=pl.ANY)]
        more, aliases = (whole,), {7: 0}
    return pl.pallas_call(
        final_kernel,
        grid_spec=pltpu.PrefetchScalarGridSpec(
            num_scalar_prefetch=1,
            grid=(2,),
            in_specs=in_specs,
            out_specs=pl.BlockSpec(
                (part, half), lambda i, place: (0, lax.rem(place[1] + i, 2) * 2 + k)
            ),
        ),
        out_shape=jax.ShapeDtypeStruct((part, 2 * columns), f32),
        input_output_aliases=aliases,
        compiler_params=pltpu.CompilerParams(vmem_limit_bytes=16 * 2**20),
        cost_estimate=pl.CostEstimate(
            flops=6 * part * columns, bytes_accessed=12 * part * columns, transcendentals=0
        ),
    )(place, kept, first, second, s_left, t_own, t_mate, *more)


def per_device(student, teacher, starts, weights, counts):
    y, x, z, c = (lax.axis_index(n) for n in ("y", "x", "row", "col"))
    shard = y * SIDE + x
    rows = starts.shape[0]
    columns = teacher.shape[1]
    half = columns // 2
    width = student.shape[1] // SIDE
    part = width // SIDE

    up = [(i, (i + 1) % 16) for i in range(16)]
    down = [(j, i) for i, j in up]
    before = lax.ppermute(teacher[rows - HALO :], ("y", "x"), up)
    behind = lax.ppermute(teacher[:HALO], ("y", "x"), down)

    steps = (0, 1, -1, 2)

    def send_x(chunk):
        return [chunk[0]] + [ring(chunk[r], "x", steps[r]) for r in (1, 2, 3)]

    packed = pack(jnp.stack([y, x]).astype(jnp.int32), student)
    packed, before, behind = lax.optimization_barrier((packed, before, behind))
    got0 = send_x(packed[0::2])
    meta = jnp.concatenate([(starts - shard * rows)[:, None], weights], axis=1)
    standard, half0, half1, stats = pool(counts[0], before, teacher, behind, meta)
    near = ring_all(stats, "x")
    got0, standard, half0, half1, packed1 = lax.optimization_barrier(
        (got0, standard, half0, half1, packed[1::2])
    )

    got1 = send_x(packed1)
    own_count = lax.dynamic_slice_in_dim(counts[0], z, 1)
    turned0, mean0 = turn(own_count, got0)
    up0, down0 = ring(turned0, "row", 1), ring(turned0, "row", -1)
    got1, half0, near, _ = lax.optimization_barrier((got1, half0, near, turned0))

    quarter = half // 2
    right0, left0 = ring(half0, "x", 1), ring(half0, "x", -1)
    turned1, mean1 = turn(own_count, got1)
    t_standard = swap(standard)
    group = jnp.stack([n[3, :SIDE] for n in near])
    z_counts = jnp.stack(
        [lax.dynamic_index_in_dim(group, lax.rem(z + k, SIDE), 1, keepdims=False) for k in COMING]
    )
    z_counts = z_counts.reshape(SIDE * SIDE).astype(jnp.int32)
    pieces = [p for pair in zip(got0, got1) for p in pair]
    moment = moments(z_counts, pieces)
    up0, down0, turned1, moment = lax.optimization_barrier((up0, down0, turned1, moment))
    far0 = [ring(up0[:part], "row", 1), ring(down0[part:], "row", -1)]
    t_right0, t_left0 = swap(right0), swap(left0)
    right0, left0, moment, _ = lax.optimization_barrier((right0, left0, moment, up0))
    x_far0 = [ring(right0[:, :quarter], "x", 1), ring(left0[:, quarter:], "x", -1)]
    far0, turned1, moment = lax.optimization_barrier((far0, turned1, moment))
    every_z = ring_all(moment, "row")
    turned1 = after(turned1, every_z)
    up1, down1 = ring(turned1, "row", 1), ring(turned1, "row", -1)
    t_x_far0 = [swap(f) for f in x_far0]
    x_far0, half1 = lax.optimization_barrier((x_far0, half1))
    right1, left1 = ring(half1, "x", 1), ring(half1, "x", -1)

    every = ring_all(shards(z_counts, every_z, near), "y")
    t_rows, s_left = settle(every)
    t_mate = swap(t_rows)

    place = jnp.stack([z, c]).astype(jnp.int32)
    z0 = [turned0, up0, down0] + far0
    own0 = [standard, right0, left0] + x_far0
    mate0 = [t_standard, t_right0, t_left0] + t_x_far0
    open0 = product(place, 0, z0, own0, mate0, mean0)
    open0, up1, down1, right1, left1 = lax.optimization_barrier(
        (open0, up1, down1, right1, left1)
    )
    u0 = [ring(open0[0], "y", 1), ring(open0[1], "y", -1)]
    far1 = [ring(up1[:part], "row", 1), ring(down1[part:], "row", -1)]
    x_far1 = [ring(right1[:, :quarter], "x", 1), ring(left1[:, quarter:], "x", -1)]
    t_right1, t_left1 = swap(right1), swap(left1)
    u0, far1, t_rows, t_mate, s_left = lax.optimization_barrier((u0, far1, t_rows, t_mate, s_left))
    z1 = [turned1, up1, down1] + far1
    close0 = product(place, 0, z1, own0, mate0, mean1, u0)
    close0, x_far1 = lax.optimization_barrier((close0, x_far1))
    v0 = [ring(close0[0], "y", 1), ring(close0[1], "y", -1)]
    t_x_far1 = [swap(f) for f in x_far1]
    own1 = [standard, right1, left1] + x_far1
    mate1 = [t_standard, t_right1, t_left1] + t_x_far1
    open1 = product(place, 1, z0, own1, mate1, mean0)
    u1 = [ring(open1[0], "y", 1), ring(open1[1], "y", -1)]
    close1 = product(place, 1, z1, own1, mate1, mean1, u1)
    v1 = [ring(close1[0], "y", 1), ring(close1[1], "y", -1)]
    out = final(place, 0, open0[2], *v0, s_left, t_rows, t_mate)
    out = final(place, 1, open1[2], *v1, s_left, t_rows, t_mate, out)
    return out[None, None]


def solution(mesh):
    fine = Mesh(mesh.devices.reshape(SIDE, SIDE, SIDE, 2), ("y", "x", "row", "col"))
    seq = ("y", "x")
    placed = (
        P(seq + ("row",), "col"),
        P(seq, ("row", "col")),
        P(seq),
        P(seq, None),
        P(seq, None),
    )
    return jax.shard_map(
        per_device,
        mesh=fine,
        in_specs=placed,
        out_specs=P("col", seq, None, "row"),
        check_vma=False,
    )
```

```python
import jax
import jax.numpy as jnp
from jax import lax
from jax.experimental import pallas as pl
from jax.experimental.pallas import tpu as pltpu
from jax.sharding import Mesh
from jax.sharding import PartitionSpec as P

SUB = 192
BAND = 4
HALO = 16
SIDE = 4
COMING = (0, SIDE - 1, 1, 2)
epsilon = 1e-05
f32 = jnp.float32
bf16 = jnp.bfloat16


def ring(value, axis, step):
    return lax.ppermute(value, axis, [(i, (i + step) % SIDE) for i in range(SIDE)])


def ring_all(value, axis):
    return [value, ring(value, axis, 1), ring(value, axis, -1), ring(value, axis, 2)]


def swap(value):
    return lax.ppermute(value, "col", [(0, 1), (1, 0)])


def after(value, *others):
    return lax.optimization_barrier((value, others))[0]


def smem():
    return pl.BlockSpec(memory_space=pltpu.SMEM)


def vmem():
    return pl.BlockSpec(memory_space=pltpu.VMEM)


def pack_kernel(place, student, *outs):
    y, x, count = place[0], place[1], place[2]
    moments = outs[SIDE]
    part = outs[0].shape[1] // SIDE
    for r, x_step in enumerate((0, 1, SIDE - 1, 2)):
        at = lax.rem(x + x_step, SIDE)
        for i, y_step in enumerate((2, 0, 1, SIDE - 1)):
            slot = lax.rem(y + y_step, SIDE) * SIDE + at
            first = pl.multiple_of(slot * part, 128)
            columns = slice(i * part, (i + 1) * part)
            block = student[:, pl.ds(first, part)]
            outs[r][:, columns] = block
            value = block.astype(f32)
            live = lax.broadcasted_iota(jnp.int32, value.shape, 0) < count
            total = jnp.sum(jnp.where(live, value, 0.0), axis=0, keepdims=True)
            dev = jnp.where(live, value - total / count.astype(f32), 0.0)
            moments[r : r + 1, columns] = total
            moments[SIDE + r : SIDE + r + 1, columns] = jnp.sum(dev * dev, axis=0, keepdims=True)


def pack(place, student):
    width = student.shape[1] // SIDE
    return pl.pallas_call(
        pack_kernel,
        in_specs=[smem(), vmem()],
        out_specs=[vmem()] * (SIDE + 1),
        out_shape=[jax.ShapeDtypeStruct((SUB, width), bf16)] * SIDE
        + [jax.ShapeDtypeStruct((2 * SIDE, width), f32)],
        compiler_params=pltpu.CompilerParams(vmem_limit_bytes=24 * 2**20),
        cost_estimate=pl.CostEstimate(
            flops=8 * SUB * student.shape[1],
            bytes_accessed=4 * SUB * student.shape[1],
            transcendentals=0,
        ),
    )(place, student)


def turn_kernel(own_count, p0, p1, p2, p3, turned, near):
    rows = jnp.concatenate([p[...] for p in (p0, p1, p2, p3)], axis=0)
    flat = rows.T
    turned[...] = flat
    mine = flat[:, :SUB].astype(f32)
    live = lax.broadcasted_iota(jnp.int32, mine.shape, 1) < own_count[0]
    total = jnp.sum(jnp.where(live, mine, 0.0), axis=1, keepdims=True)
    near[...] = total / own_count[0].astype(f32)


def turn(own_count, pieces):
    width = pieces[0].shape[1]
    return pl.pallas_call(
        turn_kernel,
        in_specs=[smem()] + [vmem()] * SIDE,
        out_specs=[vmem()] * 2,
        out_shape=[
            jax.ShapeDtypeStruct((width, SIDE * SUB), bf16),
            jax.ShapeDtypeStruct((width, 1), f32),
        ],
        compiler_params=pltpu.CompilerParams(vmem_limit_bytes=16 * 2**20),
        cost_estimate=pl.CostEstimate(
            flops=0, bytes_accessed=4 * SUB * SIDE * width, transcendentals=0
        ),
    )(own_count, *pieces)


def shards_kernel(counts, teacher, *refs):
    blocks, out = refs[:SIDE], refs[-1]
    out[:SIDE, :] = teacher[...]
    size = [counts[q].astype(f32) for q in range(SIDE)]
    totals = [b[:SIDE, :] for b in blocks]
    total = totals[0] + totals[1] + totals[2] + totals[3]
    mean = total / (size[0] + size[1] + size[2] + size[3])
    square = jnp.zeros_like(total)
    for q in range(SIDE):
        off = totals[q] / size[q] - mean
        square = square + blocks[q][SIDE:, :] + size[q] * off * off
    out[SIDE : 2 * SIDE, :] = total
    out[2 * SIDE :, :] = square


def shards(counts, teacher, blocks):
    columns = blocks[0].shape[1]
    return pl.pallas_call(
        shards_kernel,
        in_specs=[smem()] + [vmem()] * (1 + SIDE),
        out_specs=vmem(),
        out_shape=jax.ShapeDtypeStruct((3 * SIDE, columns), f32),
        compiler_params=pltpu.CompilerParams(vmem_limit_bytes=8 * 2**20),
    )(counts, teacher, *blocks)


def gather_kernel(n0, n1, n2, n3, out):
    for r, (n, row) in enumerate(zip((n0, n1, n2, n3), (0, 1, 2, 3))):
        for i in range(3):
            out[i * SIDE + r : i * SIDE + r + 1, :] = n[i : i + 1, :]
        for i in range(2):
            at = (1 + i) * SIDE + row
            out[(3 + i) * SIDE + r : (3 + i) * SIDE + r + 1, :] = n[at : at + 1, :]


def gather_stats(near):
    columns = near[0].shape[1]
    return pl.pallas_call(
        gather_kernel,
        in_specs=[vmem()] * SIDE,
        out_specs=vmem(),
        out_shape=jax.ShapeDtypeStruct((5 * SIDE, columns), f32),
        compiler_params=pltpu.CompilerParams(vmem_limit_bytes=8 * 2**20),
    )(*near)


def settle_kernel(e0, e1, e2, e3, t_rows, s_left, work):
    every = (e0, e1, e2, e3)
    part = work.shape[1]

    def pieces(first, columns):
        return [e[first * SIDE : (first + 1) * SIDE, c] for e, c in zip(every, columns)]

    def combine(totals, squares, counts):
        tokens = sum(jnp.sum(n, axis=0, keepdims=True) for n in counts)
        mean = sum(jnp.sum(t, axis=0, keepdims=True) for t in totals) / tokens
        offs = [t / n - mean for t, n in zip(totals, counts)]
        square = sum(
            jnp.sum(q + n * o * o, axis=0, keepdims=True)
            for q, n, o in zip(squares, counts, offs)
        )
        return offs, lax.rsqrt(square / tokens + epsilon), tokens

    whole = [slice(None)] * SIDE
    offs, scale, _ = combine(pieces(0, whole), pieces(1, whole), pieces(2, whole))
    for j in range(SIDE):
        t_rows[j * SIDE : (j + 1) * SIDE, :] = offs[j] * scale
    t_rows[SIDE * SIDE : SIDE * SIDE + 1, :] = scale
    slots = [slice(i * part, (i + 1) * part) for i in (1, 2, 3, 0)]
    counts = pieces(2, [slice(0, part)] * SIDE)
    offs, scale, tokens = combine(pieces(3, slots), pieces(4, slots), counts)
    scale = scale / jnp.sqrt(tokens)
    work[...] = jnp.zeros_like(work)
    for j in range(SIDE):
        work[j * SIDE : (j + 1) * SIDE, :] = offs[j] * scale * counts[j]
    work[SIDE * SIDE : SIDE * SIDE + 1, :] = scale
    s_left[...] = work[...].T


def settle(every):
    columns = every[0].shape[1]
    part = columns // SIDE
    return pl.pallas_call(
        settle_kernel,
        in_specs=[vmem()] * SIDE,
        out_specs=[vmem()] * 2,
        out_shape=[
            jax.ShapeDtypeStruct((SIDE * SIDE + 1, columns), f32),
            jax.ShapeDtypeStruct((part, 128), f32),
        ],
        scratch_shapes=[pltpu.VMEM((128, part), f32)],
        compiler_params=pltpu.CompilerParams(vmem_limit_bytes=8 * 2**20),
    )(*every)


def pool_kernel(counts, before, teacher, behind, meta, full, stats, mix, share, pooled):
    window = SUB + 2 * HALO
    length = teacher.shape[0]
    j = pl.program_id(0)

    @pl.when(j == 0)
    def _():
        for r in range(SIDE):
            rows = slice(r * SUB, (r + 1) * SUB)
            place = lax.broadcasted_iota(jnp.int32, (SUB, window), 1)
            local = meta[rows, 0:1] - (r * SUB - HALO)
            found = jnp.zeros((SUB, window), jnp.int32)
            whole = jnp.zeros((SUB, 1), jnp.int32)
            for k in range(BAND):
                weight = meta[rows, 1 + k : 2 + k]
                found = found + jnp.where(place == local + k, weight, 0)
                whole = whole + weight
            mix[rows, :] = found.astype(f32).astype(bf16)
            share[rows, :] = jnp.broadcast_to(whole.astype(f32), (SUB, 128))

    total = jnp.zeros((1, teacher.shape[1]), f32)
    alive = jnp.int32(0)
    for r in range(SIDE):
        rows = slice(r * SUB, (r + 1) * SUB)
        low, high = r * SUB - HALO, (r + 1) * SUB + HALO
        parts = [teacher[max(low, 0) : min(high, length), :]]
        if low < 0:
            parts = [before[...]] + parts
        if high > length:
            parts = parts + [behind[...]]
        seen = jnp.concatenate(parts, axis=0) if len(parts) > 1 else parts[0]
        value = jnp.dot(mix[rows, :], seen, preferred_element_type=f32)
        value = value / share[rows, 0:1]
        pooled[rows, :] = value
        live = lax.broadcasted_iota(jnp.int32, value.shape, 0) < counts[r]
        total = total + jnp.sum(jnp.where(live, value, 0.0), axis=0, keepdims=True)
        alive = alive + counts[r]
    mean = total / alive.astype(f32)
    square = jnp.zeros_like(total)
    for r in range(SIDE):
        rows = slice(r * SUB, (r + 1) * SUB)
        value = pooled[rows, :]
        live = lax.broadcasted_iota(jnp.int32, value.shape, 0) < counts[r]
        dev = jnp.where(live, value - mean, 0.0)
        small = dev.astype(bf16)
        full[rows, :] = small
        square = square + jnp.sum(dev * dev, axis=0, keepdims=True)
    stats[0:1, :] = total
    stats[1:2, :] = square
    stats[2:3, :] = jnp.broadcast_to(alive.astype(f32), total.shape)
    lane = lax.broadcasted_iota(jnp.int32, total.shape, 1)
    row = jnp.zeros(total.shape, jnp.int32)
    for r in range(SIDE):
        row = row + jnp.where(lane == r, counts[r], 0)
    stats[3:4, :] = row.astype(f32)


def pool(counts, before, teacher, behind, meta):
    rows, columns = teacher.shape
    tile = 256
    return pl.pallas_call(
        pool_kernel,
        grid=(columns // tile,),
        in_specs=[
            smem(),
            pl.BlockSpec((HALO, tile), lambda j: (0, j)),
            pl.BlockSpec((rows, tile), lambda j: (0, j)),
            pl.BlockSpec((HALO, tile), lambda j: (0, j)),
            pl.BlockSpec(meta.shape, lambda j: (0, 0)),
        ],
        out_specs=[
            pl.BlockSpec((rows, tile), lambda j: (0, j)),
            pl.BlockSpec((4, tile), lambda j: (0, j)),
        ],
        out_shape=[
            jax.ShapeDtypeStruct((rows, columns), bf16),
            jax.ShapeDtypeStruct((4, columns), f32),
        ],
        scratch_shapes=[
            pltpu.VMEM((rows, SUB + 2 * HALO), bf16),
            pltpu.VMEM((rows, 128), f32),
            pltpu.VMEM((rows, tile), f32),
        ],
        compiler_params=pltpu.CompilerParams(vmem_limit_bytes=32 * 2**20),
        cost_estimate=pl.CostEstimate(
            flops=2 * rows * 256 * columns, bytes_accessed=6 * rows * columns, transcendentals=0
        ),
    )(counts, before, teacher, behind, meta)


def with_ones(a):
    return jnp.concatenate([a, jnp.ones((16, a.shape[1]), bf16)], axis=0)


def less_mean(total, near):
    part = total.shape[0] - 16
    return total[:part] - near * total[part : part + 1]


def first_kernel(place, a0, a1, a2, b0, b1, b2, near, out):
    z = place[0]
    depth = a0.shape[1]
    fill = jnp.zeros((depth - 3 * SUB, b0.shape[1]), bf16)
    total = None
    for a, step in zip((a0, a1, a2), COMING):
        rows = pl.ds(pl.multiple_of(lax.rem(z + step, SIDE) * SUB, 16), SUB)
        b = jnp.concatenate([b0[rows, :], b1[rows, :], b2[rows, :], fill], axis=0)
        term = jnp.dot(with_ones(a[...]), b, preferred_element_type=f32)
        total = term if total is None else total + term
    out[...] = less_mean(total, near[...])


def first_product(place, left, right, near):
    rows, depth = left[0].shape
    part = rows // SIDE
    length, columns = right[0].shape
    near_depth = 640
    return pl.pallas_call(
        first_kernel,
        grid_spec=pltpu.PrefetchScalarGridSpec(
            num_scalar_prefetch=1,
            grid=(SIDE,),
            in_specs=[pl.BlockSpec((part, near_depth), lambda i, place: (i, 0))] * 3
            + [pl.BlockSpec((length, columns), lambda i, place: (0, 0))] * 3
            + [pl.BlockSpec((part, 1), lambda i, place: (i, 0))],
            out_specs=pl.BlockSpec((part, columns), lambda i, place: (i, 0)),
        ),
        out_shape=jax.ShapeDtypeStruct((rows, columns), f32),
        compiler_params=pltpu.CompilerParams(vmem_limit_bytes=40 * 2**20),
        cost_estimate=pl.CostEstimate(
            flops=2 * rows * 3 * near_depth * columns,
            bytes_accessed=6 * rows * depth + 6 * length * columns + 4 * rows * columns,
            transcendentals=0,
        ),
    )(place, *left, *right, near)


def last_sums(place, refs):
    z = place[0]
    tails, far_a, near = refs[:3], refs[3], refs[4]
    sides = (refs[5:10], refs[10:15])
    results = []
    lefts = [with_ones(t[...]) for t in tails]
    far_left = with_ones(far_a[...])
    for b0, b1, b2, far_b, done in sides:
        fill = jnp.zeros((tails[0].shape[1] - SUB, far_b.shape[1]), bf16)
        total = None
        for a, step in zip(lefts, COMING):
            rows = pl.ds(pl.multiple_of(lax.rem(z + step, SIDE) * SUB, 16), SUB)
            b = jnp.concatenate([fill, far_b[rows, :]], axis=0)
            term = jnp.dot(a, b, preferred_element_type=f32)
            total = term if total is None else total + term
        rows = pl.ds(pl.multiple_of(lax.rem(z + 2, SIDE) * SUB, 16), SUB)
        b = jnp.concatenate([b0[...], b1[...], b2[...], far_b[rows, :]], axis=0)
        total = total + jnp.dot(far_left, b, preferred_element_type=f32)
        results.append(less_mean(total, near[...]) + done[...])
    return results


def open_kernel(place, *refs):
    up, down, kept = refs[15:]
    i = pl.program_id(0)
    half = up.shape[1]
    results = last_sums(place, refs)

    @pl.when(i == 0)
    def _():
        up[...] = results[0].astype(bf16)
        down[...] = results[1].astype(bf16)

    @pl.when(i == 1)
    def _():
        kept[:, :half] = results[0]
        kept[:, half:] = results[1]


def close_kernel(place, *refs):
    from_back, from_next, up, down = refs[15:]
    i = pl.program_id(0)
    half = from_back.shape[1]
    results = last_sums(place, refs)

    @pl.when(i == 0)
    def _():
        up[:, :half] = (results[0] + from_back[...].astype(f32)).astype(bf16)
        up[:, half:] = results[1].astype(bf16)

    @pl.when(i == 1)
    def _():
        down[:, :half] = results[0].astype(bf16)
        down[:, half:] = (results[1] + from_next[...].astype(f32)).astype(bf16)


def last_product(place, k, left, far_left, near, own, mate, arrived=None):
    depth = left[0].shape[1]
    part = left[0].shape[0] // SIDE
    half = own[0].shape[1] // 2
    start = 0 if arrived is None else 2
    one = lambda i, place: (0, 0)
    tail = 256
    side = (
        [pl.BlockSpec((SUB, half), lambda i, place: (lax.rem(place[0] + 2, SIDE), k))] * 3
        + [pl.BlockSpec((own[3].shape[0], half), one)]
        + [pl.BlockSpec((part, half), lambda i, place: (start + i, k))]
    )
    in_specs = (
        [pl.BlockSpec((part, tail), lambda i, place: (start + i, depth // tail - 1))] * 3
        + [pl.BlockSpec((part, depth), lambda i, place: (i, 0))]
        + [pl.BlockSpec((part, 1), lambda i, place: (start + i, 0))]
        + side * 2
    )
    S = jax.ShapeDtypeStruct
    if arrived is None:
        kernel, extra = open_kernel, ()
        shapes = [S((part, half), bf16), S((part, half), bf16), S((part, 2 * half), f32)]
    else:
        kernel, extra = close_kernel, arrived
        in_specs = in_specs + [pl.BlockSpec((part, half), one)] * 2
        shapes = [S((part, 2 * half), bf16), S((part, 2 * half), bf16)]
    return pl.pallas_call(
        kernel,
        grid_spec=pltpu.PrefetchScalarGridSpec(
            num_scalar_prefetch=1,
            grid=(2,),
            in_specs=in_specs,
            out_specs=[pl.BlockSpec(s.shape, one) for s in shapes],
        ),
        out_shape=shapes,
        compiler_params=pltpu.CompilerParams(vmem_limit_bytes=40 * 2**20),
        cost_estimate=pl.CostEstimate(
            flops=2 * 2 * part * 2 * depth * 2 * half,
            bytes_accessed=6 * depth * part + 5 * depth * half + 14 * part * half,
            transcendentals=0,
        ),
    )(place, *left, far_left, near, *own, *mate, *extra)


def final_kernel(place, kept, first, second, s_left, t_own, t_mate, *rest):
    out = rest[-1]
    t = jnp.where(pl.program_id(0) == 0, t_own[...], t_mate[...])
    shards_all = SIDE * SIDE
    between = jnp.dot(
        s_left[:, :shards_all],
        t[:shards_all],
        preferred_element_type=f32,
        precision=lax.Precision.HIGHEST,
    )
    inside = kept[...] + first[...].astype(f32) + second[...].astype(f32)
    row_scale = s_left[:, shards_all : shards_all + 1]
    out[...] = inside * row_scale * t[shards_all : shards_all + 1] + between


def final(place, k, kept, first, second, s_left, t_own, t_mate, whole=None):
    part, columns = kept.shape
    half = columns // 2
    block = pl.BlockSpec((part, half), lambda i, place: (0, i))
    in_specs = (
        [block] * 3
        + [pl.BlockSpec(s_left.shape, lambda i, place: (0, 0))]
        + [pl.BlockSpec((t_own.shape[0], half), lambda i, place: (0, k))] * 2
    )
    more, aliases = (), {}
    if whole is not None:
        in_specs = in_specs + [pl.BlockSpec(memory_space=pl.ANY)]
        more, aliases = (whole,), {7: 0}
    return pl.pallas_call(
        final_kernel,
        grid_spec=pltpu.PrefetchScalarGridSpec(
            num_scalar_prefetch=1,
            grid=(2,),
            in_specs=in_specs,
            out_specs=pl.BlockSpec(
                (part, half), lambda i, place: (0, lax.rem(place[1] + i, 2) * 2 + k)
            ),
        ),
        out_shape=jax.ShapeDtypeStruct((part, 2 * columns), f32),
        input_output_aliases=aliases,
        compiler_params=pltpu.CompilerParams(vmem_limit_bytes=16 * 2**20),
        cost_estimate=pl.CostEstimate(
            flops=6 * part * columns, bytes_accessed=12 * part * columns, transcendentals=0
        ),
    )(place, kept, first, second, s_left, t_own, t_mate, *more)


def per_device(student, teacher, starts, weights, counts):
    y, x, z, c = (lax.axis_index(n) for n in ("y", "x", "row", "col"))
    shard = y * SIDE + x
    rows = starts.shape[0]
    columns = teacher.shape[1]
    half = columns // 2
    width = student.shape[1] // SIDE
    part = width // SIDE

    up = [(i, (i + 1) % 16) for i in range(16)]
    down = [(j, i) for i, j in up]
    before = lax.ppermute(teacher[rows - HALO :], ("y", "x"), up)
    behind = lax.ppermute(teacher[:HALO], ("y", "x"), down)

    own_count = lax.dynamic_slice_in_dim(counts[0], z, 1)
    *packed, block = pack(jnp.stack([y, x, own_count[0]]).astype(jnp.int32), student)
    packed, block, before, behind = lax.optimization_barrier((packed, block, before, behind))
    got = [packed[0], ring(packed[1], "x", 1), ring(packed[2], "x", -1), ring(packed[3], "x", 2)]
    blocks = ring_all(block, "row")
    meta = jnp.concatenate([(starts - shard * rows)[:, None], weights], axis=1)
    standard, stats = pool(counts[0], before, teacher, behind, meta)
    z_counts = jnp.concatenate(
        [lax.dynamic_slice_in_dim(counts[0], lax.rem(z + k, SIDE), 1) for k in COMING]
    )
    own_stats = shards(z_counts, stats, blocks)
    got, own_stats, standard = lax.optimization_barrier((got, own_stats, standard))
    near_stats = ring_all(own_stats, "x")
    turned, mean = turn(own_count, got)
    near_stats, turned, standard = lax.optimization_barrier((near_stats, turned, standard))

    right, left = ring(standard, "x", 1), ring(standard, "x", -1)
    up, down = ring(turned, "row", 1), ring(turned, "row", -1)
    t_standard = swap(standard)
    t_rows, s_left = settle(ring_all(gather_stats(near_stats), "y"))
    t_mate = swap(t_rows)
    right, left, up, down, t_standard, t_rows, t_mate, s_left = lax.optimization_barrier(
        (right, left, up, down, t_standard, t_rows, t_mate, s_left)
    )

    x_far = [ring(right[:, :half], "x", 1), ring(left[:, half:], "x", -1)]
    z_far = [ring(up[: width // 2], "row", 1), ring(down[width // 2 :], "row", -1)]
    t_right, t_left = swap(right), swap(left)
    place = jnp.stack([z, c]).astype(jnp.int32)
    own, mate = [standard, right, left], [t_standard, t_right, t_left]
    near_z = [turned, up, down]
    own_sum = first_product(place, near_z, own, mean)
    mate_sum = first_product(place, near_z, mate, mean)
    x_far, z_far, own_sum, mate_sum = lax.optimization_barrier((x_far, z_far, own_sum, mate_sum))

    t_x_far = [swap(f) for f in x_far]
    opened = []
    for k in range(2):
        sides = (own + [x_far[k], own_sum], mate + [t_x_far[k], mate_sum])
        opened.append((last_product(place, k, near_z, z_far[0], mean, *sides), sides))
    arrived = [(ring(o[0], "y", 1), ring(o[1], "y", -1)) for o, _ in opened]
    out = None
    for k in range(2):
        (_, _, kept), sides = opened[k]
        v = last_product(place, k, near_z, z_far[1], mean, *sides, arrived[k])
        out = final(
            place, k, kept, ring(v[0], "y", 1), ring(v[1], "y", -1), s_left, t_rows, t_mate, out
        )
    return out[None, None]


def solution(mesh):
    fine = Mesh(mesh.devices.reshape(SIDE, SIDE, SIDE, 2), ("y", "x", "row", "col"))
    seq = ("y", "x")
    placed = (
        P(seq + ("row",), "col"),
        P(seq, ("row", "col")),
        P(seq),
        P(seq, None),
        P(seq, None),
    )
    return jax.shard_map(
        per_device,
        mesh=fine,
        in_specs=placed,
        out_specs=P("col", seq, None, "row"),
        check_vma=False,
    )
```

```python
import jax
import jax.numpy as jnp
from jax import lax
from jax.experimental import pallas as pl
from jax.experimental.pallas import tpu as pltpu
from jax.sharding import Mesh
from jax.sharding import PartitionSpec as P

SUB = 192
BAND = 4
HALO = 16
SIDE = 4
COMING = (0, SIDE - 1, 1, 2)
epsilon = 1e-05
f32 = jnp.float32
bf16 = jnp.bfloat16


def ring(value, axis, step):
    return lax.ppermute(value, axis, [(i, (i + step) % SIDE) for i in range(SIDE)])


def ring_all(value, axis):
    return [value, ring(value, axis, 1), ring(value, axis, -1), ring(value, axis, 2)]


def swap(value):
    return lax.ppermute(value, "col", [(0, 1), (1, 0)])


def after(value, *others):
    return lax.optimization_barrier((value, others))[0]


def smem():
    return pl.BlockSpec(memory_space=pltpu.SMEM)


def vmem():
    return pl.BlockSpec(memory_space=pltpu.VMEM)


def pack_kernel(place, counts, student, *outs):
    y, x, count = place[2], place[3], counts[0, place[0]]
    moments = outs[SIDE]
    part = outs[0].shape[1] // SIDE
    for r, x_step in enumerate((0, 1, SIDE - 1, 2)):
        at = lax.rem(x + x_step, SIDE)
        for i, y_step in enumerate((2, 0, 1, SIDE - 1)):
            slot = lax.rem(y + y_step, SIDE) * SIDE + at
            first = pl.multiple_of(slot * part, 128)
            columns = slice(i * part, (i + 1) * part)
            block = student[:, pl.ds(first, part)]
            outs[r][:, columns] = block
            value = block.astype(f32)
            live = lax.broadcasted_iota(jnp.int32, value.shape, 0) < count
            total = jnp.sum(jnp.where(live, value, 0.0), axis=0, keepdims=True)
            dev = jnp.where(live, value - total / count.astype(f32), 0.0)
            moments[r : r + 1, columns] = total
            moments[SIDE + r : SIDE + r + 1, columns] = jnp.sum(dev * dev, axis=0, keepdims=True)


def pack(place, counts, student):
    width = student.shape[1] // SIDE
    return pl.pallas_call(
        pack_kernel,
        in_specs=[smem(), smem(), vmem()],
        out_specs=[vmem()] * (SIDE + 1),
        out_shape=[jax.ShapeDtypeStruct((SUB, width), bf16)] * SIDE
        + [jax.ShapeDtypeStruct((2 * SIDE, width), f32)],
        compiler_params=pltpu.CompilerParams(vmem_limit_bytes=24 * 2**20),
        cost_estimate=pl.CostEstimate(
            flops=8 * SUB * student.shape[1],
            bytes_accessed=4 * SUB * student.shape[1],
            transcendentals=0,
        ),
    )(place, counts, student)


def turn_kernel(place, counts, p0, p1, p2, p3, turned, near):
    count = counts[0, place[0]]
    rows = jnp.concatenate([p[...] for p in (p0, p1, p2, p3)], axis=0)
    flat = rows.T
    turned[...] = flat
    mine = flat[:, :SUB].astype(f32)
    live = lax.broadcasted_iota(jnp.int32, mine.shape, 1) < count
    total = jnp.sum(jnp.where(live, mine, 0.0), axis=1, keepdims=True)
    near[...] = total / count.astype(f32)


def turn(place, counts, pieces):
    width = pieces[0].shape[1]
    return pl.pallas_call(
        turn_kernel,
        in_specs=[smem()] * 2 + [vmem()] * SIDE,
        out_specs=[vmem()] * 2,
        out_shape=[
            jax.ShapeDtypeStruct((width, SIDE * SUB), bf16),
            jax.ShapeDtypeStruct((width, 1), f32),
        ],
        compiler_params=pltpu.CompilerParams(vmem_limit_bytes=16 * 2**20),
        cost_estimate=pl.CostEstimate(
            flops=0, bytes_accessed=4 * SUB * SIDE * width, transcendentals=0
        ),
    )(place, counts, *pieces)


def shards_kernel(place, counts, teacher, *refs):
    blocks, out = refs[:SIDE], refs[-1]
    out[:SIDE, :] = teacher[...]
    size = [counts[0, lax.rem(place[0] + k, SIDE)].astype(f32) for k in COMING]
    totals = [b[:SIDE, :] for b in blocks]
    total = totals[0] + totals[1] + totals[2] + totals[3]
    mean = total / (size[0] + size[1] + size[2] + size[3])
    square = jnp.zeros_like(total)
    for q in range(SIDE):
        off = totals[q] / size[q] - mean
        square = square + blocks[q][SIDE:, :] + size[q] * off * off
    out[SIDE : 2 * SIDE, :] = total
    out[2 * SIDE :, :] = square


def shards(place, counts, teacher, blocks):
    columns = blocks[0].shape[1]
    return pl.pallas_call(
        shards_kernel,
        in_specs=[smem()] * 2 + [vmem()] * (1 + SIDE),
        out_specs=vmem(),
        out_shape=jax.ShapeDtypeStruct((3 * SIDE, columns), f32),
        compiler_params=pltpu.CompilerParams(vmem_limit_bytes=8 * 2**20),
    )(place, counts, teacher, *blocks)


def spread_kernel(e0, e1, e2, e3, *outs):
    part = e0.shape[1] // SIDE
    for r, out in enumerate(outs):
        for i, (e, slot) in enumerate(zip((e0, e1, e2, e3), (1, 2, 3, 0))):
            for m in range(3):
                out[m * SIDE + i : m * SIDE + i + 1, :] = e[m : m + 1, :]
            for m in range(2):
                row = (1 + m) * SIDE + r
                out[12 + m : 13 + m, i * part : (i + 1) * part] = e[
                    row : row + 1, slot * part : (slot + 1) * part
                ]
        out[14:16, :] = jnp.zeros((2, out.shape[1]), f32)


def spread(every):
    columns = every[0].shape[1]
    return pl.pallas_call(
        spread_kernel,
        in_specs=[vmem()] * SIDE,
        out_specs=[vmem()] * SIDE,
        out_shape=[jax.ShapeDtypeStruct((16, columns), f32)] * SIDE,
        compiler_params=pltpu.CompilerParams(vmem_limit_bytes=8 * 2**20),
    )(*every)


def settle_kernel(n0, n1, n2, n3, t_rows, s_left, work):
    every = (n0, n1, n2, n3)
    part = work.shape[1]

    def combine(totals, squares, counts):
        tokens = sum(jnp.sum(n, axis=0, keepdims=True) for n in counts)
        mean = sum(jnp.sum(t, axis=0, keepdims=True) for t in totals) / tokens
        offs = [t / n - mean for t, n in zip(totals, counts)]
        square = sum(
            jnp.sum(q + n * o * o, axis=0, keepdims=True)
            for q, n, o in zip(squares, counts, offs)
        )
        return offs, lax.rsqrt(square / tokens + epsilon), tokens

    offs, scale, _ = combine(
        [n[0:4, :] for n in every], [n[4:8, :] for n in every], [n[8:12, :] for n in every]
    )
    for j in range(SIDE):
        t_rows[j * SIDE : (j + 1) * SIDE, :] = offs[j] * scale
    t_rows[SIDE * SIDE : SIDE * SIDE + 1, :] = scale
    spots = [(n, i, slice(i * part, (i + 1) * part)) for n in every for i in range(SIDE)]
    counts = [n[8 + i : 9 + i, 0:part] for n, i, _ in spots]
    offs, scale, tokens = combine(
        [n[12:13, c] for n, _, c in spots], [n[13:14, c] for n, _, c in spots], counts
    )
    scale = scale / jnp.sqrt(tokens)
    work[...] = jnp.zeros_like(work)
    for j in range(SIDE * SIDE):
        work[j : j + 1, :] = offs[j] * scale * counts[j]
    work[SIDE * SIDE : SIDE * SIDE + 1, :] = scale
    s_left[...] = work[...].T


def settle(every):
    columns = every[0].shape[1]
    part = columns // SIDE
    return pl.pallas_call(
        settle_kernel,
        in_specs=[vmem()] * SIDE,
        out_specs=[vmem()] * 2,
        out_shape=[
            jax.ShapeDtypeStruct((SIDE * SIDE + 1, columns), f32),
            jax.ShapeDtypeStruct((part, 128), f32),
        ],
        scratch_shapes=[pltpu.VMEM((128, part), f32)],
        compiler_params=pltpu.CompilerParams(vmem_limit_bytes=8 * 2**20),
        cost_estimate=pl.CostEstimate(
            flops=10**11, bytes_accessed=2 * 10**8, transcendentals=0
        ),
    )(*every)


def pool_kernel(place, counts, before, teacher, behind, starts, weights, full, stats, mix, share, pooled, lines, meta):
    window = SUB + 2 * HALO
    length = teacher.shape[0]
    j = pl.program_id(0)

    @pl.when(j == 0)
    def _():
        lines[...] = jnp.zeros_like(lines)
        lines[0:1, :] = (starts[...] - (place[2] * SIDE + place[3]) * length).astype(f32)
        lines[1 : 1 + BAND, :] = weights[...].astype(f32)
        meta[...] = lines[...].T.astype(jnp.int32)
        for r in range(SIDE):
            rows = slice(r * SUB, (r + 1) * SUB)
            spot = lax.broadcasted_iota(jnp.int32, (SUB, window), 1)
            local = meta[rows, 0:1] - (r * SUB - HALO)
            found = jnp.zeros((SUB, window), jnp.int32)
            whole = jnp.zeros((SUB, 1), jnp.int32)
            for k in range(BAND):
                weight = meta[rows, 1 + k : 2 + k]
                found = found + jnp.where(spot == local + k, weight, 0)
                whole = whole + weight
            mix[rows, :] = found.astype(f32).astype(bf16)
            share[rows, :] = jnp.broadcast_to(whole.astype(f32), (SUB, 128))

    total = jnp.zeros((1, teacher.shape[1]), f32)
    alive = jnp.int32(0)
    for r in range(SIDE):
        rows = slice(r * SUB, (r + 1) * SUB)
        low, high = r * SUB - HALO, (r + 1) * SUB + HALO
        parts = [teacher[max(low, 0) : min(high, length), :]]
        if low < 0:
            parts = [before[...]] + parts
        if high > length:
            parts = parts + [behind[...]]
        seen = jnp.concatenate(parts, axis=0) if len(parts) > 1 else parts[0]
        value = jnp.dot(mix[rows, :], seen, preferred_element_type=f32)
        value = value / share[rows, 0:1]
        pooled[rows, :] = value
        live = lax.broadcasted_iota(jnp.int32, value.shape, 0) < counts[0, r]
        total = total + jnp.sum(jnp.where(live, value, 0.0), axis=0, keepdims=True)
        alive = alive + counts[0, r]
    mean = total / alive.astype(f32)
    square = jnp.zeros_like(total)
    for r in range(SIDE):
        rows = slice(r * SUB, (r + 1) * SUB)
        value = pooled[rows, :]
        live = lax.broadcasted_iota(jnp.int32, value.shape, 0) < counts[0, r]
        dev = jnp.where(live, value - mean, 0.0)
        small = dev.astype(bf16)
        full[rows, :] = small
        square = square + jnp.sum(dev * dev, axis=0, keepdims=True)
    stats[0:1, :] = total
    stats[1:2, :] = square
    stats[2:3, :] = jnp.broadcast_to(alive.astype(f32), total.shape)
    lane = lax.broadcasted_iota(jnp.int32, total.shape, 1)
    row = jnp.zeros(total.shape, jnp.int32)
    for r in range(SIDE):
        row = row + jnp.where(lane == r, counts[0, r], 0)
    stats[3:4, :] = row.astype(f32)


def pool(place, counts, before, teacher, behind, starts, weights):
    rows, columns = teacher.shape
    tile = 256
    return pl.pallas_call(
        pool_kernel,
        grid=(columns // tile,),
        in_specs=[
            smem(),
            smem(),
            pl.BlockSpec((HALO, tile), lambda j: (0, j)),
            pl.BlockSpec((rows, tile), lambda j: (0, j)),
            pl.BlockSpec((HALO, tile), lambda j: (0, j)),
            pl.BlockSpec(starts.shape, lambda j: (0, 0)),
            pl.BlockSpec(weights.shape, lambda j: (0, 0)),
        ],
        out_specs=[
            pl.BlockSpec((rows, tile), lambda j: (0, j)),
            pl.BlockSpec((4, tile), lambda j: (0, j)),
        ],
        out_shape=[
            jax.ShapeDtypeStruct((rows, columns), bf16),
            jax.ShapeDtypeStruct((4, columns), f32),
        ],
        scratch_shapes=[
            pltpu.VMEM((rows, SUB + 2 * HALO), bf16),
            pltpu.VMEM((rows, 128), f32),
            pltpu.VMEM((rows, tile), f32),
            pltpu.VMEM((128, rows), f32),
            pltpu.VMEM((rows, 128), jnp.int32),
        ],
        compiler_params=pltpu.CompilerParams(vmem_limit_bytes=32 * 2**20),
        cost_estimate=pl.CostEstimate(
            flops=2 * rows * 256 * columns, bytes_accessed=6 * rows * columns, transcendentals=0
        ),
    )(place, counts, before, teacher, behind, starts, weights)


def with_ones(a):
    return jnp.concatenate([a, jnp.ones((16, a.shape[1]), bf16)], axis=0)


def less_mean(total, near):
    part = total.shape[0] - 16
    return total[:part] - near * total[part : part + 1]


def first_kernel(place, a0, a1, a2, b0, b1, b2, near, out):
    z = place[0]
    depth = a0.shape[1]
    fill = jnp.zeros((depth - 3 * SUB, b0.shape[1]), bf16)
    total = None
    for a, step in zip((a0, a1, a2), COMING):
        rows = pl.ds(pl.multiple_of(lax.rem(z + step, SIDE) * SUB, 16), SUB)
        b = jnp.concatenate([b0[rows, :], b1[rows, :], b2[rows, :], fill], axis=0)
        term = jnp.dot(with_ones(a[...]), b, preferred_element_type=f32)
        total = term if total is None else total + term
    out[...] = less_mean(total, near[...])


def first_product(place, left, right, near):
    rows, depth = left[0].shape
    part = rows // SIDE
    length, columns = right[0].shape
    near_depth = 640
    return pl.pallas_call(
        first_kernel,
        grid_spec=pltpu.PrefetchScalarGridSpec(
            num_scalar_prefetch=1,
            grid=(SIDE,),
            in_specs=[pl.BlockSpec((part, near_depth), lambda i, place: (i, 0))] * 3
            + [pl.BlockSpec((length, columns), lambda i, place: (0, 0))] * 3
            + [pl.BlockSpec((part, 1), lambda i, place: (i, 0))],
            out_specs=pl.BlockSpec((part, columns), lambda i, place: (i, 0)),
        ),
        out_shape=jax.ShapeDtypeStruct((rows, columns), f32),
        compiler_params=pltpu.CompilerParams(vmem_limit_bytes=60 * 2**20),
        cost_estimate=pl.CostEstimate(
            flops=2 * rows * 3 * near_depth * columns,
            bytes_accessed=6 * rows * depth + 6 * length * columns + 4 * rows * columns,
            transcendentals=0,
        ),
    )(place, *left, *right, near)


def last_sums(place, refs):
    z = place[0]
    tails, far_a, near = refs[:3], refs[3], refs[4]
    sides = (refs[5:10], refs[10:15])
    results = []
    lefts = [with_ones(t[...]) for t in tails]
    far_left = with_ones(far_a[...])
    for b0, b1, b2, far_b, done in sides:
        fill = jnp.zeros((tails[0].shape[1] - SUB, far_b.shape[1]), bf16)
        total = None
        for a, step in zip(lefts, COMING):
            rows = pl.ds(pl.multiple_of(lax.rem(z + step, SIDE) * SUB, 16), SUB)
            b = jnp.concatenate([fill, far_b[rows, :]], axis=0)
            term = jnp.dot(a, b, preferred_element_type=f32)
            total = term if total is None else total + term
        rows = pl.ds(pl.multiple_of(lax.rem(z + 2, SIDE) * SUB, 16), SUB)
        b = jnp.concatenate([b0[...], b1[...], b2[...], far_b[rows, :]], axis=0)
        total = total + jnp.dot(far_left, b, preferred_element_type=f32)
        results.append(less_mean(total, near[...]) + done[...])
    return results


def far_kernel(place, *refs):
    up, down = refs[15:]
    results = last_sums(place, refs)
    up[...] = results[0].astype(bf16)
    down[...] = results[1].astype(bf16)


def own_kernel(place, *refs):
    kept = refs[15]
    half = kept.shape[1] // 2
    results = last_sums(place, refs)
    kept[:, :half] = results[0]
    kept[:, half:] = results[1]


def close_kernel(place, *refs):
    from_back, from_next, up, down = refs[15:]
    i = pl.program_id(0)
    half = from_back.shape[1]
    results = last_sums(place, refs)

    @pl.when(i == 0)
    def _():
        up[:, :half] = (results[0] + from_back[...].astype(f32)).astype(bf16)
        up[:, half:] = results[1].astype(bf16)

    @pl.when(i == 1)
    def _():
        down[:, :half] = results[0].astype(bf16)
        down[:, half:] = (results[1] + from_next[...].astype(f32)).astype(bf16)


def last_product(place, k, kind, left, far_left, near, own, mate, arrived=()):
    depth = left[0].shape[1]
    part = left[0].shape[0] // SIDE
    half = own[0].shape[1] // 2
    kernel, start, far_start, steps = {
        "far": (far_kernel, 0, 0, 1),
        "own": (own_kernel, 1, 1, 1),
        "close": (close_kernel, 2, 0, 2),
    }[kind]
    one = lambda i, place: (0, 0)
    tail = 256
    side = (
        [pl.BlockSpec((SUB, half), lambda i, place: (lax.rem(place[0] + 2, SIDE), k))] * 3
        + [pl.BlockSpec((own[3].shape[0], half), one)]
        + [pl.BlockSpec((part, half), lambda i, place: (start + i, k))]
    )
    in_specs = (
        [pl.BlockSpec((part, tail), lambda i, place: (start + i, depth // tail - 1))] * 3
        + [pl.BlockSpec((part, depth), lambda i, place: (far_start + i, 0))]
        + [pl.BlockSpec((part, 1), lambda i, place: (start + i, 0))]
        + side * 2
        + [pl.BlockSpec((part, half), one)] * len(arrived)
    )
    S = jax.ShapeDtypeStruct
    shapes = {
        "far": [S((part, half), bf16)] * 2,
        "own": [S((part, 2 * half), f32)],
        "close": [S((part, 2 * half), bf16)] * 2,
    }[kind]
    return pl.pallas_call(
        kernel,
        grid_spec=pltpu.PrefetchScalarGridSpec(
            num_scalar_prefetch=1,
            grid=(steps,),
            in_specs=in_specs,
            out_specs=[pl.BlockSpec(s.shape, one) for s in shapes],
        ),
        out_shape=shapes,
        compiler_params=pltpu.CompilerParams(vmem_limit_bytes=60 * 2**20),
        cost_estimate=pl.CostEstimate(
            flops=2 * steps * part * 2 * depth * 2 * half,
            bytes_accessed=3 * steps * depth * part + 5 * depth * half + 8 * part * half,
            transcendentals=0,
        ),
    )(place, *left, far_left, near, *own, *mate, *arrived)


def final_kernel(place, kept, first, second, s_left, t_own, t_mate, *rest):
    out = rest[-1]
    t = jnp.where(pl.program_id(0) == 0, t_own[...], t_mate[...])
    shards_all = SIDE * SIDE
    between = jnp.dot(
        s_left[:, :shards_all],
        t[:shards_all],
        preferred_element_type=f32,
        precision=lax.Precision.HIGHEST,
    )
    inside = kept[...] + first[...].astype(f32) + second[...].astype(f32)
    row_scale = s_left[:, shards_all : shards_all + 1]
    out[...] = inside * row_scale * t[shards_all : shards_all + 1] + between


def final(place, k, kept, first, second, s_left, t_own, t_mate, whole=None):
    part, columns = kept.shape
    half = columns // 2
    block = pl.BlockSpec((part, half), lambda i, place: (0, i))
    in_specs = (
        [block] * 3
        + [pl.BlockSpec(s_left.shape, lambda i, place: (0, 0))]
        + [pl.BlockSpec((t_own.shape[0], half), lambda i, place: (0, k))] * 2
    )
    more, aliases = (), {}
    if whole is not None:
        in_specs = in_specs + [pl.BlockSpec(memory_space=pl.ANY)]
        more, aliases = (whole,), {7: 0}
    return pl.pallas_call(
        final_kernel,
        grid_spec=pltpu.PrefetchScalarGridSpec(
            num_scalar_prefetch=1,
            grid=(2,),
            in_specs=in_specs,
            out_specs=pl.BlockSpec(
                (part, half), lambda i, place: (0, lax.rem(place[1] + i, 2) * 2 + k)
            ),
        ),
        out_shape=jax.ShapeDtypeStruct((part, 2 * columns), f32),
        input_output_aliases=aliases,
        compiler_params=pltpu.CompilerParams(vmem_limit_bytes=16 * 2**20),
        cost_estimate=pl.CostEstimate(
            flops=6 * part * columns, bytes_accessed=12 * part * columns, transcendentals=0
        ),
    )(place, kept, first, second, s_left, t_own, t_mate, *more)


def per_device(student, teacher, starts, weights, counts):
    y, x, z, c = (lax.axis_index(n) for n in ("y", "x", "row", "col"))
    place = jnp.stack([z, c, y, x]).astype(jnp.int32)
    rows = starts.shape[0]
    columns = teacher.shape[1]
    half = columns // 2
    width = student.shape[1] // SIDE

    up = [(i, (i + 1) % 16) for i in range(16)]
    down = [(j, i) for i, j in up]
    before = lax.ppermute(teacher[rows - HALO :], ("y", "x"), up)
    behind = lax.ppermute(teacher[:HALO], ("y", "x"), down)

    *packed, block = pack(place, counts, student)
    packed, block, before, behind = lax.optimization_barrier((packed, block, before, behind))
    got = [packed[0], ring(packed[1], "x", 1), ring(packed[2], "x", -1), ring(packed[3], "x", 2)]
    blocks = ring_all(block, "row")
    standard, stats = pool(place, counts, before, teacher, behind, starts[None], weights.T)
    every = ring_all(shards(place, counts, stats, blocks), "y")
    got, every, standard = lax.optimization_barrier((got, every, standard))
    to = spread(every)
    near = [to[0], ring(to[1], "x", 1), ring(to[2], "x", -1), ring(to[3], "x", 2)]
    turned, mean = turn(place, counts, got)

    right, left = ring(standard, "x", 1), ring(standard, "x", -1)
    up, down = ring(turned, "row", 1), ring(turned, "row", -1)
    t_standard = swap(standard)
    t_rows, s_left = settle(near)
    t_mate = swap(t_rows)
    right, left, up, down, t_standard, t_rows, t_mate, s_left = lax.optimization_barrier(
        (right, left, up, down, t_standard, t_rows, t_mate, s_left)
    )

    x_far = [ring(right[:, :half], "x", 1), ring(left[:, half:], "x", -1)]
    z_far = [ring(up[: width // 2], "row", 1), ring(down[width // 2 :], "row", -1)]
    t_right, t_left = swap(right), swap(left)
    own, mate = [standard, right, left], [t_standard, t_right, t_left]
    near_z = [turned, up, down]
    own_sum = first_product(place, near_z, own, mean)
    mate_sum = first_product(place, near_z, mate, mean)
    x_far, z_far, own_sum, mate_sum = lax.optimization_barrier((x_far, z_far, own_sum, mate_sum))

    t_x_far = [swap(f) for f in x_far]
    sides = [
        (own + [x_far[k], own_sum], mate + [t_x_far[k], mate_sum]) for k in range(2)
    ]
    arrived = []
    for k in range(2):
        o = last_product(place, k, "far", near_z, z_far[0], mean, *sides[k])
        arrived.append((ring(o[0], "y", 1), ring(o[1], "y", -1)))
    passed = []
    for k in range(2):
        v = last_product(place, k, "close", near_z, z_far[1], mean, *sides[k], arrived[k])
        passed.append((ring(v[0], "y", 1), ring(v[1], "y", -1)))
    out = None
    for k in range(2):
        kept = last_product(place, k, "own", near_z, z_far[0], mean, *sides[k])[0]
        out = final(place, k, kept, *passed[k], s_left, t_rows, t_mate, out)
    return out[None, None]


def solution(mesh):
    fine = Mesh(mesh.devices.reshape(SIDE, SIDE, SIDE, 2), ("y", "x", "row", "col"))
    seq = ("y", "x")
    placed = (
        P(seq + ("row",), "col"),
        P(seq, ("row", "col")),
        P(seq),
        P(seq, None),
        P(seq, None),
    )
    return jax.shard_map(
        per_device,
        mesh=fine,
        in_specs=placed,
        out_specs=P("col", seq, None, "row"),
        check_vma=False,
    )
```

```python
import jax
import jax.numpy as jnp
from jax import lax
from jax.experimental import pallas as pl
from jax.experimental.pallas import tpu as pltpu
from jax.sharding import Mesh
from jax.sharding import PartitionSpec as P

SUB = 192
BAND = 4
HALO = 16
EXTRA = 16
SIDE = 4
COMING = (0, SIDE - 1, 1, 2)
epsilon = 1e-05
f32 = jnp.float32
bf16 = jnp.bfloat16


def ring(value, axis, step):
    return lax.ppermute(value, axis, [(i, (i + step) % SIDE) for i in range(SIDE)])


def ring_all(value, axis):
    return [value, ring(value, axis, 1), ring(value, axis, -1), ring(value, axis, 2)]


def swap(value):
    return lax.ppermute(value, "col", [(0, 1), (1, 0)])


def after(value, *others):
    return lax.optimization_barrier((value, others))[0]


def in_parts(value):
    high = value.astype(bf16)
    rest = value - high.astype(f32)
    middle = rest.astype(bf16)
    low = (rest - middle.astype(f32)).astype(bf16)
    return high, middle, low


def from_parts(rows):
    rows = rows.astype(f32)
    return rows[0:1] + rows[1:2] + rows[2:3]


def smem():
    return pl.BlockSpec(memory_space=pltpu.SMEM)


def vmem():
    return pl.BlockSpec(memory_space=pltpu.VMEM)


def pack_kernel(place, counts, student, *outs):
    y, x, count = place[2], place[3], counts[0, place[0]]
    part = outs[0].shape[1] // SIDE
    for r, x_step in enumerate((0, 1, SIDE - 1, 2)):
        at = lax.rem(x + x_step, SIDE)
        for i, y_step in enumerate((2, 0, 1, SIDE - 1)):
            slot = lax.rem(y + y_step, SIDE) * SIDE + at
            first = pl.multiple_of(slot * part, 128)
            columns = slice(i * part, (i + 1) * part)
            block = student[:, pl.ds(first, part)]
            outs[r][:SUB, columns] = block
            value = block.astype(f32)
            live = lax.broadcasted_iota(jnp.int32, value.shape, 0) < count
            total = jnp.sum(jnp.where(live, value, 0.0), axis=0, keepdims=True)
            dev = jnp.where(live, value - total / count.astype(f32), 0.0)
            square = jnp.sum(dev * dev, axis=0, keepdims=True)
            rows = in_parts(total) + in_parts(square)
            rows = rows + (jnp.zeros((EXTRA - len(rows), part), bf16),)
            outs[r][SUB:, columns] = jnp.concatenate(rows, axis=0)


def pack(place, counts, student):
    width = student.shape[1] // SIDE
    return pl.pallas_call(
        pack_kernel,
        in_specs=[smem(), smem(), vmem()],
        out_specs=[vmem()] * SIDE,
        out_shape=[jax.ShapeDtypeStruct((SUB + EXTRA, width), bf16)] * SIDE,
        compiler_params=pltpu.CompilerParams(vmem_limit_bytes=24 * 2**20),
        cost_estimate=pl.CostEstimate(
            flops=8 * SUB * student.shape[1],
            bytes_accessed=4 * SUB * student.shape[1],
            transcendentals=0,
        ),
    )(place, counts, student)


def turn_kernel(place, counts, p0, p1, p2, p3, turned, near):
    count = counts[0, place[0]]
    pieces = (p0, p1, p2, p3)
    rows = jnp.concatenate([p[:SUB, :] for p in pieces], axis=0)
    flat = rows.T
    width, depth = flat.shape
    turned[:width, :] = flat
    moments = jnp.concatenate([p[SUB : SUB + 6, :].astype(f32) for p in pieces], axis=0)
    rests = [
        jnp.concatenate([moments[3 * m + i : 3 * m + i + 1, depth:] for i in range(3)], axis=1)
        for m in range(8)
    ]
    turned[width:, :] = jnp.concatenate([moments[:, :depth]] + rests, axis=0).astype(bf16)
    mine = flat[:, :SUB].astype(f32)
    live = lax.broadcasted_iota(jnp.int32, mine.shape, 1) < count
    total = jnp.sum(jnp.where(live, mine, 0.0), axis=1, keepdims=True)
    near[...] = total / count.astype(f32)


def turn(place, counts, pieces):
    width = pieces[0].shape[1]
    return pl.pallas_call(
        turn_kernel,
        in_specs=[smem()] * 2 + [vmem()] * SIDE,
        out_specs=[vmem()] * 2,
        out_shape=[
            jax.ShapeDtypeStruct((width + 2 * EXTRA, SIDE * SUB), bf16),
            jax.ShapeDtypeStruct((width, 1), f32),
        ],
        compiler_params=pltpu.CompilerParams(vmem_limit_bytes=16 * 2**20),
        cost_estimate=pl.CostEstimate(
            flops=0, bytes_accessed=4 * SUB * SIDE * width, transcendentals=0
        ),
    )(place, counts, *pieces)


def shards_kernel(place, *refs):
    zs, own, mate, out = refs[:SIDE], refs[SIDE : SIDE + 5], refs[SIDE + 5 : SIDE + 10], refs[-1]
    half = own[3].shape[1]
    depth = zs[0].shape[1]
    blocks = []
    for ref in zs:
        rows = ref[...].astype(f32)
        rests = [
            rows[24 + m : 25 + m, i * (depth // 3) : (i + 1) * (depth // 3)]
            for m in range(8)
            for i in range(3)
        ]
        rests = jnp.concatenate(rests, axis=0)
        blocks.append(jnp.concatenate([rows[:24], rests], axis=1))
    lane = lax.broadcasted_iota(jnp.int32, (1, half), 1)
    for r in range(SIDE):
        for s, side in enumerate((own, mate)):
            if r < 3:
                rows = side[r][...]
            else:
                rows = jnp.concatenate([side[3][...], side[4][...]], axis=1)
            out[8 * s + r : 8 * s + r + 1, :] = from_parts(rows[0:3])
            out[8 * s + SIDE + r : 8 * s + SIDE + r + 1, :] = from_parts(rows[3:6])
        sizes = own[r][...][6:7, :half].astype(f32)
        n = jnp.sum(jnp.where(lane < SIDE, sizes, 0.0), axis=1, keepdims=True)
        out[16 + r : 17 + r, :] = jnp.broadcast_to(n, (1, out.shape[1]))
        totals = [from_parts(b[6 * r : 6 * r + 3]) for b in blocks]
        squares = [from_parts(b[6 * r + 3 : 6 * r + 6]) for b in blocks]
        total = totals[0] + totals[1] + totals[2] + totals[3]
        mean = total / n
        square = jnp.zeros_like(total)
        for q, step in enumerate(COMING):
            here = lax.rem(place[0] + step, SIDE)
            size = jnp.sum(jnp.where(lane == here, sizes, 0.0), axis=1, keepdims=True)
            off = totals[q] / size - mean
            square = square + squares[q] + size * off * off
        out[20 + r : 21 + r, :] = total
        out[24 + r : 25 + r, :] = square
    out[28:32, :] = jnp.zeros((4, out.shape[1]), f32)


def shards(place, left, far_left, own, mate):
    depth = left[0].shape[1]
    columns = own[0].shape[1]

    def low(value, rows):
        first = value.shape[0] // rows - 1
        return pl.BlockSpec((rows, value.shape[1]), lambda i, place: (first, 0))

    return pl.pallas_call(
        shards_kernel,
        grid_spec=pltpu.PrefetchScalarGridSpec(
            num_scalar_prefetch=1,
            grid=(1,),
            in_specs=[low(v, 2 * EXTRA) for v in left + [far_left]]
            + [low(v, EXTRA) for v in own + mate],
            out_specs=pl.BlockSpec((32, columns), lambda i, place: (0, 0)),
        ),
        out_shape=jax.ShapeDtypeStruct((32, columns), f32),
        compiler_params=pltpu.CompilerParams(vmem_limit_bytes=8 * 2**20),
    )(place, *left, far_left, *own, *mate)


def settle_kernel(e0, e1, e2, e3, t_own, t_mate, s_left, work):
    every = (e0, e1, e2, e3)
    part = work.shape[1]

    def combine(totals, squares, counts):
        tokens = sum(jnp.sum(n, axis=0, keepdims=True) for n in counts)
        mean = sum(jnp.sum(t, axis=0, keepdims=True) for t in totals) / tokens
        offs = [t / n - mean for t, n in zip(totals, counts)]
        square = sum(
            jnp.sum(q + n * o * o, axis=0, keepdims=True)
            for q, n, o in zip(squares, counts, offs)
        )
        return offs, lax.rsqrt(square / tokens + epsilon), tokens

    for s, t_rows in enumerate((t_own, t_mate)):
        offs, scale, _ = combine(
            [e[8 * s : 8 * s + 4, :] for e in every],
            [e[8 * s + 4 : 8 * s + 8, :] for e in every],
            [e[16:20, :] for e in every],
        )
        for j in range(SIDE):
            t_rows[j * SIDE : (j + 1) * SIDE, :] = offs[j] * scale
        t_rows[SIDE * SIDE : SIDE * SIDE + 1, :] = scale
    slots = [slice(i * part, (i + 1) * part) for i in (1, 2, 3, 0)]
    counts = [e[16:20, 0:part] for e in every]
    offs, scale, tokens = combine(
        [e[20:24, c] for e, c in zip(every, slots)],
        [e[24:28, c] for e, c in zip(every, slots)],
        counts,
    )
    scale = scale / jnp.sqrt(tokens)
    work[...] = jnp.zeros_like(work)
    for j in range(SIDE):
        work[j * SIDE : (j + 1) * SIDE, :] = offs[j] * scale * counts[j]
    work[SIDE * SIDE : SIDE * SIDE + 1, :] = scale
    s_left[...] = work[...].T


def settle(every):
    columns = every[0].shape[1]
    part = columns // SIDE
    S = jax.ShapeDtypeStruct
    return pl.pallas_call(
        settle_kernel,
        in_specs=[vmem()] * SIDE,
        out_specs=[vmem()] * 3,
        out_shape=[S((SIDE * SIDE + 1, columns), f32)] * 2 + [S((part, 128), f32)],
        scratch_shapes=[pltpu.VMEM((128, part), f32)],
        compiler_params=pltpu.CompilerParams(vmem_limit_bytes=8 * 2**20),
    )(*every)


def pool_kernel(place, counts, before, teacher, behind, starts, weights, full, mix, share, pooled, lines, meta):
    window = SUB + 2 * HALO
    length = teacher.shape[0]
    j = pl.program_id(0)

    @pl.when(j == 0)
    def _():
        lines[...] = jnp.zeros_like(lines)
        lines[0:1, :] = (starts[...] - (place[2] * SIDE + place[3]) * length).astype(f32)
        lines[1 : 1 + BAND, :] = weights[...].astype(f32)
        meta[...] = lines[...].T.astype(jnp.int32)
        for r in range(SIDE):
            rows = slice(r * SUB, (r + 1) * SUB)
            spot = lax.broadcasted_iota(jnp.int32, (SUB, window), 1)
            local = meta[rows, 0:1] - (r * SUB - HALO)
            found = jnp.zeros((SUB, window), jnp.int32)
            whole = jnp.zeros((SUB, 1), jnp.int32)
            for k in range(BAND):
                weight = meta[rows, 1 + k : 2 + k]
                found = found + jnp.where(spot == local + k, weight, 0)
                whole = whole + weight
            mix[rows, :] = found.astype(f32).astype(bf16)
            share[rows, :] = jnp.broadcast_to(whole.astype(f32), (SUB, 128))

    total = jnp.zeros((1, teacher.shape[1]), f32)
    alive = jnp.int32(0)
    for r in range(SIDE):
        rows = slice(r * SUB, (r + 1) * SUB)
        low, high = r * SUB - HALO, (r + 1) * SUB + HALO
        parts = [teacher[max(low, 0) : min(high, length), :]]
        if low < 0:
            parts = [before[...]] + parts
        if high > length:
            parts = parts + [behind[...]]
        seen = jnp.concatenate(parts, axis=0) if len(parts) > 1 else parts[0]
        value = jnp.dot(mix[rows, :], seen, preferred_element_type=f32)
        value = value / share[rows, 0:1]
        pooled[rows, :] = value
        live = lax.broadcasted_iota(jnp.int32, value.shape, 0) < counts[0, r]
        total = total + jnp.sum(jnp.where(live, value, 0.0), axis=0, keepdims=True)
        alive = alive + counts[0, r]
    mean = total / alive.astype(f32)
    square = jnp.zeros_like(total)
    for r in range(SIDE):
        rows = slice(r * SUB, (r + 1) * SUB)
        value = pooled[rows, :]
        live = lax.broadcasted_iota(jnp.int32, value.shape, 0) < counts[0, r]
        dev = jnp.where(live, value - mean, 0.0)
        small = dev.astype(bf16)
        full[rows, :] = small
        square = square + jnp.sum(dev * dev, axis=0, keepdims=True)
    lane = lax.broadcasted_iota(jnp.int32, total.shape, 1)
    sizes = jnp.zeros(total.shape, jnp.int32)
    for r in range(SIDE):
        sizes = sizes + jnp.where(lane == r, counts[0, r], 0)
    rows = in_parts(total) + in_parts(square) + (sizes.astype(f32).astype(bf16),)
    rows = rows + (jnp.zeros((EXTRA - len(rows), total.shape[1]), bf16),)
    full[length:, :] = jnp.concatenate(rows, axis=0)


def pool(place, counts, before, teacher, behind, starts, weights):
    rows, columns = teacher.shape
    tile = 256
    return pl.pallas_call(
        pool_kernel,
        grid=(columns // tile,),
        in_specs=[
            smem(),
            smem(),
            pl.BlockSpec((HALO, tile), lambda j: (0, j)),
            pl.BlockSpec((rows, tile), lambda j: (0, j)),
            pl.BlockSpec((HALO, tile), lambda j: (0, j)),
            pl.BlockSpec(starts.shape, lambda j: (0, 0)),
            pl.BlockSpec(weights.shape, lambda j: (0, 0)),
        ],
        out_specs=pl.BlockSpec((rows + EXTRA, tile), lambda j: (0, j)),
        out_shape=jax.ShapeDtypeStruct((rows + EXTRA, columns), bf16),
        scratch_shapes=[
            pltpu.VMEM((rows, SUB + 2 * HALO), bf16),
            pltpu.VMEM((rows, 128), f32),
            pltpu.VMEM((rows, tile), f32),
            pltpu.VMEM((128, rows), f32),
            pltpu.VMEM((rows, 128), jnp.int32),
        ],
        compiler_params=pltpu.CompilerParams(vmem_limit_bytes=32 * 2**20),
        cost_estimate=pl.CostEstimate(
            flops=2 * rows * 256 * columns, bytes_accessed=6 * rows * columns, transcendentals=0
        ),
    )(place, counts, before, teacher, behind, starts, weights)


def with_ones(a):
    return jnp.concatenate([a, jnp.ones((16, a.shape[1]), bf16)], axis=0)


def less_mean(total, near):
    part = total.shape[0] - 16
    return total[:part] - near * total[part : part + 1]


def first_kernel(place, a0, a1, a2, b0, b1, b2, near, out):
    z = place[0]
    depth = a0.shape[1]
    fill = jnp.zeros((depth - 3 * SUB, b0.shape[1]), bf16)
    total = None
    for a, step in zip((a0, a1, a2), COMING):
        rows = pl.ds(pl.multiple_of(lax.rem(z + step, SIDE) * SUB, 16), SUB)
        b = jnp.concatenate([b0[rows, :], b1[rows, :], b2[rows, :], fill], axis=0)
        term = jnp.dot(with_ones(a[...]), b, preferred_element_type=f32)
        total = term if total is None else total + term
    out[...] = less_mean(total, near[...])


def first_product(place, left, right, near):
    depth = left[0].shape[1]
    rows = near.shape[0]
    part = rows // SIDE
    length, columns = right[0].shape
    near_depth = 640
    return pl.pallas_call(
        first_kernel,
        grid_spec=pltpu.PrefetchScalarGridSpec(
            num_scalar_prefetch=1,
            grid=(SIDE,),
            in_specs=[pl.BlockSpec((part, near_depth), lambda i, place: (i, 0))] * 3
            + [pl.BlockSpec((length, columns), lambda i, place: (0, 0))] * 3
            + [pl.BlockSpec((part, 1), lambda i, place: (i, 0))],
            out_specs=pl.BlockSpec((part, columns), lambda i, place: (i, 0)),
        ),
        out_shape=pltpu.HBM((rows, columns), f32),
        compiler_params=pltpu.CompilerParams(vmem_limit_bytes=40 * 2**20),
        cost_estimate=pl.CostEstimate(
            flops=2 * rows * 3 * near_depth * columns,
            bytes_accessed=6 * rows * depth + 6 * length * columns + 4 * rows * columns,
            transcendentals=0,
        ),
    )(place, *left, *right, near)


def last_sums(place, refs):
    z = place[0]
    tails, far_a, near = refs[:3], refs[3], refs[4]
    sides = (refs[5:10], refs[10:15])
    results = []
    lefts = [with_ones(t[...]) for t in tails]
    far_left = with_ones(far_a[...])
    for b0, b1, b2, far_b, done in sides:
        fill = jnp.zeros((tails[0].shape[1] - SUB, far_b.shape[1]), bf16)
        total = None
        for a, step in zip(lefts, COMING):
            rows = pl.ds(pl.multiple_of(lax.rem(z + step, SIDE) * SUB, 16), SUB)
            b = jnp.concatenate([fill, far_b[rows, :]], axis=0)
            term = jnp.dot(a, b, preferred_element_type=f32)
            total = term if total is None else total + term
        rows = pl.ds(pl.multiple_of(lax.rem(z + 2, SIDE) * SUB, 16), SUB)
        b = jnp.concatenate([b0[...], b1[...], b2[...], far_b[rows, :]], axis=0)
        total = total + jnp.dot(far_left, b, preferred_element_type=f32)
        results.append(less_mean(total, near[...]) + done[...])
    return results


def far_kernel(place, *refs):
    up, down = refs[15:]
    results = last_sums(place, refs)
    up[...] = results[0].astype(bf16)
    down[...] = results[1].astype(bf16)


def own_kernel(place, *refs):
    kept = refs[15]
    half = kept.shape[1] // 2
    results = last_sums(place, refs)
    kept[:, :half] = results[0]
    kept[:, half:] = results[1]


def close_kernel(place, *refs):
    from_back, from_next, up, down = refs[15:]
    i = pl.program_id(0)
    half = from_back.shape[1]
    results = last_sums(place, refs)

    @pl.when(i == 0)
    def _():
        up[:, :half] = (results[0] + from_back[...].astype(f32)).astype(bf16)
        up[:, half:] = results[1].astype(bf16)

    @pl.when(i == 1)
    def _():
        down[:, :half] = results[0].astype(bf16)
        down[:, half:] = (results[1] + from_next[...].astype(f32)).astype(bf16)


def last_product(place, k, kind, left, far_left, near, own, mate, arrived=()):
    depth = left[0].shape[1]
    part = near.shape[0] // SIDE
    half = own[0].shape[1] // 2
    kernel, start, far_start, steps = {
        "far": (far_kernel, 0, 0, 1),
        "own": (own_kernel, 1, 1, 1),
        "close": (close_kernel, 2, 0, 2),
    }[kind]
    one = lambda i, place: (0, 0)
    tail = 256
    side = (
        [pl.BlockSpec((SUB, half), lambda i, place: (lax.rem(place[0] + 2, SIDE), k))] * 3
        + [pl.BlockSpec((own[3].shape[0], half), one)]
        + [pl.BlockSpec((part, half), lambda i, place: (start + i, k))]
    )
    in_specs = (
        [pl.BlockSpec((part, tail), lambda i, place: (start + i, depth // tail - 1))] * 3
        + [pl.BlockSpec((part, depth), lambda i, place: (far_start + i, 0))]
        + [pl.BlockSpec((part, 1), lambda i, place: (start + i, 0))]
        + side * 2
        + [pl.BlockSpec((part, half), one)] * len(arrived)
    )
    S = jax.ShapeDtypeStruct
    shapes = {
        "far": [S((part, half), bf16)] * 2,
        "own": [S((part, 2 * half), f32)],
        "close": [S((part, 2 * half), bf16)] * 2,
    }[kind]
    return pl.pallas_call(
        kernel,
        grid_spec=pltpu.PrefetchScalarGridSpec(
            num_scalar_prefetch=1,
            grid=(steps,),
            in_specs=in_specs,
            out_specs=[pl.BlockSpec(s.shape, one) for s in shapes],
        ),
        out_shape=shapes,
        compiler_params=pltpu.CompilerParams(vmem_limit_bytes=40 * 2**20),
        cost_estimate=pl.CostEstimate(
            flops=2 * steps * part * 2 * depth * 2 * half,
            bytes_accessed=3 * steps * depth * part + 5 * depth * half + 8 * part * half,
            transcendentals=0,
        ),
    )(place, *left, far_left, near, *own, *mate, *arrived)


def final_kernel(place, kept, first, second, s_left, t_own, t_mate, *rest):
    out = rest[-1]
    t = jnp.where(pl.program_id(0) == 0, t_own[...], t_mate[...])
    shards_all = SIDE * SIDE
    between = jnp.dot(
        s_left[:, :shards_all],
        t[:shards_all],
        preferred_element_type=f32,
        precision=lax.Precision.HIGHEST,
    )
    inside = kept[...] + first[...].astype(f32) + second[...].astype(f32)
    row_scale = s_left[:, shards_all : shards_all + 1]
    out[...] = inside * row_scale * t[shards_all : shards_all + 1] + between


def final(place, k, kept, first, second, s_left, t_own, t_mate, whole=None):
    part, columns = kept.shape
    half = columns // 2
    block = pl.BlockSpec((part, half), lambda i, place: (0, i))
    in_specs = (
        [block] * 3
        + [pl.BlockSpec(s_left.shape, lambda i, place: (0, 0))]
        + [pl.BlockSpec((t_own.shape[0], half), lambda i, place: (0, k))] * 2
    )
    more, aliases = (), {}
    if whole is not None:
        in_specs = in_specs + [pl.BlockSpec(memory_space=pl.ANY)]
        more, aliases = (whole,), {7: 0}
    return pl.pallas_call(
        final_kernel,
        grid_spec=pltpu.PrefetchScalarGridSpec(
            num_scalar_prefetch=1,
            grid=(2,),
            in_specs=in_specs,
            out_specs=pl.BlockSpec(
                (part, half), lambda i, place: (0, lax.rem(place[1] + i, 2) * 2 + k)
            ),
        ),
        out_shape=jax.ShapeDtypeStruct((part, 2 * columns), f32),
        input_output_aliases=aliases,
        compiler_params=pltpu.CompilerParams(vmem_limit_bytes=16 * 2**20),
        cost_estimate=pl.CostEstimate(
            flops=6 * part * columns, bytes_accessed=12 * part * columns, transcendentals=0
        ),
    )(place, kept, first, second, s_left, t_own, t_mate, *more)


def per_device(student, teacher, starts, weights, counts):
    y, x, z, c = (lax.axis_index(n) for n in ("y", "x", "row", "col"))
    place = jnp.stack([z, c, y, x]).astype(jnp.int32)
    rows = starts.shape[0]
    columns = teacher.shape[1]
    half = columns // 2
    width = student.shape[1] // SIDE

    up = [(i, (i + 1) % 16) for i in range(16)]
    down = [(j, i) for i, j in up]
    before = lax.ppermute(teacher[rows - HALO :], ("y", "x"), up)
    behind = lax.ppermute(teacher[:HALO], ("y", "x"), down)

    packed = pack(place, counts, student)
    packed, before, behind = lax.optimization_barrier((packed, before, behind))
    got = [packed[0], ring(packed[1], "x", 1), ring(packed[2], "x", -1), ring(packed[3], "x", 2)]
    standard = pool(place, counts, before, teacher, behind, starts[None], weights.T)
    got, standard = lax.optimization_barrier((got, standard))
    turned, mean = turn(place, counts, got)

    right, left = ring(standard, "x", 1), ring(standard, "x", -1)
    up, down = ring(turned, "row", 1), ring(turned, "row", -1)
    t_standard = swap(standard)
    right, left, up, down, t_standard = lax.optimization_barrier(
        (right, left, up, down, t_standard)
    )

    x_far = [ring(right[:, :half], "x", 1), ring(left[:, half:], "x", -1)]
    z_far = [ring(up[: width // 2], "row", 1), ring(down[width // 2 :], "row", -1)]
    t_right, t_left = swap(right), swap(left)
    own, mate = [standard, right, left], [t_standard, t_right, t_left]
    near_z = [turned, up, down]
    own_sum = first_product(place, near_z, own, mean)
    mate_sum = first_product(place, near_z, mate, mean)
    x_far, z_far, own_sum, mate_sum = lax.optimization_barrier((x_far, z_far, own_sum, mate_sum))

    t_x_far = [swap(f) for f in x_far]
    sides = [
        (own + [x_far[k], own_sum], mate + [t_x_far[k], mate_sum]) for k in range(2)
    ]
    arrived = []
    for k in range(2):
        o = last_product(place, k, "far", near_z, z_far[0], mean, *sides[k])
        arrived.append((ring(o[0], "y", 1), ring(o[1], "y", -1)))
    moments = shards(place, near_z, z_far[1], own + x_far, mate + t_x_far)
    every = ring_all(moments, "y")
    arrived, every = lax.optimization_barrier((arrived, every))
    t_rows, t_mate, s_left = settle(every)
    passed = []
    for k in range(2):
        v = last_product(place, k, "close", near_z, z_far[1], mean, *sides[k], arrived[k])
        passed.append((ring(v[0], "y", 1), ring(v[1], "y", -1)))
    out = None
    for k in range(2):
        kept = last_product(place, k, "own", near_z, z_far[0], mean, *sides[k])[0]
        out = final(place, k, kept, *passed[k], s_left, t_rows, t_mate, out)
    return out[None, None]


def solution(mesh):
    fine = Mesh(mesh.devices.reshape(SIDE, SIDE, SIDE, 2), ("y", "x", "row", "col"))
    seq = ("y", "x")
    placed = (
        P(seq + ("row",), "col"),
        P(seq, ("row", "col")),
        P(seq),
        P(seq, None),
        P(seq, None),
    )
    return jax.shard_map(
        per_device,
        mesh=fine,
        in_specs=placed,
        out_specs=P("col", seq, None, "row"),
        check_vma=False,
    )
```

```python
import jax
import jax.numpy as jnp
from jax import lax
from jax.experimental import pallas as pl
from jax.experimental.pallas import tpu as pltpu
from jax.sharding import Mesh
from jax.sharding import PartitionSpec as P

SUB = 192
BAND = 4
HALO = 16
EXTRA = 16
SIDE = 4
COMING = (0, SIDE - 1, 1, 2)
epsilon = 1e-05
f32 = jnp.float32
bf16 = jnp.bfloat16


def ring(value, axis, step):
    return lax.ppermute(value, axis, [(i, (i + step) % SIDE) for i in range(SIDE)])


def ring_all(value, axis):
    return [value, ring(value, axis, 1), ring(value, axis, -1), ring(value, axis, 2)]


def swap(value):
    return lax.ppermute(value, "col", [(0, 1), (1, 0)])


def after(value, *others):
    return lax.optimization_barrier((value, others))[0]


def in_parts(value):
    high = value.astype(bf16)
    rest = value - high.astype(f32)
    middle = rest.astype(bf16)
    low = (rest - middle.astype(f32)).astype(bf16)
    return high, middle, low


def from_parts(rows):
    rows = rows.astype(f32)
    return rows[0:1] + rows[1:2] + rows[2:3]


def smem():
    return pl.BlockSpec(memory_space=pltpu.SMEM)


def vmem():
    return pl.BlockSpec(memory_space=pltpu.VMEM)


def pack_kernel(place, counts, student, *outs):
    y, x, count = place[2], place[3], counts[0, place[0]]
    part = outs[0].shape[1] // SIDE
    for r, x_step in enumerate((0, 1, SIDE - 1, 2)):
        at = lax.rem(x + x_step, SIDE)
        for i, y_step in enumerate((2, 0, 1, SIDE - 1)):
            slot = lax.rem(y + y_step, SIDE) * SIDE + at
            first = pl.multiple_of(slot * part, 128)
            columns = slice(i * part, (i + 1) * part)
            block = student[:, pl.ds(first, part)]
            outs[r][:SUB, columns] = block
            value = block.astype(f32)
            live = lax.broadcasted_iota(jnp.int32, value.shape, 0) < count
            total = jnp.sum(jnp.where(live, value, 0.0), axis=0, keepdims=True)
            dev = jnp.where(live, value - total / count.astype(f32), 0.0)
            square = jnp.sum(dev * dev, axis=0, keepdims=True)
            rows = in_parts(total) + in_parts(square)
            rows = rows + (jnp.zeros((EXTRA - len(rows), part), bf16),)
            outs[r][SUB:, columns] = jnp.concatenate(rows, axis=0)


def pack(place, counts, student):
    width = student.shape[1] // SIDE
    return pl.pallas_call(
        pack_kernel,
        in_specs=[smem(), smem(), vmem()],
        out_specs=[vmem()] * SIDE,
        out_shape=[jax.ShapeDtypeStruct((SUB + EXTRA, width), bf16)] * SIDE,
        compiler_params=pltpu.CompilerParams(vmem_limit_bytes=24 * 2**20),
        cost_estimate=pl.CostEstimate(
            flops=8 * SUB * student.shape[1],
            bytes_accessed=4 * SUB * student.shape[1],
            transcendentals=0,
        ),
    )(place, counts, student)


def turn_kernel(place, counts, p0, p1, p2, p3, turned, near):
    count = counts[0, place[0]]
    pieces = (p0, p1, p2, p3)
    rows = jnp.concatenate([p[:SUB, :] for p in pieces], axis=0)
    flat = rows.T
    width, depth = flat.shape
    turned[:width, :] = flat
    moments = jnp.concatenate([p[SUB : SUB + 6, :].astype(f32) for p in pieces], axis=0)
    rests = [
        jnp.concatenate([moments[3 * m + i : 3 * m + i + 1, depth:] for i in range(3)], axis=1)
        for m in range(8)
    ]
    turned[width:, :] = jnp.concatenate([moments[:, :depth]] + rests, axis=0).astype(bf16)
    mine = flat[:, :SUB].astype(f32)
    live = lax.broadcasted_iota(jnp.int32, mine.shape, 1) < count
    total = jnp.sum(jnp.where(live, mine, 0.0), axis=1, keepdims=True)
    near[...] = total / count.astype(f32)


def turn(place, counts, pieces):
    width = pieces[0].shape[1]
    return pl.pallas_call(
        turn_kernel,
        in_specs=[smem()] * 2 + [vmem()] * SIDE,
        out_specs=[vmem()] * 2,
        out_shape=[
            jax.ShapeDtypeStruct((width + 2 * EXTRA, SIDE * SUB), bf16),
            jax.ShapeDtypeStruct((width, 1), f32),
        ],
        compiler_params=pltpu.CompilerParams(vmem_limit_bytes=16 * 2**20),
        cost_estimate=pl.CostEstimate(
            flops=0, bytes_accessed=4 * SUB * SIDE * width, transcendentals=0
        ),
    )(place, counts, *pieces)


def shards_kernel(place, *refs):
    zs, own, mate, out = refs[:SIDE], refs[SIDE : SIDE + 5], refs[SIDE + 5 : SIDE + 10], refs[-1]
    half = own[3].shape[1]
    depth = zs[0].shape[1]
    blocks = []
    for ref in zs:
        rows = ref[...].astype(f32)
        rests = [
            rows[24 + m : 25 + m, i * (depth // 3) : (i + 1) * (depth // 3)]
            for m in range(8)
            for i in range(3)
        ]
        rests = jnp.concatenate(rests, axis=0)
        blocks.append(jnp.concatenate([rows[:24], rests], axis=1))
    lane = lax.broadcasted_iota(jnp.int32, (1, half), 1)
    for r in range(SIDE):
        for s, side in enumerate((own, mate)):
            if r < 3:
                rows = side[r][...]
            else:
                rows = jnp.concatenate([side[3][...], side[4][...]], axis=1)
            out[8 * s + r : 8 * s + r + 1, :] = from_parts(rows[0:3])
            out[8 * s + SIDE + r : 8 * s + SIDE + r + 1, :] = from_parts(rows[3:6])
        sizes = own[r][...][6:7, :half].astype(f32)
        n = jnp.sum(jnp.where(lane < SIDE, sizes, 0.0), axis=1, keepdims=True)
        out[16 + r : 17 + r, :] = jnp.broadcast_to(n, (1, out.shape[1]))
        totals = [from_parts(b[6 * r : 6 * r + 3]) for b in blocks]
        squares = [from_parts(b[6 * r + 3 : 6 * r + 6]) for b in blocks]
        total = totals[0] + totals[1] + totals[2] + totals[3]
        mean = total / n
        square = jnp.zeros_like(total)
        for q, step in enumerate(COMING):
            here = lax.rem(place[0] + step, SIDE)
            size = jnp.sum(jnp.where(lane == here, sizes, 0.0), axis=1, keepdims=True)
            off = totals[q] / size - mean
            square = square + squares[q] + size * off * off
        out[20 + r : 21 + r, :] = total
        out[24 + r : 25 + r, :] = square
    out[28:32, :] = jnp.zeros((4, out.shape[1]), f32)


def shards(place, left, far_left, own, mate):
    depth = left[0].shape[1]
    columns = own[0].shape[1]

    def low(value, rows):
        first = value.shape[0] // rows - 1
        return pl.BlockSpec((rows, value.shape[1]), lambda i, place: (first, 0))

    return pl.pallas_call(
        shards_kernel,
        grid_spec=pltpu.PrefetchScalarGridSpec(
            num_scalar_prefetch=1,
            grid=(1,),
            in_specs=[low(v, 2 * EXTRA) for v in left + [far_left]]
            + [low(v, EXTRA) for v in own + mate],
            out_specs=pl.BlockSpec((32, columns), lambda i, place: (0, 0)),
        ),
        out_shape=jax.ShapeDtypeStruct((32, columns), f32),
        compiler_params=pltpu.CompilerParams(vmem_limit_bytes=8 * 2**20),
    )(place, *left, far_left, *own, *mate)


def settle_kernel(e0, e1, e2, e3, t_own, t_mate, s_left, work):
    every = (e0, e1, e2, e3)
    part = work.shape[1]

    def combine(totals, squares, counts):
        tokens = sum(jnp.sum(n, axis=0, keepdims=True) for n in counts)
        mean = sum(jnp.sum(t, axis=0, keepdims=True) for t in totals) / tokens
        offs = [t / n - mean for t, n in zip(totals, counts)]
        square = sum(
            jnp.sum(q + n * o * o, axis=0, keepdims=True)
            for q, n, o in zip(squares, counts, offs)
        )
        return offs, lax.rsqrt(square / tokens + epsilon), tokens

    for s, t_rows in enumerate((t_own, t_mate)):
        offs, scale, _ = combine(
            [e[8 * s : 8 * s + 4, :] for e in every],
            [e[8 * s + 4 : 8 * s + 8, :] for e in every],
            [e[16:20, :] for e in every],
        )
        for j in range(SIDE):
            t_rows[j * SIDE : (j + 1) * SIDE, :] = offs[j] * scale
        t_rows[SIDE * SIDE : SIDE * SIDE + 1, :] = scale
    slots = [slice(i * part, (i + 1) * part) for i in (1, 2, 3, 0)]
    counts = [e[16:20, 0:part] for e in every]
    offs, scale, tokens = combine(
        [e[20:24, c] for e, c in zip(every, slots)],
        [e[24:28, c] for e, c in zip(every, slots)],
        counts,
    )
    scale = scale / jnp.sqrt(tokens)
    work[...] = jnp.zeros_like(work)
    for j in range(SIDE):
        work[j * SIDE : (j + 1) * SIDE, :] = offs[j] * scale * counts[j]
    work[SIDE * SIDE : SIDE * SIDE + 1, :] = scale
    s_left[...] = work[...].T


def settle(every):
    columns = every[0].shape[1]
    part = columns // SIDE
    S = jax.ShapeDtypeStruct
    return pl.pallas_call(
        settle_kernel,
        in_specs=[vmem()] * SIDE,
        out_specs=[vmem()] * 3,
        out_shape=[S((SIDE * SIDE + 1, columns), f32)] * 2 + [S((part, 128), f32)],
        scratch_shapes=[pltpu.VMEM((128, part), f32)],
        compiler_params=pltpu.CompilerParams(vmem_limit_bytes=8 * 2**20),
    )(*every)


def pool_kernel(place, counts, before, teacher, behind, starts, weights, full, mark, mix, share, pooled, lines, meta):
    window = SUB + 2 * HALO
    length = teacher.shape[0]
    j = pl.program_id(0)

    @pl.when(j == 0)
    def _():
        lines[...] = jnp.zeros_like(lines)
        lines[0:1, :] = (starts[...] - (place[2] * SIDE + place[3]) * length).astype(f32)
        lines[1 : 1 + BAND, :] = weights[...].astype(f32)
        meta[...] = lines[...].T.astype(jnp.int32)
        for r in range(SIDE):
            rows = slice(r * SUB, (r + 1) * SUB)
            spot = lax.broadcasted_iota(jnp.int32, (SUB, window), 1)
            local = meta[rows, 0:1] - (r * SUB - HALO)
            found = jnp.zeros((SUB, window), jnp.int32)
            whole = jnp.zeros((SUB, 1), jnp.int32)
            for k in range(BAND):
                weight = meta[rows, 1 + k : 2 + k]
                found = found + jnp.where(spot == local + k, weight, 0)
                whole = whole + weight
            mix[rows, :] = found.astype(f32).astype(bf16)
            share[rows, :] = jnp.broadcast_to(whole.astype(f32), (SUB, 128))

    total = jnp.zeros((1, teacher.shape[1]), f32)
    alive = jnp.int32(0)
    for r in range(SIDE):
        rows = slice(r * SUB, (r + 1) * SUB)
        low, high = r * SUB - HALO, (r + 1) * SUB + HALO
        parts = [teacher[max(low, 0) : min(high, length), :]]
        if low < 0:
            parts = [before[...]] + parts
        if high > length:
            parts = parts + [behind[...]]
        seen = jnp.concatenate(parts, axis=0) if len(parts) > 1 else parts[0]
        value = jnp.dot(mix[rows, :], seen, preferred_element_type=f32)
        value = value / share[rows, 0:1]
        pooled[rows, :] = value
        live = lax.broadcasted_iota(jnp.int32, value.shape, 0) < counts[0, r]
        total = total + jnp.sum(jnp.where(live, value, 0.0), axis=0, keepdims=True)
        alive = alive + counts[0, r]
    mean = total / alive.astype(f32)
    square = jnp.zeros_like(total)
    for r in range(SIDE):
        rows = slice(r * SUB, (r + 1) * SUB)
        value = pooled[rows, :]
        live = lax.broadcasted_iota(jnp.int32, value.shape, 0) < counts[0, r]
        dev = jnp.where(live, value - mean, 0.0)
        small = dev.astype(bf16)
        full[rows, :] = small
        square = square + jnp.sum(dev * dev, axis=0, keepdims=True)
    lane = lax.broadcasted_iota(jnp.int32, total.shape, 1)
    sizes = jnp.zeros(total.shape, jnp.int32)
    for r in range(SIDE):
        sizes = sizes + jnp.where(lane == r, counts[0, r], 0)
    rows = in_parts(total) + in_parts(square) + (sizes.astype(f32).astype(bf16),)
    rows = rows + (jnp.zeros((EXTRA - len(rows), total.shape[1]), bf16),)
    full[length:, :] = jnp.concatenate(rows, axis=0)
    mark[...] = jnp.zeros_like(mark)


def pool(place, counts, before, teacher, behind, starts, weights):
    rows, columns = teacher.shape
    tile = 256
    return pl.pallas_call(
        pool_kernel,
        grid=(columns // tile,),
        in_specs=[
            smem(),
            smem(),
            pl.BlockSpec((HALO, tile), lambda j: (0, j)),
            pl.BlockSpec((rows, tile), lambda j: (0, j)),
            pl.BlockSpec((HALO, tile), lambda j: (0, j)),
            pl.BlockSpec(starts.shape, lambda j: (0, 0)),
            pl.BlockSpec(weights.shape, lambda j: (0, 0)),
        ],
        out_specs=[
            pl.BlockSpec((rows + EXTRA, tile), lambda j: (0, j)),
            pl.BlockSpec((8, 128), lambda j: (0, 0)),
        ],
        out_shape=[
            jax.ShapeDtypeStruct((rows + EXTRA, columns), bf16),
            jax.ShapeDtypeStruct((8, 128), f32),
        ],
        scratch_shapes=[
            pltpu.VMEM((rows, SUB + 2 * HALO), bf16),
            pltpu.VMEM((rows, 128), f32),
            pltpu.VMEM((rows, tile), f32),
            pltpu.VMEM((128, rows), f32),
            pltpu.VMEM((rows, 128), jnp.int32),
        ],
        compiler_params=pltpu.CompilerParams(vmem_limit_bytes=32 * 2**20),
        cost_estimate=pl.CostEstimate(
            flops=2 * rows * 256 * columns, bytes_accessed=6 * rows * columns, transcendentals=0
        ),
    )(place, counts, before, teacher, behind, starts, weights)


def with_ones(a):
    return jnp.concatenate([a, jnp.ones((16, a.shape[1]), bf16)], axis=0)


def less_mean(total, near):
    part = total.shape[0] - 16
    return total[:part] - near * total[part : part + 1]


def first_kernel(place, a0, a1, a2, b0, b1, b2, near, out):
    z = place[0]
    depth = a0.shape[1]
    fill = jnp.zeros((depth - 3 * SUB, b0.shape[1]), bf16)
    total = None
    for a, step in zip((a0, a1, a2), COMING):
        rows = pl.ds(pl.multiple_of(lax.rem(z + step, SIDE) * SUB, 16), SUB)
        b = jnp.concatenate([b0[rows, :], b1[rows, :], b2[rows, :], fill], axis=0)
        term = jnp.dot(with_ones(a[...]), b, preferred_element_type=f32)
        total = term if total is None else total + term
    out[...] = less_mean(total, near[...])


def first_product(place, left, right, near):
    depth = left[0].shape[1]
    rows = near.shape[0]
    part = rows // SIDE
    length, columns = right[0].shape
    near_depth = 640
    return pl.pallas_call(
        first_kernel,
        grid_spec=pltpu.PrefetchScalarGridSpec(
            num_scalar_prefetch=1,
            grid=(SIDE,),
            in_specs=[pl.BlockSpec((part, near_depth), lambda i, place: (i, 0))] * 3
            + [pl.BlockSpec((length, columns), lambda i, place: (0, 0))] * 3
            + [pl.BlockSpec((part, 1), lambda i, place: (i, 0))],
            out_specs=pl.BlockSpec((part, columns), lambda i, place: (i, 0)),
        ),
        out_shape=pltpu.HBM((rows, columns), f32),
        compiler_params=pltpu.CompilerParams(vmem_limit_bytes=40 * 2**20),
        cost_estimate=pl.CostEstimate(
            flops=2 * rows * 3 * near_depth * columns,
            bytes_accessed=6 * rows * depth + 6 * length * columns + 4 * rows * columns,
            transcendentals=0,
        ),
    )(place, *left, *right, near)


def last_sums(place, refs):
    z = place[0]
    tails, far_a, near = refs[:3], refs[3], refs[4]
    sides = (refs[5:10], refs[10:15])
    results = []
    lefts = [with_ones(t[...]) for t in tails]
    far_left = with_ones(far_a[...])
    for b0, b1, b2, far_b, done in sides:
        fill = jnp.zeros((tails[0].shape[1] - SUB, far_b.shape[1]), bf16)
        total = None
        for a, step in zip(lefts, COMING):
            rows = pl.ds(pl.multiple_of(lax.rem(z + step, SIDE) * SUB, 16), SUB)
            b = jnp.concatenate([fill, far_b[rows, :]], axis=0)
            term = jnp.dot(a, b, preferred_element_type=f32)
            total = term if total is None else total + term
        rows = pl.ds(pl.multiple_of(lax.rem(z + 2, SIDE) * SUB, 16), SUB)
        b = jnp.concatenate([b0[...], b1[...], b2[...], far_b[rows, :]], axis=0)
        total = total + jnp.dot(far_left, b, preferred_element_type=f32)
        results.append(less_mean(total, near[...]) + done[...])
    return results


def far_kernel(place, *refs):
    up, down = refs[15:]
    results = last_sums(place, refs)
    up[...] = results[0].astype(bf16)
    down[...] = results[1].astype(bf16)


def own_kernel(place, *refs):
    s_left, t_own, t_mate, base = refs[15:]
    half = base.shape[1] // 2
    every = SIDE * SIDE
    results = last_sums(place, refs)
    for i, t in enumerate((t_own, t_mate)):
        between = jnp.dot(
            s_left[:, :every],
            t[:every, :],
            preferred_element_type=f32,
            precision=lax.Precision.HIGHEST,
        )
        scaled = results[i] * s_left[:, every : every + 1] * t[every : every + 1, :]
        base[:, i * half : (i + 1) * half] = scaled + between


def close_kernel(place, *refs):
    from_back, from_next, up, down = refs[15:]
    i = pl.program_id(0)
    half = from_back.shape[1]
    results = last_sums(place, refs)

    @pl.when(i == 0)
    def _():
        up[:, :half] = (results[0] + from_back[...].astype(f32)).astype(bf16)
        up[:, half:] = results[1].astype(bf16)

    @pl.when(i == 1)
    def _():
        down[:, :half] = results[0].astype(bf16)
        down[:, half:] = (results[1] + from_next[...].astype(f32)).astype(bf16)


def last_product(place, k, kind, left, far_left, near, own, mate, arrived=()):
    depth = left[0].shape[1]
    part = near.shape[0] // SIDE
    half = own[0].shape[1] // 2
    kernel, start, far_start, steps = {
        "far": (far_kernel, 0, 0, 1),
        "own": (own_kernel, 1, 1, 1),
        "close": (close_kernel, 2, 0, 2),
    }[kind]
    one = lambda i, place: (0, 0)
    tail = 256
    side = (
        [pl.BlockSpec((SUB, half), lambda i, place: (lax.rem(place[0] + 2, SIDE), k))] * 3
        + [pl.BlockSpec((own[3].shape[0], half), one)]
        + [pl.BlockSpec((part, half), lambda i, place: (start + i, k))]
    )
    in_specs = (
        [pl.BlockSpec((part, tail), lambda i, place: (start + i, depth // tail - 1))] * 3
        + [pl.BlockSpec((part, depth), lambda i, place: (far_start + i, 0))]
        + [pl.BlockSpec((part, 1), lambda i, place: (start + i, 0))]
        + side * 2
        + (
            [pl.BlockSpec(arrived[0].shape, one)]
            + [pl.BlockSpec((a.shape[0], half), lambda i, place: (0, k)) for a in arrived[1:]]
            if kind == "own"
            else [pl.BlockSpec((part, half), one)] * len(arrived)
        )
    )
    S = jax.ShapeDtypeStruct
    shapes = {
        "far": [S((part, half), bf16)] * 2,
        "own": [S((part, 2 * half), f32)],
        "close": [S((part, 2 * half), bf16)] * 2,
    }[kind]
    return pl.pallas_call(
        kernel,
        grid_spec=pltpu.PrefetchScalarGridSpec(
            num_scalar_prefetch=1,
            grid=(steps,),
            in_specs=in_specs,
            out_specs=[pl.BlockSpec(s.shape, one) for s in shapes],
        ),
        out_shape=shapes,
        compiler_params=pltpu.CompilerParams(vmem_limit_bytes=40 * 2**20),
        cost_estimate=pl.CostEstimate(
            flops=2 * steps * part * 2 * depth * 2 * half,
            bytes_accessed=3 * steps * depth * part + 5 * depth * half + 8 * part * half,
            transcendentals=0,
        ),
    )(place, *left, far_left, near, *own, *mate, *arrived)


def final_kernel(place, base, first, second, s_left, t_own, t_mate, *rest):
    out = rest[-1]
    every = SIDE * SIDE
    last = slice(every, every + 1)
    t = jnp.where(pl.program_id(0) == 0, t_own[last, :], t_mate[last, :])
    inside = first[...].astype(f32) + second[...].astype(f32)
    out[...] = inside * s_left[:, last] * t + base[...]


def final(place, k, kept, first, second, s_left, t_own, t_mate, whole=None):
    part, columns = kept.shape
    half = columns // 2
    block = pl.BlockSpec((part, half), lambda i, place: (0, i))
    in_specs = (
        [block] * 3
        + [pl.BlockSpec(s_left.shape, lambda i, place: (0, 0))]
        + [pl.BlockSpec((t_own.shape[0], half), lambda i, place: (0, k))] * 2
    )
    more, aliases = (), {}
    if whole is not None:
        in_specs = in_specs + [pl.BlockSpec(memory_space=pl.ANY)]
        more, aliases = (whole,), {7: 0}
    return pl.pallas_call(
        final_kernel,
        grid_spec=pltpu.PrefetchScalarGridSpec(
            num_scalar_prefetch=1,
            grid=(2,),
            in_specs=in_specs,
            out_specs=pl.BlockSpec(
                (part, half), lambda i, place: (0, lax.rem(place[1] + i, 2) * 2 + k)
            ),
        ),
        out_shape=jax.ShapeDtypeStruct((part, 2 * columns), f32),
        input_output_aliases=aliases,
        compiler_params=pltpu.CompilerParams(vmem_limit_bytes=16 * 2**20),
        cost_estimate=pl.CostEstimate(
            flops=6 * part * columns, bytes_accessed=12 * part * columns, transcendentals=0
        ),
    )(place, kept, first, second, s_left, t_own, t_mate, *more)


def per_device(student, teacher, starts, weights, counts):
    y, x, z, c = (lax.axis_index(n) for n in ("y", "x", "row", "col"))
    place = jnp.stack([z, c, y, x]).astype(jnp.int32)
    rows = starts.shape[0]
    columns = teacher.shape[1]
    half = columns // 2
    width = student.shape[1] // SIDE

    up = [(i, (i + 1) % 16) for i in range(16)]
    down = [(j, i) for i, j in up]
    before = lax.ppermute(teacher[rows - HALO :], ("y", "x"), up)
    behind = lax.ppermute(teacher[:HALO], ("y", "x"), down)

    packed = pack(place, counts, student)
    packed, before, behind = lax.optimization_barrier((packed, before, behind))
    got = [packed[0], ring(packed[1], "x", 1), ring(packed[2], "x", -1), ring(packed[3], "x", 2)]
    standard, mark = pool(place, counts, before, teacher, behind, starts[None], weights.T)
    got, _ = lax.optimization_barrier((got, mark))
    turned, mean = turn(place, counts, got)

    right, left = ring(standard, "x", 1), ring(standard, "x", -1)
    up, down = ring(turned, "row", 1), ring(turned, "row", -1)
    t_standard = swap(standard)
    right, left, up, down, t_standard = lax.optimization_barrier(
        (right, left, up, down, t_standard)
    )

    x_far = [ring(right[:, :half], "x", 1), ring(left[:, half:], "x", -1)]
    z_far = [ring(up[: width // 2], "row", 1), ring(down[width // 2 :], "row", -1)]
    t_right, t_left = swap(right), swap(left)
    own, mate = [standard, right, left], [t_standard, t_right, t_left]
    near_z = [turned, up, down]
    own_sum = first_product(place, near_z, own, mean)
    mate_sum = first_product(place, near_z, mate, mean)
    x_far, z_far, own_sum, mate_sum = lax.optimization_barrier((x_far, z_far, own_sum, mate_sum))

    t_x_far = [swap(f) for f in x_far]
    sides = [
        (own + [x_far[k], own_sum], mate + [t_x_far[k], mate_sum]) for k in range(2)
    ]
    arrived, sent = [], []
    for k in range(2):
        o = last_product(place, k, "far", near_z, z_far[0], mean, *sides[k])
        sent.append(o[0])
        arrived.append((ring(o[0], "y", 1), ring(o[1], "y", -1)))
    far_rows = after(z_far[1], sent)
    every = ring_all(shards(place, near_z, far_rows, own + x_far, mate + t_x_far), "y")
    passed = []
    for k in range(2):
        if k == 1:
            arrived[k], every = lax.optimization_barrier((arrived[k], every))
        v = last_product(place, k, "close", near_z, z_far[1], mean, *sides[k], arrived[k])
        passed.append((ring(v[0], "y", 1), ring(v[1], "y", -1)))
    t_rows, t_mate, s_left = settle(every)
    settled = (s_left, t_rows, t_mate)
    out = None
    for k in range(2):
        base = last_product(place, k, "own", near_z, z_far[0], mean, *sides[k], settled)[0]
        out = final(place, k, base, *passed[k], *settled, out)
    return out[None, None]


def solution(mesh):
    fine = Mesh(mesh.devices.reshape(SIDE, SIDE, SIDE, 2), ("y", "x", "row", "col"))
    seq = ("y", "x")
    placed = (
        P(seq + ("row",), "col"),
        P(seq, ("row", "col")),
        P(seq),
        P(seq, None),
        P(seq, None),
    )
    return jax.shard_map(
        per_device,
        mesh=fine,
        in_specs=placed,
        out_specs=P("col", seq, None, "row"),
        check_vma=False,
    )
```

```python
import jax
import jax.numpy as jnp
from jax import lax
from jax.experimental import pallas as pl
from jax.experimental.pallas import tpu as pltpu
from jax.sharding import Mesh
from jax.sharding import PartitionSpec as P

SUB = 192
BAND = 4
HALO = 16
EXTRA = 16
SIDE = 4
COMING = (0, SIDE - 1, 1, 2)
epsilon = 1e-05
f32 = jnp.float32
bf16 = jnp.bfloat16


def ring(value, axis, step):
    return lax.ppermute(value, axis, [(i, (i + step) % SIDE) for i in range(SIDE)])


def ring_all(value, axis):
    return [value, ring(value, axis, 1), ring(value, axis, -1), ring(value, axis, 2)]


def swap(value):
    return lax.ppermute(value, "col", [(0, 1), (1, 0)])


def after(value, *others):
    return lax.optimization_barrier((value, others))[0]


def in_parts(value):
    high = value.astype(bf16)
    rest = value - high.astype(f32)
    middle = rest.astype(bf16)
    low = (rest - middle.astype(f32)).astype(bf16)
    return high, middle, low


def from_parts(rows):
    rows = rows.astype(f32)
    return rows[0:1] + rows[1:2] + rows[2:3]


def smem():
    return pl.BlockSpec(memory_space=pltpu.SMEM)


def vmem():
    return pl.BlockSpec(memory_space=pltpu.VMEM)


def pack_kernel(place, counts, student, *outs):
    y, x, count = place[2], place[3], counts[0, place[0]]
    part = outs[0].shape[1] // SIDE
    for r, x_step in enumerate((0, 1, SIDE - 1, 2)):
        at = lax.rem(x + x_step, SIDE)
        for i, y_step in enumerate((2, 0, 1, SIDE - 1)):
            slot = lax.rem(y + y_step, SIDE) * SIDE + at
            first = pl.multiple_of(slot * part, 128)
            columns = slice(i * part, (i + 1) * part)
            block = student[:, pl.ds(first, part)]
            outs[r][:SUB, columns] = block
            value = block.astype(f32)
            live = lax.broadcasted_iota(jnp.int32, value.shape, 0) < count
            total = jnp.sum(jnp.where(live, value, 0.0), axis=0, keepdims=True)
            dev = jnp.where(live, value - total / count.astype(f32), 0.0)
            square = jnp.sum(dev * dev, axis=0, keepdims=True)
            rows = in_parts(total) + in_parts(square)
            rows = rows + (jnp.zeros((EXTRA - len(rows), part), bf16),)
            outs[r][SUB:, columns] = jnp.concatenate(rows, axis=0)


def pack(place, counts, student):
    width = student.shape[1] // SIDE
    return pl.pallas_call(
        pack_kernel,
        in_specs=[smem(), smem(), vmem()],
        out_specs=[vmem()] * SIDE,
        out_shape=[jax.ShapeDtypeStruct((SUB + EXTRA, width), bf16)] * SIDE,
        compiler_params=pltpu.CompilerParams(vmem_limit_bytes=24 * 2**20),
        cost_estimate=pl.CostEstimate(
            flops=8 * SUB * student.shape[1],
            bytes_accessed=4 * SUB * student.shape[1],
            transcendentals=0,
        ),
    )(place, counts, student)


def turn_kernel(place, counts, p0, p1, p2, p3, turned, near):
    count = counts[0, place[0]]
    pieces = (p0, p1, p2, p3)
    rows = jnp.concatenate([p[:SUB, :] for p in pieces], axis=0)
    flat = rows.T
    width, depth = flat.shape
    turned[:width, :] = flat
    moments = jnp.concatenate([p[SUB : SUB + 6, :].astype(f32) for p in pieces], axis=0)
    rests = [
        jnp.concatenate([moments[3 * m + i : 3 * m + i + 1, depth:] for i in range(3)], axis=1)
        for m in range(8)
    ]
    turned[width:, :] = jnp.concatenate([moments[:, :depth]] + rests, axis=0).astype(bf16)
    mine = flat[:, :SUB].astype(f32)
    live = lax.broadcasted_iota(jnp.int32, mine.shape, 1) < count
    total = jnp.sum(jnp.where(live, mine, 0.0), axis=1, keepdims=True)
    near[...] = total / count.astype(f32)


def turn(place, counts, pieces):
    width = pieces[0].shape[1]
    return pl.pallas_call(
        turn_kernel,
        in_specs=[smem()] * 2 + [vmem()] * SIDE,
        out_specs=[vmem()] * 2,
        out_shape=[
            jax.ShapeDtypeStruct((width + 2 * EXTRA, SIDE * SUB), bf16),
            jax.ShapeDtypeStruct((width, 1), f32),
        ],
        compiler_params=pltpu.CompilerParams(vmem_limit_bytes=16 * 2**20),
        cost_estimate=pl.CostEstimate(
            flops=0, bytes_accessed=4 * SUB * SIDE * width, transcendentals=0
        ),
    )(place, counts, *pieces)


def shards_kernel(place, *refs):
    zs, own, out = refs[:SIDE], refs[SIDE : SIDE + 5], refs[-1]
    half = own[3].shape[1]
    depth = zs[0].shape[1]
    blocks = []
    for ref in zs:
        rows = ref[...].astype(f32)
        rests = [
            rows[24 + m : 25 + m, i * (depth // 3) : (i + 1) * (depth // 3)]
            for m in range(8)
            for i in range(3)
        ]
        rests = jnp.concatenate(rests, axis=0)
        blocks.append(jnp.concatenate([rows[:24], rests], axis=1))
    lane = lax.broadcasted_iota(jnp.int32, (1, half), 1)
    for r in range(SIDE):
        if r < 3:
            rows = own[r][...]
        else:
            rows = jnp.concatenate([own[3][...], own[4][...]], axis=1)
        out[r : r + 1, :] = from_parts(rows[0:3])
        out[SIDE + r : SIDE + r + 1, :] = from_parts(rows[3:6])
        sizes = own[r][...][6:7, :half].astype(f32)
        n = jnp.sum(jnp.where(lane < SIDE, sizes, 0.0), axis=1, keepdims=True)
        out[8 + r : 9 + r, :] = jnp.broadcast_to(n, (1, out.shape[1]))
        totals = [from_parts(b[6 * r : 6 * r + 3]) for b in blocks]
        squares = [from_parts(b[6 * r + 3 : 6 * r + 6]) for b in blocks]
        total = totals[0] + totals[1] + totals[2] + totals[3]
        mean = total / n
        square = jnp.zeros_like(total)
        for q, step in enumerate(COMING):
            here = lax.rem(place[0] + step, SIDE)
            size = jnp.sum(jnp.where(lane == here, sizes, 0.0), axis=1, keepdims=True)
            off = totals[q] / size - mean
            square = square + squares[q] + size * off * off
        out[12 + r : 13 + r, :] = total
        out[16 + r : 17 + r, :] = square
    out[20:24, :] = jnp.zeros((4, out.shape[1]), f32)


def shards(place, left, far_left, own):
    depth = left[0].shape[1]
    columns = own[0].shape[1]

    def low(value, rows):
        first = value.shape[0] // rows - 1
        return pl.BlockSpec((rows, value.shape[1]), lambda i, place: (first, 0))

    return pl.pallas_call(
        shards_kernel,
        grid_spec=pltpu.PrefetchScalarGridSpec(
            num_scalar_prefetch=1,
            grid=(1,),
            in_specs=[low(v, 2 * EXTRA) for v in left + [far_left]]
            + [low(v, EXTRA) for v in own],
            out_specs=pl.BlockSpec((24, columns), lambda i, place: (0, 0)),
        ),
        out_shape=jax.ShapeDtypeStruct((24, columns), f32),
        compiler_params=pltpu.CompilerParams(vmem_limit_bytes=8 * 2**20),
    )(place, *left, far_left, *own)


def settle_kernel(e0, e1, e2, e3, t_rows, s_left, work):
    every = (e0, e1, e2, e3)
    part = work.shape[1]

    def combine(totals, squares, counts):
        tokens = sum(jnp.sum(n, axis=0, keepdims=True) for n in counts)
        mean = sum(jnp.sum(t, axis=0, keepdims=True) for t in totals) / tokens
        offs = [t / n - mean for t, n in zip(totals, counts)]
        square = sum(
            jnp.sum(q + n * o * o, axis=0, keepdims=True)
            for q, n, o in zip(squares, counts, offs)
        )
        return offs, lax.rsqrt(square / tokens + epsilon), tokens

    offs, scale, _ = combine(
        [e[0:4, :] for e in every], [e[4:8, :] for e in every], [e[8:12, :] for e in every]
    )
    for j in range(SIDE):
        t_rows[j * SIDE : (j + 1) * SIDE, :] = offs[j] * scale
    t_rows[SIDE * SIDE : SIDE * SIDE + 1, :] = scale
    slots = [slice(i * part, (i + 1) * part) for i in (1, 2, 3, 0)]
    counts = [e[8:12, 0:part] for e in every]
    offs, scale, tokens = combine(
        [e[12:16, c] for e, c in zip(every, slots)],
        [e[16:20, c] for e, c in zip(every, slots)],
        counts,
    )
    scale = scale / jnp.sqrt(tokens)
    work[...] = jnp.zeros_like(work)
    for j in range(SIDE):
        work[j * SIDE : (j + 1) * SIDE, :] = offs[j] * scale * counts[j]
    work[SIDE * SIDE : SIDE * SIDE + 1, :] = scale
    s_left[...] = work[...].T


def settle(every):
    columns = every[0].shape[1]
    part = columns // SIDE
    S = jax.ShapeDtypeStruct
    return pl.pallas_call(
        settle_kernel,
        in_specs=[vmem()] * SIDE,
        out_specs=[vmem()] * 2,
        out_shape=[S((SIDE * SIDE + 1, columns), f32), S((part, 128), f32)],
        scratch_shapes=[pltpu.VMEM((128, part), f32)],
        compiler_params=pltpu.CompilerParams(vmem_limit_bytes=8 * 2**20),
    )(*every)


def pool_kernel(place, counts, before, teacher, behind, starts, weights, full, mix, share, pooled, lines, meta):
    window = SUB + 2 * HALO
    length = teacher.shape[0]
    j = pl.program_id(0)

    @pl.when(j == 0)
    def _():
        lines[...] = jnp.zeros_like(lines)
        lines[0:1, :] = (starts[...] - (place[2] * SIDE + place[3]) * length).astype(f32)
        lines[1 : 1 + BAND, :] = weights[...].astype(f32)
        meta[...] = lines[...].T.astype(jnp.int32)
        for r in range(SIDE):
            rows = slice(r * SUB, (r + 1) * SUB)
            spot = lax.broadcasted_iota(jnp.int32, (SUB, window), 1)
            local = meta[rows, 0:1] - (r * SUB - HALO)
            found = jnp.zeros((SUB, window), jnp.int32)
            whole = jnp.zeros((SUB, 1), jnp.int32)
            for k in range(BAND):
                weight = meta[rows, 1 + k : 2 + k]
                found = found + jnp.where(spot == local + k, weight, 0)
                whole = whole + weight
            mix[rows, :] = found.astype(f32).astype(bf16)
            share[rows, :] = jnp.broadcast_to(whole.astype(f32), (SUB, 128))

    total = jnp.zeros((1, teacher.shape[1]), f32)
    alive = jnp.int32(0)
    for r in range(SIDE):
        rows = slice(r * SUB, (r + 1) * SUB)
        low, high = r * SUB - HALO, (r + 1) * SUB + HALO
        parts = [teacher[max(low, 0) : min(high, length), :]]
        if low < 0:
            parts = [before[...]] + parts
        if high > length:
            parts = parts + [behind[...]]
        seen = jnp.concatenate(parts, axis=0) if len(parts) > 1 else parts[0]
        value = jnp.dot(mix[rows, :], seen, preferred_element_type=f32)
        value = value / share[rows, 0:1]
        pooled[rows, :] = value
        live = lax.broadcasted_iota(jnp.int32, value.shape, 0) < counts[0, r]
        total = total + jnp.sum(jnp.where(live, value, 0.0), axis=0, keepdims=True)
        alive = alive + counts[0, r]
    mean = total / alive.astype(f32)
    square = jnp.zeros_like(total)
    for r in range(SIDE):
        rows = slice(r * SUB, (r + 1) * SUB)
        value = pooled[rows, :]
        live = lax.broadcasted_iota(jnp.int32, value.shape, 0) < counts[0, r]
        dev = jnp.where(live, value - mean, 0.0)
        small = dev.astype(bf16)
        full[rows, :] = small
        square = square + jnp.sum(dev * dev, axis=0, keepdims=True)
    lane = lax.broadcasted_iota(jnp.int32, total.shape, 1)
    sizes = jnp.zeros(total.shape, jnp.int32)
    for r in range(SIDE):
        sizes = sizes + jnp.where(lane == r, counts[0, r], 0)
    rows = in_parts(total) + in_parts(square) + (sizes.astype(f32).astype(bf16),)
    rows = rows + (jnp.zeros((EXTRA - len(rows), total.shape[1]), bf16),)
    full[length:, :] = jnp.concatenate(rows, axis=0)


def pool(place, counts, before, teacher, behind, starts, weights):
    rows, columns = teacher.shape
    tile = 256
    return pl.pallas_call(
        pool_kernel,
        grid=(columns // tile,),
        in_specs=[
            smem(),
            smem(),
            pl.BlockSpec((HALO, tile), lambda j: (0, j)),
            pl.BlockSpec((rows, tile), lambda j: (0, j)),
            pl.BlockSpec((HALO, tile), lambda j: (0, j)),
            pl.BlockSpec(starts.shape, lambda j: (0, 0)),
            pl.BlockSpec(weights.shape, lambda j: (0, 0)),
        ],
        out_specs=pl.BlockSpec((rows + EXTRA, tile), lambda j: (0, j)),
        out_shape=jax.ShapeDtypeStruct((rows + EXTRA, columns), bf16),
        scratch_shapes=[
            pltpu.VMEM((rows, SUB + 2 * HALO), bf16),
            pltpu.VMEM((rows, 128), f32),
            pltpu.VMEM((rows, tile), f32),
            pltpu.VMEM((128, rows), f32),
            pltpu.VMEM((rows, 128), jnp.int32),
        ],
        compiler_params=pltpu.CompilerParams(vmem_limit_bytes=32 * 2**20),
        cost_estimate=pl.CostEstimate(
            flops=2 * rows * 256 * columns, bytes_accessed=6 * rows * columns, transcendentals=0
        ),
    )(place, counts, before, teacher, behind, starts, weights)


def with_ones(a):
    return jnp.concatenate([a, jnp.ones((16, a.shape[1]), bf16)], axis=0)


def less_mean(total, near):
    part = total.shape[0] - 16
    return total[:part] - near * total[part : part + 1]


def first_kernel(place, a0, a1, a2, b0, b1, b2, near, out):
    z = place[0]
    depth = a0.shape[1]
    fill = jnp.zeros((depth - 3 * SUB, b0.shape[1]), bf16)
    total = None
    for a, step in zip((a0, a1, a2), COMING):
        rows = pl.ds(pl.multiple_of(lax.rem(z + step, SIDE) * SUB, 16), SUB)
        b = jnp.concatenate([b0[rows, :], b1[rows, :], b2[rows, :], fill], axis=0)
        term = jnp.dot(with_ones(a[...]), b, preferred_element_type=f32)
        total = term if total is None else total + term
    out[...] = less_mean(total, near[...])


def first_product(place, left, right, near):
    depth = left[0].shape[1]
    rows = near.shape[0]
    part = rows // SIDE
    length, columns = right[0].shape
    near_depth = 640
    return pl.pallas_call(
        first_kernel,
        grid_spec=pltpu.PrefetchScalarGridSpec(
            num_scalar_prefetch=1,
            grid=(SIDE,),
            in_specs=[pl.BlockSpec((part, near_depth), lambda i, place: (i, 0))] * 3
            + [pl.BlockSpec((length, columns), lambda i, place: (0, 0))] * 3
            + [pl.BlockSpec((part, 1), lambda i, place: (i, 0))],
            out_specs=pl.BlockSpec((part, columns), lambda i, place: (i, 0)),
        ),
        out_shape=pltpu.HBM((rows, columns), f32),
        compiler_params=pltpu.CompilerParams(vmem_limit_bytes=40 * 2**20),
        cost_estimate=pl.CostEstimate(
            flops=2 * rows * 3 * near_depth * columns,
            bytes_accessed=6 * rows * depth + 6 * length * columns + 4 * rows * columns,
            transcendentals=0,
        ),
    )(place, *left, *right, near)


def last_sums(place, refs):
    z = place[0]
    tails, far_a, near = refs[:3], refs[3], refs[4]
    sides = (refs[5:10], refs[10:15])
    results = []
    lefts = [with_ones(t[...]) for t in tails]
    far_left = with_ones(far_a[...])
    for b0, b1, b2, far_b, done in sides:
        fill = jnp.zeros((tails[0].shape[1] - SUB, far_b.shape[1]), bf16)
        total = None
        for a, step in zip(lefts, COMING):
            rows = pl.ds(pl.multiple_of(lax.rem(z + step, SIDE) * SUB, 16), SUB)
            b = jnp.concatenate([fill, far_b[rows, :]], axis=0)
            term = jnp.dot(a, b, preferred_element_type=f32)
            total = term if total is None else total + term
        rows = pl.ds(pl.multiple_of(lax.rem(z + 2, SIDE) * SUB, 16), SUB)
        b = jnp.concatenate([b0[...], b1[...], b2[...], far_b[rows, :]], axis=0)
        total = total + jnp.dot(far_left, b, preferred_element_type=f32)
        results.append(less_mean(total, near[...]) + done[...])
    return results


def far_kernel(place, *refs):
    up, down = refs[15:]
    results = last_sums(place, refs)
    up[...] = results[0].astype(bf16)
    down[...] = results[1].astype(bf16)


def own_kernel(place, *refs):
    s_left, t_own, t_mate, base = refs[15:]
    half = base.shape[1] // 2
    every = SIDE * SIDE
    results = last_sums(place, refs)
    for i, t in enumerate((t_own, t_mate)):
        between = jnp.dot(
            s_left[:, :every],
            t[:every, :],
            preferred_element_type=f32,
            precision=lax.Precision.HIGHEST,
        )
        scaled = results[i] * s_left[:, every : every + 1] * t[every : every + 1, :]
        base[:, i * half : (i + 1) * half] = scaled + between


def close_kernel(place, *refs):
    from_back, from_next, up, down = refs[15:]
    i = pl.program_id(0)
    half = from_back.shape[1]
    results = last_sums(place, refs)

    @pl.when(i == 0)
    def _():
        up[:, :half] = (results[0] + from_back[...].astype(f32)).astype(bf16)
        up[:, half:] = results[1].astype(bf16)

    @pl.when(i == 1)
    def _():
        down[:, :half] = results[0].astype(bf16)
        down[:, half:] = (results[1] + from_next[...].astype(f32)).astype(bf16)


def last_product(place, k, kind, left, far_left, near, own, mate, arrived=()):
    depth = left[0].shape[1]
    part = near.shape[0] // SIDE
    half = own[0].shape[1] // 2
    kernel, start, far_start, steps = {
        "far": (far_kernel, 0, 0, 1),
        "own": (own_kernel, 1, 1, 1),
        "close": (close_kernel, 2, 0, 2),
    }[kind]
    one = lambda i, place: (0, 0)
    tail = 256
    side = (
        [pl.BlockSpec((SUB, half), lambda i, place: (lax.rem(place[0] + 2, SIDE), k))] * 3
        + [pl.BlockSpec((own[3].shape[0], half), one)]
        + [pl.BlockSpec((part, half), lambda i, place: (start + i, k))]
    )
    in_specs = (
        [pl.BlockSpec((part, tail), lambda i, place: (start + i, depth // tail - 1))] * 3
        + [pl.BlockSpec((part, depth), lambda i, place: (far_start + i, 0))]
        + [pl.BlockSpec((part, 1), lambda i, place: (start + i, 0))]
        + side * 2
        + (
            [pl.BlockSpec(arrived[0].shape, one)]
            + [pl.BlockSpec((a.shape[0], half), lambda i, place: (0, k)) for a in arrived[1:]]
            if kind == "own"
            else [pl.BlockSpec((part, half), one)] * len(arrived)
        )
    )
    S = jax.ShapeDtypeStruct
    shapes = {
        "far": [S((part, half), bf16)] * 2,
        "own": [S((part, 2 * half), f32)],
        "close": [S((part, 2 * half), bf16)] * 2,
    }[kind]
    return pl.pallas_call(
        kernel,
        grid_spec=pltpu.PrefetchScalarGridSpec(
            num_scalar_prefetch=1,
            grid=(steps,),
            in_specs=in_specs,
            out_specs=[pl.BlockSpec(s.shape, one) for s in shapes],
        ),
        out_shape=shapes,
        compiler_params=pltpu.CompilerParams(vmem_limit_bytes=40 * 2**20),
        cost_estimate=pl.CostEstimate(
            flops=2 * steps * part * 2 * depth * 2 * half,
            bytes_accessed=3 * steps * depth * part + 5 * depth * half + 8 * part * half,
            transcendentals=0,
        ),
    )(place, *left, far_left, near, *own, *mate, *arrived)


def final_kernel(place, base, first, second, s_left, t_own, t_mate, *rest):
    out = rest[-1]
    every = SIDE * SIDE
    last = slice(every, every + 1)
    t = jnp.where(pl.program_id(0) == 0, t_own[last, :], t_mate[last, :])
    inside = first[...].astype(f32) + second[...].astype(f32)
    out[...] = inside * s_left[:, last] * t + base[...]


def final(place, k, kept, first, second, s_left, t_own, t_mate, whole=None):
    part, columns = kept.shape
    half = columns // 2
    block = pl.BlockSpec((part, half), lambda i, place: (0, i))
    in_specs = (
        [block] * 3
        + [pl.BlockSpec(s_left.shape, lambda i, place: (0, 0))]
        + [pl.BlockSpec((t_own.shape[0], half), lambda i, place: (0, k))] * 2
    )
    more, aliases = (), {}
    if whole is not None:
        in_specs = in_specs + [pl.BlockSpec(memory_space=pl.ANY)]
        more, aliases = (whole,), {7: 0}
    return pl.pallas_call(
        final_kernel,
        grid_spec=pltpu.PrefetchScalarGridSpec(
            num_scalar_prefetch=1,
            grid=(2,),
            in_specs=in_specs,
            out_specs=pl.BlockSpec(
                (part, half), lambda i, place: (0, lax.rem(place[1] + i, 2) * 2 + k)
            ),
        ),
        out_shape=jax.ShapeDtypeStruct((part, 2 * columns), f32),
        input_output_aliases=aliases,
        compiler_params=pltpu.CompilerParams(vmem_limit_bytes=16 * 2**20),
        cost_estimate=pl.CostEstimate(
            flops=6 * part * columns, bytes_accessed=12 * part * columns, transcendentals=0
        ),
    )(place, kept, first, second, s_left, t_own, t_mate, *more)


def per_device(student, teacher, starts, weights, counts):
    y, x, z, c = (lax.axis_index(n) for n in ("y", "x", "row", "col"))
    place = jnp.stack([z, c, y, x]).astype(jnp.int32)
    rows = starts.shape[0]
    columns = teacher.shape[1]
    half = columns // 2
    width = student.shape[1] // SIDE

    up = [(i, (i + 1) % 16) for i in range(16)]
    down = [(j, i) for i, j in up]
    before = lax.ppermute(teacher[rows - HALO :], ("y", "x"), up)
    behind = lax.ppermute(teacher[:HALO], ("y", "x"), down)

    packed = pack(place, counts, student)
    packed, before, behind = lax.optimization_barrier((packed, before, behind))
    got = [packed[0], ring(packed[1], "x", 1), ring(packed[2], "x", -1), ring(packed[3], "x", 2)]
    standard = pool(place, counts, before, teacher, behind, starts[None], weights.T)
    got, standard = lax.optimization_barrier((got, standard))
    turned, mean = turn(place, counts, got)

    right, left = ring(standard, "x", 1), ring(standard, "x", -1)
    up, down = ring(turned, "row", 1), ring(turned, "row", -1)
    t_standard = swap(standard)
    right, left, up, down, t_standard = lax.optimization_barrier(
        (right, left, up, down, t_standard)
    )

    x_far = [ring(right[:, :half], "x", 1), ring(left[:, half:], "x", -1)]
    z_far = [ring(up[: width // 2], "row", 1), ring(down[width // 2 :], "row", -1)]
    t_right, t_left = swap(right), swap(left)
    own, mate = [standard, right, left], [t_standard, t_right, t_left]
    near_z = [turned, up, down]
    own_sum = first_product(place, near_z, own, mean)
    mate_sum = first_product(place, near_z, mate, mean)
    x_far, z_far, own_sum, mate_sum = lax.optimization_barrier((x_far, z_far, own_sum, mate_sum))

    t_x_far = [swap(f) for f in x_far]
    every = ring_all(shards(place, near_z, z_far[1], own + x_far), "y")
    sides, arrived = [], []
    for k in range(2):
        if k == 1:
            every, own_sum, mate_sum = lax.optimization_barrier((every, own_sum, mate_sum))
        sides.append((own + [x_far[k], own_sum], mate + [t_x_far[k], mate_sum]))
        o = last_product(place, k, "far", near_z, z_far[0], mean, *sides[k])
        arrived.append((ring(o[0], "y", 1), ring(o[1], "y", -1)))
    t_rows, s_left = settle(every)
    settled = (s_left, t_rows, swap(t_rows))
    passed = []
    for k in range(2):
        v = last_product(place, k, "close", near_z, z_far[1], mean, *sides[k], arrived[k])
        passed.append((ring(v[0], "y", 1), ring(v[1], "y", -1)))
    out = None
    for k in range(2):
        base = last_product(place, k, "own", near_z, z_far[0], mean, *sides[k], settled)[0]
        out = final(place, k, base, *passed[k], *settled, out)
    return out[None, None]


def solution(mesh):
    fine = Mesh(mesh.devices.reshape(SIDE, SIDE, SIDE, 2), ("y", "x", "row", "col"))
    seq = ("y", "x")
    placed = (
        P(seq + ("row",), "col"),
        P(seq, ("row", "col")),
        P(seq),
        P(seq, None),
        P(seq, None),
    )
    return jax.shard_map(
        per_device,
        mesh=fine,
        in_specs=placed,
        out_specs=P("col", seq, None, "row"),
        check_vma=False,
    )
```

```python
import jax
import jax.numpy as jnp
from jax import lax
from jax.experimental import pallas as pl
from jax.experimental.pallas import tpu as pltpu
from jax.sharding import Mesh
from jax.sharding import PartitionSpec as P

SUB = 192
BAND = 4
HALO = 16
EXTRA = 16
SIDE = 4
COMING = (0, SIDE - 1, 1, 2)
epsilon = 1e-05
f32 = jnp.float32
bf16 = jnp.bfloat16


def ring(value, axis, step):
    return lax.ppermute(value, axis, [(i, (i + step) % SIDE) for i in range(SIDE)])


def ring_all(value, axis):
    return [value, ring(value, axis, 1), ring(value, axis, -1), ring(value, axis, 2)]


def swap(value):
    return lax.ppermute(value, "col", [(0, 1), (1, 0)])


def after(value, *others):
    return lax.optimization_barrier((value, others))[0]


def in_parts(value):
    high = value.astype(bf16).astype(f32)
    rest = value - high
    middle = rest.astype(bf16).astype(f32)
    return high, middle, (rest - middle).astype(bf16).astype(f32)


def below(rows):
    empty = jnp.zeros((EXTRA - len(rows), rows[0].shape[1]), f32)
    return jnp.concatenate(rows + (empty,), axis=0).astype(bf16)


def from_parts(rows):
    return rows[0:1] + rows[1:2] + rows[2:3]


def smem():
    return pl.BlockSpec(memory_space=pltpu.SMEM)


def vmem():
    return pl.BlockSpec(memory_space=pltpu.VMEM)


def pack_kernel(place, counts, student, *outs):
    y, x, count = place[2], place[3], counts[0, place[0]]
    part = outs[0].shape[1] // SIDE
    for r, x_step in enumerate((0, 1, SIDE - 1, 2)):
        at = lax.rem(x + x_step, SIDE)
        for i, y_step in enumerate((2, 0, 1, SIDE - 1)):
            slot = lax.rem(y + y_step, SIDE) * SIDE + at
            first = pl.multiple_of(slot * part, 128)
            columns = slice(i * part, (i + 1) * part)
            block = student[:, pl.ds(first, part)]
            outs[r][:SUB, columns] = block
            value = block.astype(f32)
            live = lax.broadcasted_iota(jnp.int32, value.shape, 0) < count
            total = jnp.sum(jnp.where(live, value, 0.0), axis=0, keepdims=True)
            dev = jnp.where(live, value - total / count.astype(f32), 0.0)
            square = jnp.sum(dev * dev, axis=0, keepdims=True)
            outs[r][SUB:, columns] = below(in_parts(total) + in_parts(square))


def pack(place, counts, student):
    width = student.shape[1] // SIDE
    return pl.pallas_call(
        pack_kernel,
        in_specs=[smem(), smem(), vmem()],
        out_specs=[vmem()] * SIDE,
        out_shape=[jax.ShapeDtypeStruct((SUB + EXTRA, width), bf16)] * SIDE,
        compiler_params=pltpu.CompilerParams(vmem_limit_bytes=24 * 2**20),
        cost_estimate=pl.CostEstimate(
            flops=8 * SUB * student.shape[1],
            bytes_accessed=4 * SUB * student.shape[1],
            transcendentals=0,
        ),
    )(place, counts, student)


def turn_kernel(place, counts, p0, p1, p2, p3, turned, near):
    count = counts[0, place[0]]
    pieces = (p0, p1, p2, p3)
    rows = jnp.concatenate([p[:SUB, :] for p in pieces], axis=0)
    flat = rows.T
    width, depth = flat.shape
    turned[:width, :] = flat
    moments = jnp.concatenate([p[SUB:, :].astype(f32)[:6] for p in pieces], axis=0)
    rests = [
        jnp.concatenate([moments[3 * m + i : 3 * m + i + 1, depth:] for i in range(3)], axis=1)
        for m in range(8)
    ]
    turned[width:, :] = jnp.concatenate([moments[:, :depth]] + rests, axis=0).astype(bf16)
    mine = flat[:, :SUB].astype(f32)
    live = lax.broadcasted_iota(jnp.int32, mine.shape, 1) < count
    total = jnp.sum(jnp.where(live, mine, 0.0), axis=1, keepdims=True)
    near[...] = total / count.astype(f32)


def turn(place, counts, pieces):
    width = pieces[0].shape[1]
    return pl.pallas_call(
        turn_kernel,
        in_specs=[smem()] * 2 + [vmem()] * SIDE,
        out_specs=[vmem()] * 2,
        out_shape=[
            jax.ShapeDtypeStruct((width + 2 * EXTRA, SIDE * SUB), bf16),
            jax.ShapeDtypeStruct((width, 1), f32),
        ],
        compiler_params=pltpu.CompilerParams(vmem_limit_bytes=16 * 2**20),
        cost_estimate=pl.CostEstimate(
            flops=0, bytes_accessed=4 * SUB * SIDE * width, transcendentals=0
        ),
    )(place, counts, *pieces)


def shards_kernel(place, *refs):
    zs, own, out = refs[:SIDE], refs[SIDE : SIDE + 5], refs[-1]
    half = own[3].shape[1]
    depth = zs[0].shape[1]
    blocks = []
    for ref in zs:
        rows = ref[...].astype(f32)
        rests = [
            rows[24 + m : 25 + m, i * (depth // 3) : (i + 1) * (depth // 3)]
            for m in range(8)
            for i in range(3)
        ]
        rests = jnp.concatenate(rests, axis=0)
        blocks.append(jnp.concatenate([rows[:24], rests], axis=1))
    lane = lax.broadcasted_iota(jnp.int32, (1, half), 1)
    for r in range(SIDE):
        if r < 3:
            rows = own[r][...].astype(f32)
        else:
            rows = jnp.concatenate([own[3][...].astype(f32), own[4][...].astype(f32)], axis=1)
        out[r : r + 1, :] = from_parts(rows[0:3])
        out[SIDE + r : SIDE + r + 1, :] = from_parts(rows[3:6])
        sizes = rows[6:7, :half]
        n = jnp.sum(jnp.where(lane < SIDE, sizes, 0.0), axis=1, keepdims=True)
        out[8 + r : 9 + r, :] = jnp.broadcast_to(n, (1, out.shape[1]))
        totals = [from_parts(b[6 * r : 6 * r + 3]) for b in blocks]
        squares = [from_parts(b[6 * r + 3 : 6 * r + 6]) for b in blocks]
        total = totals[0] + totals[1] + totals[2] + totals[3]
        mean = total / n
        square = jnp.zeros_like(total)
        for q, step in enumerate(COMING):
            here = lax.rem(place[0] + step, SIDE)
            size = jnp.sum(jnp.where(lane == here, sizes, 0.0), axis=1, keepdims=True)
            off = totals[q] / size - mean
            square = square + squares[q] + size * off * off
        out[12 + r : 13 + r, :] = total
        out[16 + r : 17 + r, :] = square
    out[20:24, :] = jnp.zeros((4, out.shape[1]), f32)


def shards(place, left, far_left, own):
    depth = left[0].shape[1]
    columns = own[0].shape[1]

    def low(value, rows):
        first = value.shape[0] // rows - 1
        return pl.BlockSpec((rows, value.shape[1]), lambda i, place: (first, 0))

    return pl.pallas_call(
        shards_kernel,
        grid_spec=pltpu.PrefetchScalarGridSpec(
            num_scalar_prefetch=1,
            grid=(1,),
            in_specs=[low(v, 2 * EXTRA) for v in left + [far_left]]
            + [low(v, EXTRA) for v in own],
            out_specs=pl.BlockSpec((24, columns), lambda i, place: (0, 0)),
        ),
        out_shape=jax.ShapeDtypeStruct((24, columns), f32),
        compiler_params=pltpu.CompilerParams(vmem_limit_bytes=8 * 2**20),
    )(place, *left, far_left, *own)


def settle_kernel(e0, e1, e2, e3, t_rows, s_left, work):
    every = (e0, e1, e2, e3)
    part = work.shape[1]

    def combine(totals, squares, counts):
        tokens = sum(jnp.sum(n, axis=0, keepdims=True) for n in counts)
        mean = sum(jnp.sum(t, axis=0, keepdims=True) for t in totals) / tokens
        offs = [t / n - mean for t, n in zip(totals, counts)]
        square = sum(
            jnp.sum(q + n * o * o, axis=0, keepdims=True)
            for q, n, o in zip(squares, counts, offs)
        )
        return offs, lax.rsqrt(square / tokens + epsilon), tokens

    offs, scale, _ = combine(
        [e[0:4, :] for e in every], [e[4:8, :] for e in every], [e[8:12, :] for e in every]
    )
    for j in range(SIDE):
        t_rows[j * SIDE : (j + 1) * SIDE, :] = offs[j] * scale
    t_rows[SIDE * SIDE : SIDE * SIDE + 1, :] = scale
    slots = [slice(i * part, (i + 1) * part) for i in (1, 2, 3, 0)]
    counts = [e[8:12, 0:part] for e in every]
    offs, scale, tokens = combine(
        [e[12:16, c] for e, c in zip(every, slots)],
        [e[16:20, c] for e, c in zip(every, slots)],
        counts,
    )
    scale = scale / jnp.sqrt(tokens)
    work[...] = jnp.zeros_like(work)
    for j in range(SIDE):
        work[j * SIDE : (j + 1) * SIDE, :] = offs[j] * scale * counts[j]
    work[SIDE * SIDE : SIDE * SIDE + 1, :] = scale
    s_left[...] = work[...].T


def settle(every):
    columns = every[0].shape[1]
    part = columns // SIDE
    S = jax.ShapeDtypeStruct
    return pl.pallas_call(
        settle_kernel,
        in_specs=[vmem()] * SIDE,
        out_specs=[vmem()] * 2,
        out_shape=[S((SIDE * SIDE + 1, columns), f32), S((part, 128), f32)],
        scratch_shapes=[pltpu.VMEM((128, part), f32)],
        compiler_params=pltpu.CompilerParams(vmem_limit_bytes=8 * 2**20),
    )(*every)


def pool_kernel(place, counts, before, teacher, behind, starts, weights, full, mix, share, pooled, lines, meta):
    window = SUB + 2 * HALO
    length = teacher.shape[0]
    j = pl.program_id(0)

    @pl.when(j == 0)
    def _():
        lines[...] = jnp.zeros_like(lines)
        lines[0:1, :] = (starts[...] - (place[2] * SIDE + place[3]) * length).astype(f32)
        lines[1 : 1 + BAND, :] = weights[...].astype(f32)
        meta[...] = lines[...].T.astype(jnp.int32)
        for r in range(SIDE):
            rows = slice(r * SUB, (r + 1) * SUB)
            spot = lax.broadcasted_iota(jnp.int32, (SUB, window), 1)
            local = meta[rows, 0:1] - (r * SUB - HALO)
            found = jnp.zeros((SUB, window), jnp.int32)
            whole = jnp.zeros((SUB, 1), jnp.int32)
            for k in range(BAND):
                weight = meta[rows, 1 + k : 2 + k]
                found = found + jnp.where(spot == local + k, weight, 0)
                whole = whole + weight
            mix[rows, :] = found.astype(f32).astype(bf16)
            share[rows, :] = jnp.broadcast_to(whole.astype(f32), (SUB, 128))

    total = jnp.zeros((1, teacher.shape[1]), f32)
    alive = jnp.int32(0)
    for r in range(SIDE):
        rows = slice(r * SUB, (r + 1) * SUB)
        low, high = r * SUB - HALO, (r + 1) * SUB + HALO
        parts = [teacher[max(low, 0) : min(high, length), :]]
        if low < 0:
            parts = [before[...]] + parts
        if high > length:
            parts = parts + [behind[...]]
        seen = jnp.concatenate(parts, axis=0) if len(parts) > 1 else parts[0]
        value = jnp.dot(mix[rows, :], seen, preferred_element_type=f32)
        value = value / share[rows, 0:1]
        pooled[rows, :] = value
        live = lax.broadcasted_iota(jnp.int32, value.shape, 0) < counts[0, r]
        total = total + jnp.sum(jnp.where(live, value, 0.0), axis=0, keepdims=True)
        alive = alive + counts[0, r]
    mean = total / alive.astype(f32)
    square = jnp.zeros_like(total)
    for r in range(SIDE):
        rows = slice(r * SUB, (r + 1) * SUB)
        value = pooled[rows, :]
        live = lax.broadcasted_iota(jnp.int32, value.shape, 0) < counts[0, r]
        dev = jnp.where(live, value - mean, 0.0)
        small = dev.astype(bf16)
        full[rows, :] = small
        square = square + jnp.sum(dev * dev, axis=0, keepdims=True)
    lane = lax.broadcasted_iota(jnp.int32, total.shape, 1)
    sizes = jnp.zeros(total.shape, jnp.int32)
    for r in range(SIDE):
        sizes = sizes + jnp.where(lane == r, counts[0, r], 0)
    full[length:, :] = below(in_parts(total) + in_parts(square) + (sizes.astype(f32),))


def pool(place, counts, before, teacher, behind, starts, weights):
    rows, columns = teacher.shape
    tile = 256
    return pl.pallas_call(
        pool_kernel,
        grid=(columns // tile,),
        in_specs=[
            smem(),
            smem(),
            pl.BlockSpec((HALO, tile), lambda j: (0, j)),
            pl.BlockSpec((rows, tile), lambda j: (0, j)),
            pl.BlockSpec((HALO, tile), lambda j: (0, j)),
            pl.BlockSpec(starts.shape, lambda j: (0, 0)),
            pl.BlockSpec(weights.shape, lambda j: (0, 0)),
        ],
        out_specs=pl.BlockSpec((rows + EXTRA, tile), lambda j: (0, j)),
        out_shape=jax.ShapeDtypeStruct((rows + EXTRA, columns), bf16),
        scratch_shapes=[
            pltpu.VMEM((rows, SUB + 2 * HALO), bf16),
            pltpu.VMEM((rows, 128), f32),
            pltpu.VMEM((rows, tile), f32),
            pltpu.VMEM((128, rows), f32),
            pltpu.VMEM((rows, 128), jnp.int32),
        ],
        compiler_params=pltpu.CompilerParams(vmem_limit_bytes=32 * 2**20),
        cost_estimate=pl.CostEstimate(
            flops=2 * rows * 256 * columns, bytes_accessed=6 * rows * columns, transcendentals=0
        ),
    )(place, counts, before, teacher, behind, starts, weights)


def with_ones(a):
    return jnp.concatenate([a, jnp.ones((16, a.shape[1]), bf16)], axis=0)


def less_mean(total, near):
    part = total.shape[0] - 16
    return total[:part] - near * total[part : part + 1]


def first_kernel(place, a0, a1, a2, b0, b1, b2, near, out):
    z = place[0]
    depth = a0.shape[1]
    fill = jnp.zeros((depth - 3 * SUB, b0.shape[1]), bf16)
    total = None
    for a, step in zip((a0, a1, a2), COMING):
        rows = pl.ds(pl.multiple_of(lax.rem(z + step, SIDE) * SUB, 16), SUB)
        b = jnp.concatenate([b0[rows, :], b1[rows, :], b2[rows, :], fill], axis=0)
        term = jnp.dot(with_ones(a[...]), b, preferred_element_type=f32)
        total = term if total is None else total + term
    out[...] = less_mean(total, near[...])


def first_product(place, left, right, near):
    depth = left[0].shape[1]
    rows = near.shape[0]
    part = rows // SIDE
    length, columns = right[0].shape
    near_depth = 640
    return pl.pallas_call(
        first_kernel,
        grid_spec=pltpu.PrefetchScalarGridSpec(
            num_scalar_prefetch=1,
            grid=(SIDE,),
            in_specs=[pl.BlockSpec((part, near_depth), lambda i, place: (i, 0))] * 3
            + [pl.BlockSpec((length, columns), lambda i, place: (0, 0))] * 3
            + [pl.BlockSpec((part, 1), lambda i, place: (i, 0))],
            out_specs=pl.BlockSpec((part, columns), lambda i, place: (i, 0)),
        ),
        out_shape=pltpu.HBM((rows, columns), f32),
        compiler_params=pltpu.CompilerParams(vmem_limit_bytes=40 * 2**20),
        cost_estimate=pl.CostEstimate(
            flops=2 * rows * 3 * near_depth * columns,
            bytes_accessed=6 * rows * depth + 6 * length * columns + 4 * rows * columns,
            transcendentals=0,
        ),
    )(place, *left, *right, near)


def last_sums(place, refs):
    z = place[0]
    tails, far_a, near = refs[:3], refs[3], refs[4]
    sides = (refs[5:10], refs[10:15])
    results = []
    lefts = [with_ones(t[...]) for t in tails]
    far_left = with_ones(far_a[...])
    for b0, b1, b2, far_b, done in sides:
        fill = jnp.zeros((tails[0].shape[1] - SUB, far_b.shape[1]), bf16)
        total = None
        for a, step in zip(lefts, COMING):
            rows = pl.ds(pl.multiple_of(lax.rem(z + step, SIDE) * SUB, 16), SUB)
            b = jnp.concatenate([fill, far_b[rows, :]], axis=0)
            term = jnp.dot(a, b, preferred_element_type=f32)
            total = term if total is None else total + term
        rows = pl.ds(pl.multiple_of(lax.rem(z + 2, SIDE) * SUB, 16), SUB)
        b = jnp.concatenate([b0[...], b1[...], b2[...], far_b[rows, :]], axis=0)
        total = total + jnp.dot(far_left, b, preferred_element_type=f32)
        results.append(less_mean(total, near[...]) + done[...])
    return results


def far_kernel(place, *refs):
    up, down = refs[15:]
    results = last_sums(place, refs)
    up[...] = results[0].astype(bf16)
    down[...] = results[1].astype(bf16)


def own_kernel(place, *refs):
    s_left, t_own, t_mate, base = refs[15:]
    half = base.shape[1] // 2
    every = SIDE * SIDE
    results = last_sums(place, refs)
    for i, t in enumerate((t_own, t_mate)):
        between = jnp.dot(
            s_left[:, :every],
            t[:every, :],
            preferred_element_type=f32,
            precision=lax.Precision.HIGHEST,
        )
        scaled = results[i] * s_left[:, every : every + 1] * t[every : every + 1, :]
        base[:, i * half : (i + 1) * half] = scaled + between


def close_kernel(place, *refs):
    from_back, from_next, up, down = refs[15:]
    i = pl.program_id(0)
    half = from_back.shape[1]
    results = last_sums(place, refs)

    @pl.when(i == 0)
    def _():
        up[:, :half] = (results[0] + from_back[...].astype(f32)).astype(bf16)
        up[:, half:] = results[1].astype(bf16)

    @pl.when(i == 1)
    def _():
        down[:, :half] = results[0].astype(bf16)
        down[:, half:] = (results[1] + from_next[...].astype(f32)).astype(bf16)


def last_product(place, k, kind, left, far_left, near, own, mate, arrived=()):
    depth = left[0].shape[1]
    part = near.shape[0] // SIDE
    half = own[0].shape[1] // 2
    kernel, start, far_start, steps = {
        "far": (far_kernel, 0, 0, 1),
        "own": (own_kernel, 1, 1, 1),
        "close": (close_kernel, 2, 0, 2),
    }[kind]
    one = lambda i, place: (0, 0)
    tail = 256
    side = (
        [pl.BlockSpec((SUB, half), lambda i, place: (lax.rem(place[0] + 2, SIDE), k))] * 3
        + [pl.BlockSpec((own[3].shape[0], half), one)]
        + [pl.BlockSpec((part, half), lambda i, place: (start + i, k))]
    )
    in_specs = (
        [pl.BlockSpec((part, tail), lambda i, place: (start + i, depth // tail - 1))] * 3
        + [pl.BlockSpec((part, depth), lambda i, place: (far_start + i, 0))]
        + [pl.BlockSpec((part, 1), lambda i, place: (start + i, 0))]
        + side * 2
        + (
            [pl.BlockSpec(arrived[0].shape, one)]
            + [pl.BlockSpec((a.shape[0], half), lambda i, place: (0, k)) for a in arrived[1:]]
            if kind == "own"
            else [pl.BlockSpec((part, half), one)] * len(arrived)
        )
    )
    S = jax.ShapeDtypeStruct
    shapes = {
        "far": [S((part, half), bf16)] * 2,
        "own": [S((part, 2 * half), f32)],
        "close": [S((part, 2 * half), bf16)] * 2,
    }[kind]
    return pl.pallas_call(
        kernel,
        grid_spec=pltpu.PrefetchScalarGridSpec(
            num_scalar_prefetch=1,
            grid=(steps,),
            in_specs=in_specs,
            out_specs=[pl.BlockSpec(s.shape, one) for s in shapes],
        ),
        out_shape=shapes,
        compiler_params=pltpu.CompilerParams(vmem_limit_bytes=40 * 2**20),
        cost_estimate=pl.CostEstimate(
            flops=2 * steps * part * 2 * depth * 2 * half,
            bytes_accessed=3 * steps * depth * part + 5 * depth * half + 8 * part * half,
            transcendentals=0,
        ),
    )(place, *left, far_left, near, *own, *mate, *arrived)


def final_kernel(place, base, first, second, s_left, t_own, t_mate, *rest):
    out = rest[-1]
    every = SIDE * SIDE
    last = slice(every, every + 1)
    t = jnp.where(pl.program_id(0) == 0, t_own[last, :], t_mate[last, :])
    inside = first[...].astype(f32) + second[...].astype(f32)
    out[...] = inside * s_left[:, last] * t + base[...]


def final(place, k, kept, first, second, s_left, t_own, t_mate, whole=None):
    part, columns = kept.shape
    half = columns // 2
    block = pl.BlockSpec((part, half), lambda i, place: (0, i))
    in_specs = (
        [block] * 3
        + [pl.BlockSpec(s_left.shape, lambda i, place: (0, 0))]
        + [pl.BlockSpec((t_own.shape[0], half), lambda i, place: (0, k))] * 2
    )
    more, aliases = (), {}
    if whole is not None:
        in_specs = in_specs + [pl.BlockSpec(memory_space=pl.ANY)]
        more, aliases = (whole,), {7: 0}
    return pl.pallas_call(
        final_kernel,
        grid_spec=pltpu.PrefetchScalarGridSpec(
            num_scalar_prefetch=1,
            grid=(2,),
            in_specs=in_specs,
            out_specs=pl.BlockSpec(
                (part, half), lambda i, place: (0, lax.rem(place[1] + i, 2) * 2 + k)
            ),
        ),
        out_shape=jax.ShapeDtypeStruct((part, 2 * columns), f32),
        input_output_aliases=aliases,
        compiler_params=pltpu.CompilerParams(vmem_limit_bytes=16 * 2**20),
        cost_estimate=pl.CostEstimate(
            flops=6 * part * columns, bytes_accessed=12 * part * columns, transcendentals=0
        ),
    )(place, kept, first, second, s_left, t_own, t_mate, *more)


def per_device(student, teacher, starts, weights, counts):
    y, x, z, c = (lax.axis_index(n) for n in ("y", "x", "row", "col"))
    place = jnp.stack([z, c, y, x]).astype(jnp.int32)
    rows = starts.shape[0]
    columns = teacher.shape[1]
    half = columns // 2
    width = student.shape[1] // SIDE

    up = [(i, (i + 1) % 16) for i in range(16)]
    down = [(j, i) for i, j in up]
    before = lax.ppermute(teacher[rows - HALO :], ("y", "x"), up)
    behind = lax.ppermute(teacher[:HALO], ("y", "x"), down)

    packed = pack(place, counts, student)
    packed, before, behind = lax.optimization_barrier((packed, before, behind))
    got = [packed[0], ring(packed[1], "x", 1), ring(packed[2], "x", -1), ring(packed[3], "x", 2)]
    standard = pool(place, counts, before, teacher, behind, starts[None], weights.T)
    got, standard = lax.optimization_barrier((got, standard))
    turned, mean = turn(place, counts, got)

    right, left = ring(standard, "x", 1), ring(standard, "x", -1)
    up, down = ring(turned, "row", 1), ring(turned, "row", -1)
    t_standard = swap(standard)
    right, left, up, down, t_standard = lax.optimization_barrier(
        (right, left, up, down, t_standard)
    )

    x_far = [ring(right[:, :half], "x", 1), ring(left[:, half:], "x", -1)]
    z_far = [ring(up[: width // 2], "row", 1), ring(down[width // 2 :], "row", -1)]
    t_right, t_left = swap(right), swap(left)
    own, mate = [standard, right, left], [t_standard, t_right, t_left]
    near_z = [turned, up, down]
    own_sum = first_product(place, near_z, own, mean)
    mate_sum = first_product(place, near_z, mate, mean)
    x_far, z_far, own_sum, mate_sum = lax.optimization_barrier((x_far, z_far, own_sum, mate_sum))

    t_x_far = [swap(f) for f in x_far]
    every = ring_all(shards(place, near_z, z_far[1], own + x_far), "y")
    sides, arrived = [], []
    for k in range(2):
        if k == 1:
            every, own_sum, mate_sum = lax.optimization_barrier((every, own_sum, mate_sum))
        sides.append((own + [x_far[k], own_sum], mate + [t_x_far[k], mate_sum]))
        o = last_product(place, k, "far", near_z, z_far[0], mean, *sides[k])
        arrived.append((ring(o[0], "y", 1), ring(o[1], "y", -1)))
    t_rows, s_left = settle(every)
    settled = (s_left, t_rows, swap(t_rows))
    passed = []
    for k in range(2):
        v = last_product(place, k, "close", near_z, z_far[1], mean, *sides[k], arrived[k])
        passed.append((ring(v[0], "y", 1), ring(v[1], "y", -1)))
    out = None
    for k in range(2):
        base = last_product(place, k, "own", near_z, z_far[0], mean, *sides[k], settled)[0]
        out = final(place, k, base, *passed[k], *settled, out)
    return out[None, None]


def solution(mesh):
    fine = Mesh(mesh.devices.reshape(SIDE, SIDE, SIDE, 2), ("y", "x", "row", "col"))
    seq = ("y", "x")
    placed = (
        P(seq + ("row",), "col"),
        P(seq, ("row", "col")),
        P(seq),
        P(seq, None),
        P(seq, None),
    )
    return jax.shard_map(
        per_device,
        mesh=fine,
        in_specs=placed,
        out_specs=P("col", seq, None, "row"),
        check_vma=False,
    )
```

```python
import jax
import jax.numpy as jnp
from jax import lax
from jax.experimental import pallas as pl
from jax.experimental.pallas import tpu as pltpu
from jax.sharding import Mesh
from jax.sharding import PartitionSpec as P

SUB = 192
BAND = 4
HALO = 16
EXTRA = 16
SIDE = 4
COMING = (0, SIDE - 1, 1, 2)
epsilon = 1e-05
f32 = jnp.float32
bf16 = jnp.bfloat16


def ring(value, axis, step):
    return lax.ppermute(value, axis, [(i, (i + step) % SIDE) for i in range(SIDE)])


def ring_all(value, axis):
    return [value, ring(value, axis, 1), ring(value, axis, -1), ring(value, axis, 2)]


def swap(value):
    return lax.ppermute(value, "col", [(0, 1), (1, 0)])


def after(value, *others):
    return lax.optimization_barrier((value, others))[0]


def in_parts(value):
    high = value.astype(bf16).astype(f32)
    rest = value - high
    middle = rest.astype(bf16).astype(f32)
    return high, middle, (rest - middle).astype(bf16).astype(f32)


def below(rows):
    empty = jnp.zeros((EXTRA - len(rows), rows[0].shape[1]), f32)
    return jnp.concatenate(rows + (empty,), axis=0).astype(bf16)


def from_parts(rows):
    return rows[0:1] + rows[1:2] + rows[2:3]


def smem():
    return pl.BlockSpec(memory_space=pltpu.SMEM)


def vmem():
    return pl.BlockSpec(memory_space=pltpu.VMEM)


def pack_kernel(place, counts, student, *outs):
    y, x, count = place[2], place[3], counts[0, place[0]]
    part = outs[0].shape[1] // SIDE
    for r, x_step in enumerate((0, 1, SIDE - 1, 2)):
        at = lax.rem(x + x_step, SIDE)
        for i, y_step in enumerate((2, 0, 1, SIDE - 1)):
            slot = lax.rem(y + y_step, SIDE) * SIDE + at
            first = pl.multiple_of(slot * part, 128)
            columns = slice(i * part, (i + 1) * part)
            block = student[:, pl.ds(first, part)]
            outs[r][:SUB, columns] = block
            value = block.astype(f32)
            live = lax.broadcasted_iota(jnp.int32, value.shape, 0) < count
            total = jnp.sum(jnp.where(live, value, 0.0), axis=0, keepdims=True)
            dev = jnp.where(live, value - total / count.astype(f32), 0.0)
            square = jnp.sum(dev * dev, axis=0, keepdims=True)
            outs[r][SUB:, columns] = below(in_parts(total) + in_parts(square))


def pack(place, counts, student):
    width = student.shape[1] // SIDE
    return pl.pallas_call(
        pack_kernel,
        in_specs=[smem(), smem(), vmem()],
        out_specs=[vmem()] * SIDE,
        out_shape=[jax.ShapeDtypeStruct((SUB + EXTRA, width), bf16)] * SIDE,
        compiler_params=pltpu.CompilerParams(vmem_limit_bytes=24 * 2**20),
        cost_estimate=pl.CostEstimate(
            flops=8 * SUB * student.shape[1],
            bytes_accessed=4 * SUB * student.shape[1],
            transcendentals=0,
        ),
    )(place, counts, student)


def turn_kernel(place, counts, p0, p1, p2, p3, turned, near):
    count = counts[0, place[0]]
    pieces = (p0, p1, p2, p3)
    rows = jnp.concatenate([p[:SUB, :] for p in pieces], axis=0)
    flat = rows.T
    width, depth = flat.shape
    turned[:width, :] = flat
    moments = jnp.concatenate([p[SUB:, :].astype(f32)[:6] for p in pieces], axis=0)
    rests = [
        jnp.concatenate([moments[3 * m + i : 3 * m + i + 1, depth:] for i in range(3)], axis=1)
        for m in range(8)
    ]
    turned[width:, :] = jnp.concatenate([moments[:, :depth]] + rests, axis=0).astype(bf16)
    mine = flat[:, :SUB].astype(f32)
    live = lax.broadcasted_iota(jnp.int32, mine.shape, 1) < count
    total = jnp.sum(jnp.where(live, mine, 0.0), axis=1, keepdims=True)
    near[...] = total / count.astype(f32)


def turn(place, counts, pieces):
    width = pieces[0].shape[1]
    return pl.pallas_call(
        turn_kernel,
        in_specs=[smem()] * 2 + [vmem()] * SIDE,
        out_specs=[vmem()] * 2,
        out_shape=[
            jax.ShapeDtypeStruct((width + 2 * EXTRA, SIDE * SUB), bf16),
            jax.ShapeDtypeStruct((width, 1), f32),
        ],
        compiler_params=pltpu.CompilerParams(vmem_limit_bytes=16 * 2**20),
        cost_estimate=pl.CostEstimate(
            flops=0, bytes_accessed=4 * SUB * SIDE * width, transcendentals=0
        ),
    )(place, counts, *pieces)


def shards_kernel(place, *refs):
    zs, own, out = refs[:SIDE], refs[SIDE : SIDE + 5], refs[-1]
    half = own[3].shape[1]
    depth = zs[0].shape[1]
    blocks = []
    for ref in zs:
        rows = ref[...].astype(f32)
        rests = [
            rows[24 + m : 25 + m, i * (depth // 3) : (i + 1) * (depth // 3)]
            for m in range(8)
            for i in range(3)
        ]
        rests = jnp.concatenate(rests, axis=0)
        blocks.append(jnp.concatenate([rows[:24], rests], axis=1))
    lane = lax.broadcasted_iota(jnp.int32, (1, half), 1)
    for r in range(SIDE):
        if r < 3:
            rows = own[r][...].astype(f32)
        else:
            rows = jnp.concatenate([own[3][...].astype(f32), own[4][...].astype(f32)], axis=1)
        out[r : r + 1, :] = from_parts(rows[0:3])
        out[SIDE + r : SIDE + r + 1, :] = from_parts(rows[3:6])
        sizes = rows[6:7, :half]
        n = jnp.sum(jnp.where(lane < SIDE, sizes, 0.0), axis=1, keepdims=True)
        out[8 + r : 9 + r, :] = jnp.broadcast_to(n, (1, out.shape[1]))
        totals = [from_parts(b[6 * r : 6 * r + 3]) for b in blocks]
        squares = [from_parts(b[6 * r + 3 : 6 * r + 6]) for b in blocks]
        total = totals[0] + totals[1] + totals[2] + totals[3]
        mean = total / n
        square = jnp.zeros_like(total)
        for q, step in enumerate(COMING):
            here = lax.rem(place[0] + step, SIDE)
            size = jnp.sum(jnp.where(lane == here, sizes, 0.0), axis=1, keepdims=True)
            off = totals[q] / size - mean
            square = square + squares[q] + size * off * off
        out[12 + r : 13 + r, :] = total
        out[16 + r : 17 + r, :] = square
    out[20:24, :] = jnp.zeros((4, out.shape[1]), f32)


def shards(place, left, far_left, own):
    depth = left[0].shape[1]
    columns = own[0].shape[1]

    def low(value, rows):
        first = value.shape[0] // rows - 1
        return pl.BlockSpec((rows, value.shape[1]), lambda i, place: (first, 0))

    return pl.pallas_call(
        shards_kernel,
        grid_spec=pltpu.PrefetchScalarGridSpec(
            num_scalar_prefetch=1,
            grid=(1,),
            in_specs=[low(v, 2 * EXTRA) for v in left + [far_left]]
            + [low(v, EXTRA) for v in own],
            out_specs=pl.BlockSpec((24, columns), lambda i, place: (0, 0)),
        ),
        out_shape=jax.ShapeDtypeStruct((24, columns), f32),
        compiler_params=pltpu.CompilerParams(vmem_limit_bytes=8 * 2**20),
    )(place, *left, far_left, *own)


def settle_kernel(e0, e1, e2, e3, t_rows, s_left, work):
    every = (e0, e1, e2, e3)
    part = work.shape[1]

    def combine(totals, squares, counts):
        tokens = sum(jnp.sum(n, axis=0, keepdims=True) for n in counts)
        mean = sum(jnp.sum(t, axis=0, keepdims=True) for t in totals) / tokens
        offs = [t / n - mean for t, n in zip(totals, counts)]
        square = sum(
            jnp.sum(q + n * o * o, axis=0, keepdims=True)
            for q, n, o in zip(squares, counts, offs)
        )
        return offs, lax.rsqrt(square / tokens + epsilon), tokens

    offs, scale, _ = combine(
        [e[0:4, :] for e in every], [e[4:8, :] for e in every], [e[8:12, :] for e in every]
    )
    for j in range(SIDE):
        t_rows[j * SIDE : (j + 1) * SIDE, :] = offs[j] * scale
    t_rows[SIDE * SIDE : SIDE * SIDE + 1, :] = scale
    slots = [slice(i * part, (i + 1) * part) for i in (1, 2, 3, 0)]
    counts = [e[8:12, 0:part] for e in every]
    offs, scale, tokens = combine(
        [e[12:16, c] for e, c in zip(every, slots)],
        [e[16:20, c] for e, c in zip(every, slots)],
        counts,
    )
    scale = scale / jnp.sqrt(tokens)
    work[...] = jnp.zeros_like(work)
    for j in range(SIDE):
        work[j * SIDE : (j + 1) * SIDE, :] = offs[j] * scale * counts[j]
    work[SIDE * SIDE : SIDE * SIDE + 1, :] = scale
    s_left[...] = work[...].T


def settle(every):
    columns = every[0].shape[1]
    part = columns // SIDE
    S = jax.ShapeDtypeStruct
    return pl.pallas_call(
        settle_kernel,
        in_specs=[vmem()] * SIDE,
        out_specs=[vmem()] * 2,
        out_shape=[S((SIDE * SIDE + 1, columns), f32), S((part, 128), f32)],
        scratch_shapes=[pltpu.VMEM((128, part), f32)],
        compiler_params=pltpu.CompilerParams(vmem_limit_bytes=8 * 2**20),
    )(*every)


def pool_kernel(place, counts, before, teacher, behind, starts, weights, full, mix, share, pooled, lines, meta):
    window = SUB + 2 * HALO
    length = teacher.shape[0]
    j = pl.program_id(0)

    @pl.when(j == 0)
    def _():
        lines[...] = jnp.zeros_like(lines)
        lines[0:1, :] = (starts[...] - (place[2] * SIDE + place[3]) * length).astype(f32)
        lines[1 : 1 + BAND, :] = weights[...].astype(f32)
        meta[...] = lines[...].T.astype(jnp.int32)
        for r in range(SIDE):
            rows = slice(r * SUB, (r + 1) * SUB)
            spot = lax.broadcasted_iota(jnp.int32, (SUB, window), 1)
            local = meta[rows, 0:1] - (r * SUB - HALO)
            found = jnp.zeros((SUB, window), jnp.int32)
            whole = jnp.zeros((SUB, 1), jnp.int32)
            for k in range(BAND):
                weight = meta[rows, 1 + k : 2 + k]
                found = found + jnp.where(spot == local + k, weight, 0)
                whole = whole + weight
            mix[rows, :] = found.astype(f32).astype(bf16)
            share[rows, :] = jnp.broadcast_to(whole.astype(f32), (SUB, 128))

    total = jnp.zeros((1, teacher.shape[1]), f32)
    alive = jnp.int32(0)
    for r in range(SIDE):
        rows = slice(r * SUB, (r + 1) * SUB)
        low, high = r * SUB - HALO, (r + 1) * SUB + HALO
        parts = [teacher[max(low, 0) : min(high, length), :]]
        if low < 0:
            parts = [before[...]] + parts
        if high > length:
            parts = parts + [behind[...]]
        seen = jnp.concatenate(parts, axis=0) if len(parts) > 1 else parts[0]
        value = jnp.dot(mix[rows, :], seen, preferred_element_type=f32)
        value = value / share[rows, 0:1]
        pooled[rows, :] = value
        live = lax.broadcasted_iota(jnp.int32, value.shape, 0) < counts[0, r]
        total = total + jnp.sum(jnp.where(live, value, 0.0), axis=0, keepdims=True)
        alive = alive + counts[0, r]
    mean = total / alive.astype(f32)
    square = jnp.zeros_like(total)
    for r in range(SIDE):
        rows = slice(r * SUB, (r + 1) * SUB)
        value = pooled[rows, :]
        live = lax.broadcasted_iota(jnp.int32, value.shape, 0) < counts[0, r]
        dev = jnp.where(live, value - mean, 0.0)
        small = dev.astype(bf16)
        full[rows, :] = small
        square = square + jnp.sum(dev * dev, axis=0, keepdims=True)
    lane = lax.broadcasted_iota(jnp.int32, total.shape, 1)
    sizes = jnp.zeros(total.shape, jnp.int32)
    for r in range(SIDE):
        sizes = sizes + jnp.where(lane == r, counts[0, r], 0)
    full[length:, :] = below(in_parts(total) + in_parts(square) + (sizes.astype(f32),))


def pool(place, counts, before, teacher, behind, starts, weights):
    rows, columns = teacher.shape
    tile = 256
    return pl.pallas_call(
        pool_kernel,
        grid=(columns // tile,),
        in_specs=[
            smem(),
            smem(),
            pl.BlockSpec((HALO, tile), lambda j: (0, j)),
            pl.BlockSpec((rows, tile), lambda j: (0, j)),
            pl.BlockSpec((HALO, tile), lambda j: (0, j)),
            pl.BlockSpec(starts.shape, lambda j: (0, 0)),
            pl.BlockSpec(weights.shape, lambda j: (0, 0)),
        ],
        out_specs=pl.BlockSpec((rows + EXTRA, tile), lambda j: (0, j)),
        out_shape=jax.ShapeDtypeStruct((rows + EXTRA, columns), bf16),
        scratch_shapes=[
            pltpu.VMEM((rows, SUB + 2 * HALO), bf16),
            pltpu.VMEM((rows, 128), f32),
            pltpu.VMEM((rows, tile), f32),
            pltpu.VMEM((128, rows), f32),
            pltpu.VMEM((rows, 128), jnp.int32),
        ],
        compiler_params=pltpu.CompilerParams(vmem_limit_bytes=32 * 2**20),
        cost_estimate=pl.CostEstimate(
            flops=2 * rows * 256 * columns, bytes_accessed=6 * rows * columns, transcendentals=0
        ),
    )(place, counts, before, teacher, behind, starts, weights)


def with_ones(a):
    return jnp.concatenate([a, jnp.ones((16, a.shape[1]), bf16)], axis=0)


def less_mean(total, near):
    part = total.shape[0] - 16
    return total[:part] - near * total[part : part + 1]


def first_kernel(place, a0, a1, a2, b0, b1, b2, near, out):
    z = place[0]
    depth = a0.shape[1]
    fill = jnp.zeros((depth - 3 * SUB, b0.shape[1]), bf16)
    total = None
    for a, step in zip((a0, a1, a2), COMING):
        rows = pl.ds(pl.multiple_of(lax.rem(z + step, SIDE) * SUB, 16), SUB)
        b = jnp.concatenate([b0[rows, :], b1[rows, :], b2[rows, :], fill], axis=0)
        term = jnp.dot(with_ones(a[...]), b, preferred_element_type=f32)
        total = term if total is None else total + term
    out[...] = less_mean(total, near[...])


def first_product(place, left, right, near):
    depth = left[0].shape[1]
    rows = near.shape[0]
    part = rows // SIDE
    length, columns = right[0].shape
    near_depth = 640
    return pl.pallas_call(
        first_kernel,
        grid_spec=pltpu.PrefetchScalarGridSpec(
            num_scalar_prefetch=1,
            grid=(SIDE,),
            in_specs=[pl.BlockSpec((part, near_depth), lambda i, place: (i, 0))] * 3
            + [pl.BlockSpec((length, columns), lambda i, place: (0, 0))] * 3
            + [pl.BlockSpec((part, 1), lambda i, place: (i, 0))],
            out_specs=pl.BlockSpec((part, columns), lambda i, place: (i, 0)),
        ),
        out_shape=pltpu.HBM((rows, columns), f32),
        compiler_params=pltpu.CompilerParams(vmem_limit_bytes=26 * 2**20),
        cost_estimate=pl.CostEstimate(
            flops=2 * rows * 3 * near_depth * columns,
            bytes_accessed=6 * rows * depth + 6 * length * columns + 4 * rows * columns,
            transcendentals=0,
        ),
    )(place, *left, *right, near)


def last_sums(place, refs):
    z = place[0]
    tails, far_a, near = refs[:3], refs[3], refs[4]
    sides = (refs[5:10], refs[10:15])
    results = []
    lefts = [with_ones(t[...]) for t in tails]
    far_left = with_ones(far_a[...])
    for b0, b1, b2, far_b, done in sides:
        fill = jnp.zeros((tails[0].shape[1] - SUB, far_b.shape[1]), bf16)
        total = None
        for a, step in zip(lefts, COMING):
            rows = pl.ds(pl.multiple_of(lax.rem(z + step, SIDE) * SUB, 16), SUB)
            b = jnp.concatenate([fill, far_b[rows, :]], axis=0)
            term = jnp.dot(a, b, preferred_element_type=f32)
            total = term if total is None else total + term
        rows = pl.ds(pl.multiple_of(lax.rem(z + 2, SIDE) * SUB, 16), SUB)
        b = jnp.concatenate([b0[...], b1[...], b2[...], far_b[rows, :]], axis=0)
        total = total + jnp.dot(far_left, b, preferred_element_type=f32)
        results.append(less_mean(total, near[...]) + done[...])
    return results


def far_kernel(place, *refs):
    up, down = refs[15:]
    results = last_sums(place, refs)
    up[...] = results[0].astype(bf16)
    down[...] = results[1].astype(bf16)


def own_kernel(place, *refs):
    s_left, t_own, t_mate, base = refs[15:]
    half = base.shape[1] // 2
    every = SIDE * SIDE
    results = last_sums(place, refs)
    for i, t in enumerate((t_own, t_mate)):
        between = jnp.dot(
            s_left[:, :every],
            t[:every, :],
            preferred_element_type=f32,
            precision=lax.Precision.HIGHEST,
        )
        scaled = results[i] * s_left[:, every : every + 1] * t[every : every + 1, :]
        base[:, i * half : (i + 1) * half] = scaled + between


def close_kernel(place, *refs):
    from_back, from_next, up, down = refs[15:]
    i = pl.program_id(0)
    half = from_back.shape[1]
    results = last_sums(place, refs)

    @pl.when(i == 0)
    def _():
        up[:, :half] = (results[0] + from_back[...].astype(f32)).astype(bf16)
        up[:, half:] = results[1].astype(bf16)

    @pl.when(i == 1)
    def _():
        down[:, :half] = results[0].astype(bf16)
        down[:, half:] = (results[1] + from_next[...].astype(f32)).astype(bf16)


def last_product(place, k, kind, left, far_left, near, own, mate, arrived=()):
    depth = left[0].shape[1]
    part = near.shape[0] // SIDE
    half = own[0].shape[1] // 2
    kernel, start, far_start, steps = {
        "far": (far_kernel, 0, 0, 1),
        "own": (own_kernel, 1, 1, 1),
        "close": (close_kernel, 2, 0, 2),
    }[kind]
    one = lambda i, place: (0, 0)
    tail = 256
    side = (
        [pl.BlockSpec((SUB, half), lambda i, place: (lax.rem(place[0] + 2, SIDE), k))] * 3
        + [pl.BlockSpec((own[3].shape[0], half), one)]
        + [pl.BlockSpec((part, half), lambda i, place: (start + i, k))]
    )
    in_specs = (
        [pl.BlockSpec((part, tail), lambda i, place: (start + i, depth // tail - 1))] * 3
        + [pl.BlockSpec((part, depth), lambda i, place: (far_start + i, 0))]
        + [pl.BlockSpec((part, 1), lambda i, place: (start + i, 0))]
        + side * 2
        + (
            [pl.BlockSpec(arrived[0].shape, one)]
            + [pl.BlockSpec((a.shape[0], half), lambda i, place: (0, k)) for a in arrived[1:]]
            if kind == "own"
            else [pl.BlockSpec((part, half), one)] * len(arrived)
        )
    )
    S = jax.ShapeDtypeStruct
    shapes = {
        "far": [S((part, half), bf16)] * 2,
        "own": [S((part, 2 * half), f32)],
        "close": [S((part, 2 * half), bf16)] * 2,
    }[kind]
    return pl.pallas_call(
        kernel,
        grid_spec=pltpu.PrefetchScalarGridSpec(
            num_scalar_prefetch=1,
            grid=(steps,),
            in_specs=in_specs,
            out_specs=[pl.BlockSpec(s.shape, one) for s in shapes],
        ),
        out_shape=shapes,
        compiler_params=pltpu.CompilerParams(vmem_limit_bytes=26 * 2**20),
        cost_estimate=pl.CostEstimate(
            flops=2 * steps * part * 2 * depth * 2 * half,
            bytes_accessed=3 * steps * depth * part + 5 * depth * half + 8 * part * half,
            transcendentals=0,
        ),
    )(place, *left, far_left, near, *own, *mate, *arrived)


def final_kernel(place, base, first, second, s_left, t_own, t_mate, *rest):
    out = rest[-1]
    every = SIDE * SIDE
    last = slice(every, every + 1)
    t = jnp.where(pl.program_id(0) == 0, t_own[last, :], t_mate[last, :])
    inside = first[...].astype(f32) + second[...].astype(f32)
    out[...] = inside * s_left[:, last] * t + base[...]


def final(place, k, kept, first, second, s_left, t_own, t_mate, whole=None):
    part, columns = kept.shape
    half = columns // 2
    block = pl.BlockSpec((part, half), lambda i, place: (0, i))
    in_specs = (
        [block] * 3
        + [pl.BlockSpec(s_left.shape, lambda i, place: (0, 0))]
        + [pl.BlockSpec((t_own.shape[0], half), lambda i, place: (0, k))] * 2
    )
    more, aliases = (), {}
    if whole is not None:
        in_specs = in_specs + [pl.BlockSpec(memory_space=pl.ANY)]
        more, aliases = (whole,), {7: 0}
    return pl.pallas_call(
        final_kernel,
        grid_spec=pltpu.PrefetchScalarGridSpec(
            num_scalar_prefetch=1,
            grid=(2,),
            in_specs=in_specs,
            out_specs=pl.BlockSpec(
                (part, half), lambda i, place: (0, lax.rem(place[1] + i, 2) * 2 + k)
            ),
        ),
        out_shape=jax.ShapeDtypeStruct((part, 2 * columns), f32),
        input_output_aliases=aliases,
        compiler_params=pltpu.CompilerParams(vmem_limit_bytes=16 * 2**20),
        cost_estimate=pl.CostEstimate(
            flops=6 * part * columns, bytes_accessed=12 * part * columns, transcendentals=0
        ),
    )(place, kept, first, second, s_left, t_own, t_mate, *more)


def per_device(student, teacher, starts, weights, counts):
    y, x, z, c = (lax.axis_index(n) for n in ("y", "x", "row", "col"))
    place = jnp.stack([z, c, y, x]).astype(jnp.int32)
    rows = starts.shape[0]
    columns = teacher.shape[1]
    half = columns // 2
    width = student.shape[1] // SIDE

    up = [(i, (i + 1) % 16) for i in range(16)]
    down = [(j, i) for i, j in up]
    before = lax.ppermute(teacher[rows - HALO :], ("y", "x"), up)
    behind = lax.ppermute(teacher[:HALO], ("y", "x"), down)

    packed = pack(place, counts, student)
    packed, before, behind = lax.optimization_barrier((packed, before, behind))
    got = [packed[0], ring(packed[1], "x", 1), ring(packed[2], "x", -1), ring(packed[3], "x", 2)]
    standard = pool(place, counts, before, teacher, behind, starts[None], weights.T)
    got, standard = lax.optimization_barrier((got, standard))
    turned, mean = turn(place, counts, got)

    right, left = ring(standard, "x", 1), ring(standard, "x", -1)
    up, down = ring(turned, "row", 1), ring(turned, "row", -1)
    t_standard = swap(standard)
    right, left, up, down, t_standard = lax.optimization_barrier(
        (right, left, up, down, t_standard)
    )

    x_far = [ring(right[:, :half], "x", 1), ring(left[:, half:], "x", -1)]
    z_far = [ring(up[: width // 2], "row", 1), ring(down[width // 2 :], "row", -1)]
    t_right, t_left = swap(right), swap(left)
    own, mate = [standard, right, left], [t_standard, t_right, t_left]
    near_z = [turned, up, down]
    own_sum = first_product(place, near_z, own, mean)
    mate_sum = first_product(place, near_z, mate, mean)
    x_far, z_far, own_sum, mate_sum = lax.optimization_barrier((x_far, z_far, own_sum, mate_sum))

    t_x_far = [swap(f) for f in x_far]
    every = ring_all(shards(place, near_z, z_far[1], own + x_far), "y")
    sides, arrived = [], []
    for k in range(2):
        if k == 1:
            every, own_sum, mate_sum = lax.optimization_barrier((every, own_sum, mate_sum))
        sides.append((own + [x_far[k], own_sum], mate + [t_x_far[k], mate_sum]))
        o = last_product(place, k, "far", near_z, z_far[0], mean, *sides[k])
        arrived.append((ring(o[0], "y", 1), ring(o[1], "y", -1)))
    t_rows, s_left = settle(every)
    settled = (s_left, t_rows, swap(t_rows))
    passed = []
    for k in range(2):
        v = last_product(place, k, "close", near_z, z_far[1], mean, *sides[k], arrived[k])
        passed.append((ring(v[0], "y", 1), ring(v[1], "y", -1)))
    out = None
    for k in range(2):
        base = last_product(place, k, "own", near_z, z_far[0], mean, *sides[k], settled)[0]
        out = final(place, k, base, *passed[k], *settled, out)
    return out[None, None]


def solution(mesh):
    fine = Mesh(mesh.devices.reshape(SIDE, SIDE, SIDE, 2), ("y", "x", "row", "col"))
    seq = ("y", "x")
    placed = (
        P(seq + ("row",), "col"),
        P(seq, ("row", "col")),
        P(seq),
        P(seq, None),
        P(seq, None),
    )
    return jax.shard_map(
        per_device,
        mesh=fine,
        in_specs=placed,
        out_specs=P("col", seq, None, "row"),
        check_vma=False,
    )
```

```python
import jax
import jax.numpy as jnp
from jax import lax
from jax.experimental import pallas as pl
from jax.experimental.pallas import tpu as pltpu
from jax.sharding import Mesh
from jax.sharding import PartitionSpec as P

SUB = 192
BAND = 4
HALO = 16
EXTRA = 16
SIDE = 4
COMING = (0, SIDE - 1, 1, 2)
epsilon = 1e-05
f32 = jnp.float32
bf16 = jnp.bfloat16


def ring(value, axis, step):
    return lax.ppermute(value, axis, [(i, (i + step) % SIDE) for i in range(SIDE)])


def ring_all(value, axis):
    return [value, ring(value, axis, 1), ring(value, axis, -1), ring(value, axis, 2)]


def swap(value):
    return lax.ppermute(value, "col", [(0, 1), (1, 0)])


def after(value, *others):
    return lax.optimization_barrier((value, others))[0]


def in_parts(value):
    high = value.astype(bf16).astype(f32)
    rest = value - high
    middle = rest.astype(bf16).astype(f32)
    return high, middle, (rest - middle).astype(bf16).astype(f32)


def below(rows):
    empty = jnp.zeros((EXTRA - len(rows), rows[0].shape[1]), f32)
    return jnp.concatenate(rows + (empty,), axis=0).astype(bf16)


def from_parts(rows):
    return rows[0:1] + rows[1:2] + rows[2:3]


def smem():
    return pl.BlockSpec(memory_space=pltpu.SMEM)


def vmem():
    return pl.BlockSpec(memory_space=pltpu.VMEM)


def pack_kernel(place, counts, student, *outs):
    y, x, count = place[2], place[3], counts[0, place[0]]
    part = outs[0].shape[1] // SIDE
    for r, x_step in enumerate((0, 1, SIDE - 1, 2)):
        at = lax.rem(x + x_step, SIDE)
        for i, y_step in enumerate((2, 0, 1, SIDE - 1)):
            slot = lax.rem(y + y_step, SIDE) * SIDE + at
            first = pl.multiple_of(slot * part, 128)
            columns = slice(i * part, (i + 1) * part)
            block = student[:, pl.ds(first, part)]
            outs[r][:SUB, columns] = block
            value = block.astype(f32)
            live = lax.broadcasted_iota(jnp.int32, value.shape, 0) < count
            total = jnp.sum(jnp.where(live, value, 0.0), axis=0, keepdims=True)
            dev = jnp.where(live, value - total / count.astype(f32), 0.0)
            square = jnp.sum(dev * dev, axis=0, keepdims=True)
            outs[r][SUB:, columns] = below(in_parts(total) + in_parts(square))


def pack(place, counts, student):
    width = student.shape[1] // SIDE
    return pl.pallas_call(
        pack_kernel,
        in_specs=[smem(), smem(), vmem()],
        out_specs=[vmem()] * SIDE,
        out_shape=[jax.ShapeDtypeStruct((SUB + EXTRA, width), bf16)] * SIDE,
        compiler_params=pltpu.CompilerParams(vmem_limit_bytes=24 * 2**20),
        cost_estimate=pl.CostEstimate(
            flops=8 * SUB * student.shape[1],
            bytes_accessed=4 * SUB * student.shape[1],
            transcendentals=0,
        ),
    )(place, counts, student)


def turn_kernel(place, counts, p0, p1, p2, p3, turned, near):
    count = counts[0, place[0]]
    pieces = (p0, p1, p2, p3)
    rows = jnp.concatenate([p[:SUB, :] for p in pieces], axis=0)
    flat = rows.T
    width, depth = flat.shape
    turned[:width, :] = flat
    moments = jnp.concatenate([p[SUB:, :].astype(f32)[:6] for p in pieces], axis=0)
    rests = [
        jnp.concatenate([moments[3 * m + i : 3 * m + i + 1, depth:] for i in range(3)], axis=1)
        for m in range(8)
    ]
    turned[width:, :] = jnp.concatenate([moments[:, :depth]] + rests, axis=0).astype(bf16)
    mine = flat[:, :SUB].astype(f32)
    live = lax.broadcasted_iota(jnp.int32, mine.shape, 1) < count
    total = jnp.sum(jnp.where(live, mine, 0.0), axis=1, keepdims=True)
    near[...] = total / count.astype(f32)


def turn(place, counts, pieces):
    width = pieces[0].shape[1]
    return pl.pallas_call(
        turn_kernel,
        in_specs=[smem()] * 2 + [vmem()] * SIDE,
        out_specs=[vmem()] * 2,
        out_shape=[
            jax.ShapeDtypeStruct((width + 2 * EXTRA, SIDE * SUB), bf16),
            jax.ShapeDtypeStruct((width, 1), f32),
        ],
        compiler_params=pltpu.CompilerParams(vmem_limit_bytes=16 * 2**20),
        cost_estimate=pl.CostEstimate(
            flops=0, bytes_accessed=4 * SUB * SIDE * width, transcendentals=0
        ),
    )(place, counts, *pieces)


def shards_kernel(place, *refs):
    zs, own, out = refs[:SIDE], refs[SIDE : SIDE + 5], refs[-1]
    half = own[3].shape[1]
    depth = zs[0].shape[1]
    blocks = []
    for ref in zs:
        rows = ref[...].astype(f32)
        rests = [
            rows[24 + m : 25 + m, i * (depth // 3) : (i + 1) * (depth // 3)]
            for m in range(8)
            for i in range(3)
        ]
        rests = jnp.concatenate(rests, axis=0)
        blocks.append(jnp.concatenate([rows[:24], rests], axis=1))
    lane = lax.broadcasted_iota(jnp.int32, (1, half), 1)
    for r in range(SIDE):
        if r < 3:
            rows = own[r][...].astype(f32)
        else:
            rows = jnp.concatenate([own[3][...].astype(f32), own[4][...].astype(f32)], axis=1)
        out[r : r + 1, :] = from_parts(rows[0:3])
        out[SIDE + r : SIDE + r + 1, :] = from_parts(rows[3:6])
        sizes = rows[6:7, :half]
        n = jnp.sum(jnp.where(lane < SIDE, sizes, 0.0), axis=1, keepdims=True)
        out[8 + r : 9 + r, :] = jnp.broadcast_to(n, (1, out.shape[1]))
        totals = [from_parts(b[6 * r : 6 * r + 3]) for b in blocks]
        squares = [from_parts(b[6 * r + 3 : 6 * r + 6]) for b in blocks]
        total = totals[0] + totals[1] + totals[2] + totals[3]
        mean = total / n
        square = jnp.zeros_like(total)
        for q, step in enumerate(COMING):
            here = lax.rem(place[0] + step, SIDE)
            size = jnp.sum(jnp.where(lane == here, sizes, 0.0), axis=1, keepdims=True)
            off = totals[q] / size - mean
            square = square + squares[q] + size * off * off
        out[12 + r : 13 + r, :] = total
        out[16 + r : 17 + r, :] = square
    out[20:24, :] = jnp.zeros((4, out.shape[1]), f32)


def shards(place, left, far_left, own):
    depth = left[0].shape[1]
    columns = own[0].shape[1]

    def low(value, rows):
        first = value.shape[0] // rows - 1
        return pl.BlockSpec((rows, value.shape[1]), lambda i, place: (first, 0))

    return pl.pallas_call(
        shards_kernel,
        grid_spec=pltpu.PrefetchScalarGridSpec(
            num_scalar_prefetch=1,
            grid=(1,),
            in_specs=[low(v, 2 * EXTRA) for v in left + [far_left]]
            + [low(v, EXTRA) for v in own],
            out_specs=pl.BlockSpec((24, columns), lambda i, place: (0, 0)),
        ),
        out_shape=jax.ShapeDtypeStruct((24, columns), f32),
        compiler_params=pltpu.CompilerParams(vmem_limit_bytes=8 * 2**20),
    )(place, *left, far_left, *own)


def settle_kernel(e0, e1, e2, e3, t_rows, s_left, work):
    every = (e0, e1, e2, e3)
    part = work.shape[1]

    def combine(totals, squares, counts):
        tokens = sum(jnp.sum(n, axis=0, keepdims=True) for n in counts)
        mean = sum(jnp.sum(t, axis=0, keepdims=True) for t in totals) / tokens
        offs = [t / n - mean for t, n in zip(totals, counts)]
        square = sum(
            jnp.sum(q + n * o * o, axis=0, keepdims=True)
            for q, n, o in zip(squares, counts, offs)
        )
        return offs, lax.rsqrt(square / tokens + epsilon), tokens

    offs, scale, _ = combine(
        [e[0:4, :] for e in every], [e[4:8, :] for e in every], [e[8:12, :] for e in every]
    )
    for j in range(SIDE):
        t_rows[j * SIDE : (j + 1) * SIDE, :] = offs[j] * scale
    t_rows[SIDE * SIDE : SIDE * SIDE + 1, :] = scale
    slots = [slice(i * part, (i + 1) * part) for i in (1, 2, 3, 0)]
    counts = [e[8:12, 0:part] for e in every]
    offs, scale, tokens = combine(
        [e[12:16, c] for e, c in zip(every, slots)],
        [e[16:20, c] for e, c in zip(every, slots)],
        counts,
    )
    scale = scale / jnp.sqrt(tokens)
    work[...] = jnp.zeros_like(work)
    for j in range(SIDE):
        work[j * SIDE : (j + 1) * SIDE, :] = offs[j] * scale * counts[j]
    work[SIDE * SIDE : SIDE * SIDE + 1, :] = scale
    s_left[...] = work[...].T


def settle(every):
    columns = every[0].shape[1]
    part = columns // SIDE
    S = jax.ShapeDtypeStruct
    return pl.pallas_call(
        settle_kernel,
        in_specs=[vmem()] * SIDE,
        out_specs=[vmem()] * 2,
        out_shape=[S((SIDE * SIDE + 1, columns), f32), S((part, 128), f32)],
        scratch_shapes=[pltpu.VMEM((128, part), f32)],
        compiler_params=pltpu.CompilerParams(vmem_limit_bytes=8 * 2**20),
    )(*every)


def pool_kernel(place, counts, before, teacher, behind, starts, weights, full, mix, share, pooled, lines, meta):
    window = SUB + 2 * HALO
    length = teacher.shape[0]
    j = pl.program_id(0)

    @pl.when(j == 0)
    def _():
        lines[...] = jnp.zeros_like(lines)
        lines[0:1, :] = (starts[...] - (place[2] * SIDE + place[3]) * length).astype(f32)
        lines[1 : 1 + BAND, :] = weights[...].astype(f32)
        meta[...] = lines[...].T.astype(jnp.int32)
        for r in range(SIDE):
            rows = slice(r * SUB, (r + 1) * SUB)
            spot = lax.broadcasted_iota(jnp.int32, (SUB, window), 1)
            local = meta[rows, 0:1] - (r * SUB - HALO)
            found = jnp.zeros((SUB, window), jnp.int32)
            whole = jnp.zeros((SUB, 1), jnp.int32)
            for k in range(BAND):
                weight = meta[rows, 1 + k : 2 + k]
                found = found + jnp.where(spot == local + k, weight, 0)
                whole = whole + weight
            mix[rows, :] = found.astype(f32).astype(bf16)
            share[rows, :] = jnp.broadcast_to(whole.astype(f32), (SUB, 128))

    total = jnp.zeros((1, teacher.shape[1]), f32)
    alive = jnp.int32(0)
    for r in range(SIDE):
        rows = slice(r * SUB, (r + 1) * SUB)
        low, high = r * SUB - HALO, (r + 1) * SUB + HALO
        parts = [teacher[max(low, 0) : min(high, length), :]]
        if low < 0:
            parts = [before[...]] + parts
        if high > length:
            parts = parts + [behind[...]]
        seen = jnp.concatenate(parts, axis=0) if len(parts) > 1 else parts[0]
        value = jnp.dot(mix[rows, :], seen, preferred_element_type=f32)
        value = value / share[rows, 0:1]
        pooled[rows, :] = value
        live = lax.broadcasted_iota(jnp.int32, value.shape, 0) < counts[0, r]
        total = total + jnp.sum(jnp.where(live, value, 0.0), axis=0, keepdims=True)
        alive = alive + counts[0, r]
    mean = total / alive.astype(f32)
    square = jnp.zeros_like(total)
    for r in range(SIDE):
        rows = slice(r * SUB, (r + 1) * SUB)
        value = pooled[rows, :]
        live = lax.broadcasted_iota(jnp.int32, value.shape, 0) < counts[0, r]
        dev = jnp.where(live, value - mean, 0.0)
        small = dev.astype(bf16)
        full[rows, :] = small
        square = square + jnp.sum(dev * dev, axis=0, keepdims=True)
    lane = lax.broadcasted_iota(jnp.int32, total.shape, 1)
    sizes = jnp.zeros(total.shape, jnp.int32)
    for r in range(SIDE):
        sizes = sizes + jnp.where(lane == r, counts[0, r], 0)
    full[length:, :] = below(in_parts(total) + in_parts(square) + (sizes.astype(f32),))


def pool(place, counts, before, teacher, behind, starts, weights):
    rows, columns = teacher.shape
    tile = 256
    return pl.pallas_call(
        pool_kernel,
        grid=(columns // tile,),
        in_specs=[
            smem(),
            smem(),
            pl.BlockSpec((HALO, tile), lambda j: (0, j)),
            pl.BlockSpec((rows, tile), lambda j: (0, j)),
            pl.BlockSpec((HALO, tile), lambda j: (0, j)),
            pl.BlockSpec(starts.shape, lambda j: (0, 0)),
            pl.BlockSpec(weights.shape, lambda j: (0, 0)),
        ],
        out_specs=pl.BlockSpec((rows + EXTRA, tile), lambda j: (0, j)),
        out_shape=jax.ShapeDtypeStruct((rows + EXTRA, columns), bf16),
        scratch_shapes=[
            pltpu.VMEM((rows, SUB + 2 * HALO), bf16),
            pltpu.VMEM((rows, 128), f32),
            pltpu.VMEM((rows, tile), f32),
            pltpu.VMEM((128, rows), f32),
            pltpu.VMEM((rows, 128), jnp.int32),
        ],
        compiler_params=pltpu.CompilerParams(vmem_limit_bytes=32 * 2**20),
        cost_estimate=pl.CostEstimate(
            flops=2 * rows * 256 * columns, bytes_accessed=6 * rows * columns, transcendentals=0
        ),
    )(place, counts, before, teacher, behind, starts, weights)


def with_ones(a):
    return jnp.concatenate([a, jnp.ones((16, a.shape[1]), bf16)], axis=0)


def less_mean(total, near):
    part = total.shape[0] - 16
    return total[:part] - near * total[part : part + 1]


def first_kernel(place, a0, a1, a2, b0, b1, b2, near, out):
    z = place[0]
    depth = a0.shape[1]
    fill = jnp.zeros((depth - 3 * SUB, b0.shape[1]), bf16)
    total = None
    for a, step in zip((a0, a1, a2), COMING):
        rows = pl.ds(pl.multiple_of(lax.rem(z + step, SIDE) * SUB, 16), SUB)
        b = jnp.concatenate([b0[rows, :], b1[rows, :], b2[rows, :], fill], axis=0)
        term = jnp.dot(with_ones(a[...]), b, preferred_element_type=f32)
        total = term if total is None else total + term
    out[...] = less_mean(total, near[...])


def first_product(place, left, right, near):
    depth = left[0].shape[1]
    rows = near.shape[0]
    part = rows // SIDE
    length, columns = right[0].shape
    near_depth = 640
    return pl.pallas_call(
        first_kernel,
        grid_spec=pltpu.PrefetchScalarGridSpec(
            num_scalar_prefetch=1,
            grid=(SIDE,),
            in_specs=[pl.BlockSpec((part, near_depth), lambda i, place: (i, 0))] * 3
            + [pl.BlockSpec((length, columns), lambda i, place: (0, 0))] * 3
            + [pl.BlockSpec((part, 1), lambda i, place: (i, 0))],
            out_specs=pl.BlockSpec((part, columns), lambda i, place: (i, 0)),
        ),
        out_shape=pltpu.HBM((rows, columns), f32),
        compiler_params=pltpu.CompilerParams(vmem_limit_bytes=26 * 2**20),
        cost_estimate=pl.CostEstimate(
            flops=2 * rows * 3 * near_depth * columns,
            bytes_accessed=6 * rows * depth + 6 * length * columns + 4 * rows * columns,
            transcendentals=0,
        ),
    )(place, *left, *right, near)


def last_sums(place, refs):
    z = place[0]
    tails, far_a, near = refs[:3], refs[3], refs[4]
    sides = (refs[5:10], refs[10:15])
    results = []
    lefts = [with_ones(t[...]) for t in tails]
    far_left = with_ones(far_a[...])
    for b0, b1, b2, far_b, done in sides:
        fill = jnp.zeros((tails[0].shape[1] - SUB, far_b.shape[1]), bf16)
        total = None
        for a, step in zip(lefts, COMING):
            rows = pl.ds(pl.multiple_of(lax.rem(z + step, SIDE) * SUB, 16), SUB)
            b = jnp.concatenate([fill, far_b[rows, :]], axis=0)
            term = jnp.dot(a, b, preferred_element_type=f32)
            total = term if total is None else total + term
        rows = pl.ds(pl.multiple_of(lax.rem(z + 2, SIDE) * SUB, 16), SUB)
        b = jnp.concatenate([b0[...], b1[...], b2[...], far_b[rows, :]], axis=0)
        total = total + jnp.dot(far_left, b, preferred_element_type=f32)
        results.append(less_mean(total, near[...]) + done[...])
    return results


def far_kernel(place, *refs):
    up, down = refs[15:]
    results = last_sums(place, refs)
    up[...] = results[0].astype(bf16)
    down[...] = results[1].astype(bf16)


def own_kernel(place, *refs):
    s_left, t_own, t_mate, base = refs[15:]
    half = base.shape[1] // 2
    every = SIDE * SIDE
    results = last_sums(place, refs)
    for i, t in enumerate((t_own, t_mate)):
        between = jnp.dot(
            s_left[:, :every],
            t[:every, :],
            preferred_element_type=f32,
            precision=lax.Precision.HIGHEST,
        )
        scaled = results[i] * s_left[:, every : every + 1] * t[every : every + 1, :]
        base[:, i * half : (i + 1) * half] = scaled + between


def close_kernel(place, *refs):
    from_back, from_next, up, down = refs[15:]
    i = pl.program_id(0)
    half = from_back.shape[1]
    results = last_sums(place, refs)

    @pl.when(i == 0)
    def _():
        up[:, :half] = (results[0] + from_back[...].astype(f32)).astype(bf16)
        up[:, half:] = results[1].astype(bf16)

    @pl.when(i == 1)
    def _():
        down[:, :half] = results[0].astype(bf16)
        down[:, half:] = (results[1] + from_next[...].astype(f32)).astype(bf16)


def last_product(place, k, kind, left, far_left, near, own, mate, arrived=()):
    depth = left[0].shape[1]
    part = near.shape[0] // SIDE
    half = own[0].shape[1] // 2
    kernel, start, far_start, steps = {
        "far": (far_kernel, 0, 0, 1),
        "own": (own_kernel, 1, 1, 1),
        "close": (close_kernel, 2, 0, 2),
    }[kind]
    one = lambda i, place: (0, 0)
    tail = 256
    side = (
        [pl.BlockSpec((SUB, half), lambda i, place: (lax.rem(place[0] + 2, SIDE), k))] * 3
        + [pl.BlockSpec((own[3].shape[0], half), one)]
        + [pl.BlockSpec((part, half), lambda i, place: (start + i, k))]
    )
    in_specs = (
        [pl.BlockSpec((part, tail), lambda i, place: (start + i, depth // tail - 1))] * 3
        + [pl.BlockSpec((part, depth), lambda i, place: (far_start + i, 0))]
        + [pl.BlockSpec((part, 1), lambda i, place: (start + i, 0))]
        + side * 2
        + (
            [pl.BlockSpec(arrived[0].shape, one)]
            + [pl.BlockSpec((a.shape[0], half), lambda i, place: (0, k)) for a in arrived[1:]]
            if kind == "own"
            else [pl.BlockSpec((part, half), one)] * len(arrived)
        )
    )
    S = jax.ShapeDtypeStruct
    shapes = {
        "far": [S((part, half), bf16)] * 2,
        "own": [S((part, 2 * half), f32)],
        "close": [S((part, 2 * half), bf16)] * 2,
    }[kind]
    return pl.pallas_call(
        kernel,
        grid_spec=pltpu.PrefetchScalarGridSpec(
            num_scalar_prefetch=1,
            grid=(steps,),
            in_specs=in_specs,
            out_specs=[pl.BlockSpec(s.shape, one) for s in shapes],
        ),
        out_shape=shapes,
        compiler_params=pltpu.CompilerParams(vmem_limit_bytes=26 * 2**20),
        cost_estimate=pl.CostEstimate(
            flops=2 * steps * part * 2 * depth * 2 * half,
            bytes_accessed=3 * steps * depth * part + 5 * depth * half + 8 * part * half,
            transcendentals=0,
        ),
    )(place, *left, far_left, near, *own, *mate, *arrived)


def final_kernel(place, base, first, second, s_left, t_own, t_mate, *rest):
    out = rest[-1]
    every = SIDE * SIDE
    last = slice(every, every + 1)
    t = jnp.where(pl.program_id(0) < 2, t_own[last, :], t_mate[last, :])
    inside = first[...].astype(f32) + second[...].astype(f32)
    out[...] = inside * s_left[:, last] * t + base[...]


def final(place, k, kept, first, second, s_left, t_own, t_mate, whole=None):
    part, columns = kept.shape
    quarter = columns // 4
    block = pl.BlockSpec((part, quarter), lambda i, place: (0, i))
    in_specs = (
        [block] * 3
        + [pl.BlockSpec(s_left.shape, lambda i, place: (0, 0))]
        + [pl.BlockSpec((t_own.shape[0], quarter), lambda i, place: (0, 2 * k + lax.rem(i, 2)))] * 2
    )
    more, aliases = (), {}
    if whole is not None:
        in_specs = in_specs + [pl.BlockSpec(memory_space=pl.ANY)]
        more, aliases = (whole,), {7: 0}
    return pl.pallas_call(
        final_kernel,
        grid_spec=pltpu.PrefetchScalarGridSpec(
            num_scalar_prefetch=1,
            grid=(4,),
            in_specs=in_specs,
            out_specs=pl.BlockSpec(
                (part, quarter), lambda i, place: (0, (lax.rem(place[1] + i // 2, 2) * 2 + k) * 2 + lax.rem(i, 2))
            ),
        ),
        out_shape=jax.ShapeDtypeStruct((part, 2 * columns), f32),
        input_output_aliases=aliases,
        compiler_params=pltpu.CompilerParams(vmem_limit_bytes=16 * 2**20),
        cost_estimate=pl.CostEstimate(
            flops=6 * part * columns, bytes_accessed=12 * part * columns, transcendentals=0
        ),
    )(place, kept, first, second, s_left, t_own, t_mate, *more)


def per_device(student, teacher, starts, weights, counts):
    y, x, z, c = (lax.axis_index(n) for n in ("y", "x", "row", "col"))
    place = jnp.stack([z, c, y, x]).astype(jnp.int32)
    rows = starts.shape[0]
    columns = teacher.shape[1]
    half = columns // 2
    width = student.shape[1] // SIDE

    up = [(i, (i + 1) % 16) for i in range(16)]
    down = [(j, i) for i, j in up]
    before = lax.ppermute(teacher[rows - HALO :], ("y", "x"), up)
    behind = lax.ppermute(teacher[:HALO], ("y", "x"), down)

    packed = pack(place, counts, student)
    packed, before, behind = lax.optimization_barrier((packed, before, behind))
    got = [packed[0], ring(packed[1], "x", 1), ring(packed[2], "x", -1), ring(packed[3], "x", 2)]
    standard = pool(place, counts, before, teacher, behind, starts[None], weights.T)
    got, standard = lax.optimization_barrier((got, standard))
    turned, mean = turn(place, counts, got)

    right, left = ring(standard, "x", 1), ring(standard, "x", -1)
    up, down = ring(turned, "row", 1), ring(turned, "row", -1)
    t_standard = swap(standard)
    right, left, up, down, t_standard = lax.optimization_barrier(
        (right, left, up, down, t_standard)
    )

    x_far = [ring(right[:, :half], "x", 1), ring(left[:, half:], "x", -1)]
    z_far = [ring(up[: width // 2], "row", 1), ring(down[width // 2 :], "row", -1)]
    t_right, t_left = swap(right), swap(left)
    own, mate = [standard, right, left], [t_standard, t_right, t_left]
    near_z = [turned, up, down]
    own_sum = first_product(place, near_z, own, mean)
    mate_sum = first_product(place, near_z, mate, mean)
    x_far, z_far, own_sum, mate_sum = lax.optimization_barrier((x_far, z_far, own_sum, mate_sum))

    t_x_far = [swap(f) for f in x_far]
    every = ring_all(shards(place, near_z, z_far[1], own + x_far), "y")
    sides, arrived = [], []
    for k in range(2):
        if k == 1:
            every, own_sum, mate_sum = lax.optimization_barrier((every, own_sum, mate_sum))
        sides.append((own + [x_far[k], own_sum], mate + [t_x_far[k], mate_sum]))
        o = last_product(place, k, "far", near_z, z_far[0], mean, *sides[k])
        arrived.append((ring(o[0], "y", 1), ring(o[1], "y", -1)))
    t_rows, s_left = settle(every)
    settled = (s_left, t_rows, swap(t_rows))
    passed = []
    for k in range(2):
        v = last_product(place, k, "close", near_z, z_far[1], mean, *sides[k], arrived[k])
        passed.append((ring(v[0], "y", 1), ring(v[1], "y", -1)))
    out = None
    for k in range(2):
        base = last_product(place, k, "own", near_z, z_far[0], mean, *sides[k], settled)[0]
        out = final(place, k, base, *passed[k], *settled, out)
    return out[None, None]


def solution(mesh):
    fine = Mesh(mesh.devices.reshape(SIDE, SIDE, SIDE, 2), ("y", "x", "row", "col"))
    seq = ("y", "x")
    placed = (
        P(seq + ("row",), "col"),
        P(seq, ("row", "col")),
        P(seq),
        P(seq, None),
        P(seq, None),
    )
    return jax.shard_map(
        per_device,
        mesh=fine,
        in_specs=placed,
        out_specs=P("col", seq, None, "row"),
        check_vma=False,
    )
```
